256 devices in a mesh: dp: 32 (over z, x), head: 8 (over y, core).
Axes of the slice: x: 4, y: 4, z: 8, core: 2. Of those that a mesh axis runs over, the one named last changes fastest.
Arguments:
- tokens: bfloat16 [32768, 2048], P(('dp', 'head')), may hold values from -8 to 8
- stretch_prompt: int32 [64], replicated, may hold values from 0 to 7, never falling along the last dimension, each value on 1 to 32 neighbouring positions
- last_fill: int32 [64], replicated, may hold values from 1 to 512
- ln1_gain: bfloat16 [2048], replicated, may hold values from 0.25 to 1.75
- w_qk: bfloat16 [2048, 2, 2048], P(None, None, 'head'), may hold values from -0.125 to 0.125
- w_vz: bfloat16 [2048, 2, 4096], P(None, None, 'head'), may hold values from -0.125 to 0.125
- w_ba: bfloat16 [2048, 2, 32], P(None, None, 'head'), may hold values from -2 to 2
- conv_qk: bfloat16 [4, 2, 2048], P(None, None, 'head'), may hold values from -3 to 3
- conv_value: bfloat16 [4, 4096], P(None, 'head'), may hold values from -3 to 3
- decay_log: float32 [32], P('head'), may hold values from 0 to 1
- dt_bias: float32 [32], P('head'), may hold values from -25 to -3
- norm_gain: bfloat16 [128], replicated, may hold values from 0.25 to 1.75
- w_out: bfloat16 [4096, 2048], P('head'), may hold values from -0.09375 to 0.09375
- ln2_gain: bfloat16 [2048], replicated, may hold values from 0.25 to 1.75
- w_sgate: bfloat16 [2048], replicated, may hold values from -0.125 to 0.125
- shared_weights: bfloat16 [3, 512, 2048], P(None, 'head'), may hold values from -0.25 to 0.25
Outputs:
- attention_out: bfloat16 [32768, 2048], P(('dp', 'head'))
- layer_out: bfloat16 [32768, 2048], P(('dp', 'head'))
The draws below stay inside these ranges and needn't reach their ends.
Inputs may be any that keep to these rules, and one draw needn't show every extreme that they name: stretch_prompt never falls from one stretch to the next, so each prompt holds consecutive stretches; every prompt holds 1 to 32 stretches and one holds exactly 32.
All inputs are finite; a program needn't handle non-finite values.
Results may differ from the reference program's by a relative error of at most 0.025.
Values may be sent and summed in bfloat16 or wider, within the bound.
No kernel may reach another device: no remote copies, remote signals or barrier semaphores. Data moves between devices by JAX's collectives and lax.ppermute only.
A program may use at most 128 MiB of HBM per device.

```python
import math
import jax
import jax.numpy as jnp
import numpy as np
from jax import lax

D = 2048
KH = 16
VH = 32
DK = 128
DV = 128
SH = 512
CONV = 4
BLOCK = 64
STRETCH = 512
PROMPTS = 8
STRETCHES = 64
LONGEST = 32
TOKENS = 32768
N_HEAD = 8


def shared_direction(key):
    return jnp.clip(jax.random.normal(key, (D,), jnp.float32), -3.0, 3.0)


def draw_tokens(key, part):
    common = shared_direction(key)
    key = jax.random.fold_in(key, 11)
    random_key = jax.random.fold_in(key, 0)
    random_part = jnp.clip(jax.random.normal(random_key, (TOKENS, D), jnp.float32), -5.0, 5.0)
    return (random_part + 0.3 * common[None, :]).astype(jnp.bfloat16)


def draw_w_ba(key, part):
    common = shared_direction(key)
    key = jax.random.fold_in(key, 12)
    random_part = jnp.clip(jax.random.normal(key, (D, 2, VH), jnp.float32), -4.0, 4.0)
    spreads = jnp.array([1.0, 3.0], jnp.float32)[None, :, None] * D ** (-0.5)
    pulling = jnp.array([-18.0, 0.0], jnp.float32)[None, :, None] * common[:, None, None] / D
    return (random_part * spreads + pulling).astype(jnp.bfloat16)


def set_ends(result, key, low, largest):
    place = [jax.random.randint(jax.random.fold_in(key, axis), (), 0, length) for axis, length in enumerate(result.shape)]
    widest = result.shape.index(max(result.shape))
    next_to = place[:widest] + [(place[widest] + 1) % result.shape[widest]] + place[widest + 1:]
    return result.at[tuple(place)].set(low).at[tuple(next_to)].set(largest)


def levels(rng, shape, pieces, low, top_value):
    level, own = 1.0, jax.random.fold_in(rng, 6)
    for dim, parts in pieces:
        draws = jnp.exp(jax.random.uniform(jax.random.fold_in(own, dim), (parts,), jnp.float32, low / len(pieces), top_value / len(pieces)))
        level = level * jnp.repeat(draws, shape[dim] // parts).reshape([-1 if axis == dim else 1 for axis in range(len(shape))])
    return level


def profile(amount, total, reach, slope):
    weights = [(1 << 20) // math.isqrt(standing ** slope) + 1 for standing in range(2, amount + 1)]
    spare, counts = total - reach - (amount - 1), [1] * (amount - 1)
    while spare > 0:
        candidates = [i for i in range(amount - 1) if counts[i] < reach]
        pool, remaining = sum([weights[i] for i in candidates]), spare
        for i in candidates:
            extra = min(reach - counts[i], max(1, remaining * weights[i] // pool), spare)
            counts[i] = counts[i] + extra
            spare = spare - extra
    return np.array([reach] + counts)


def uneven(key, amount, total, most, lean):
    if amount == 2:
        one = jax.random.randint(key, (), max(1, total - most), min(most, total - 1) + 1)
        return jnp.stack([one, total - one])
    sizes = jnp.asarray(profile(amount, total, most, lean), jnp.int32)
    twos = (amount - 1) // 2
    source_of, receiver = sizes[1:1 + 2 * twos:2], sizes[2:2 + 2 * twos:2]
    slack = jnp.minimum(source_of - 1, most - receiver)
    passed = jax.random.randint(jax.random.fold_in(key, 1), (twos,), 0, 1 << 20) % (slack + 1)
    sizes = sizes.at[1:1 + 2 * twos:2].set(source_of - passed).at[2:2 + 2 * twos:2].set(receiver + passed)
    return sizes[jax.random.permutation(jax.random.fold_in(key, 2), amount)]


def normal_values(rng, dims, scale, bound, pieces=(), kind=jnp.bfloat16):
    values = jax.random.normal(rng, dims, jnp.float32) * scale
    if len(pieces) > 0:
        values = levels(rng, dims, pieces, -0.22, 0.18) * values
    return jnp.clip(values, min=-bound, max=bound).astype(kind)


def setup_inputs(seed: int = 0) -> dict:
    seeds = jax.random.split(jax.random.key(seed), 17)
    tokens = draw_tokens(jax.random.fold_in(seeds[16], 71), 0)
    stretch_prompt = jnp.searchsorted(jnp.cumsum(uneven(seeds[1], PROMPTS, STRETCHES, LONGEST, 2)), jnp.arange(STRETCHES), side="right").astype(jnp.int32)
    last_fill = set_ends(jax.random.randint(seeds[2], (STRETCHES,), 1, STRETCH + 1), jax.random.fold_in(seeds[2], 1), 1, STRETCH).astype(jnp.int32)
    ln1_gain = jnp.clip(1.0 + 0.15 * jax.random.normal(seeds[3], (D,), jnp.float32), 0.25, 1.75).astype(jnp.bfloat16)
    w_qk = normal_values(seeds[4], (D, 2, KH * DK), D ** -0.5, 0.125, ((2, 8),))
    w_vz = normal_values(seeds[5], (D, 2, VH * DV), D ** -0.5, 0.125, ((2, 8),))
    w_ba = draw_w_ba(jax.random.fold_in(seeds[16], 71), 0)
    conv_qk = normal_values(seeds[7], (CONV, 2, KH * DK), CONV ** -0.5, 3.0, ((2, 8),))
    conv_value = normal_values(seeds[8], (CONV, VH * DV), CONV ** -0.5, 3.0, ((1, 8),))
    decay_log = jnp.clip(1.0 * jax.random.uniform(seeds[9], (VH,), jnp.float32) ** levels(seeds[9], (VH,), ((0, 8),), -0.2, 0.2), 0.0, 1.0)
    dt_bias = jnp.clip(-25.0 + 22.0 * jax.random.uniform(seeds[10], (VH,), jnp.float32) ** levels(seeds[10], (VH,), ((0, 8),), -0.2, 0.2), -25.0, -3.0)
    norm_gain = jnp.clip(1.0 + 0.15 * jax.random.normal(seeds[11], (DV,), jnp.float32), 0.25, 1.75).astype(jnp.bfloat16)
    w_out = normal_values(seeds[12], (VH * DV, D), (VH * DV) ** -0.5, 0.09375, ((0, 8),))
    ln2_gain = jnp.clip(1.0 + 0.15 * jax.random.normal(seeds[13], (D,), jnp.float32), 0.25, 1.75).astype(jnp.bfloat16)
    w_sgate = normal_values(seeds[14], (D,), D ** -0.5, 0.125)
    shared_weights = normal_values(seeds[15], (3, SH, D), SH ** -0.5, 0.25, ((1, 8),))
    return dict(tokens=tokens, stretch_prompt=stretch_prompt, last_fill=last_fill, ln1_gain=ln1_gain, w_qk=w_qk, w_vz=w_vz, w_ba=w_ba, conv_qk=conv_qk, conv_value=conv_value, decay_log=decay_log, dt_bias=dt_bias, norm_gain=norm_gain, w_out=w_out, ln2_gain=ln2_gain, w_sgate=w_sgate, shared_weights=shared_weights)


HIGHEST = lax.Precision.HIGHEST
EPSILON = 1e-06

def matmul_high(left, right):
    return jnp.einsum('...ij,...jk->...ik', left, right, precision=HIGHEST)

def scaled_rows(inputs, scaling):
    widened = inputs.astype(jnp.float32)
    spread = lax.optimization_barrier(jnp.mean(widened * widened, axis=-1, keepdims=True))
    return widened * lax.rsqrt(spread + EPSILON) * scaling.astype(jnp.float32)

def unit_rows(inputs):
    return inputs * lax.rsqrt(lax.optimization_barrier(jnp.sum(inputs * inputs, axis=-1, keepdims=True)) + EPSILON)

def inverse_unit_lower(strict_part):
    span = strict_part.shape[-1]
    identity_block = jnp.eye(span, dtype=jnp.float32)
    negated = -strict_part
    inverse = identity_block + negated
    powered = negated
    for doubling in range(1, (span - 1).bit_length()):
        powered = matmul_high(powered, powered)
        inverse = matmul_high(inverse, identity_block + powered)
    return inverse

def block_terms(query, keys, values, beta, rate):
    span = query.shape[-2]
    positions = jnp.arange(span)
    inclusive = positions[:, None] >= positions[None, :]
    strict = positions[:, None] > positions[None, :]
    summing = inclusive.astype(jnp.float32)
    log_decay = jnp.einsum('...j,ij->...i', rate, summing, precision=HIGHEST)
    spread = log_decay[..., :, None] - log_decay[..., None, :]
    weight_in = jnp.where(inclusive, jnp.exp(jnp.where(inclusive, spread, 0.0)), 0.0)
    weight_strict = jnp.where(strict, weight_in, 0.0)
    scaled_keys = keys * beta[..., None]
    mixing = jnp.einsum('...id,...jd->...ij', scaled_keys, keys, precision=HIGHEST) * weight_strict
    scores = jnp.einsum('...id,...jd->...ij', query, keys, precision=HIGHEST) * weight_in
    growth = jnp.exp(log_decay)
    inverse = inverse_unit_lower(mixing)
    w_rows = matmul_high(inverse, scaled_keys * growth[..., None])
    u_rows = matmul_high(inverse, values * beta[..., None])
    final_decay = log_decay[..., -1:]
    tail_keys = keys * jnp.exp(final_decay - log_decay)[..., None]
    identity_key = jnp.eye(keys.shape[-1], dtype=jnp.float32)
    carry_map = jnp.exp(final_decay)[..., None] * identity_key - jnp.einsum('...id,...ie->...de', w_rows, tail_keys, precision=HIGHEST)
    carry_add = jnp.einsum('...iv,...ie->...ve', u_rows, tail_keys, precision=HIGHEST)
    base = jnp.einsum('...ij,...jv->...iv', scores, u_rows, precision=HIGHEST)
    probe = query * growth[..., None] - jnp.einsum('...ij,...jd->...id', scores, w_rows, precision=HIGHEST)
    return (base, probe, carry_map, carry_add)

def causal_mix(inputs, taps, owner):
    widened = inputs.astype(jnp.float32)
    weights = taps.astype(jnp.float32)
    depth = weights.shape[0]
    total = widened * weights[depth - 1]
    for offset in range(1, depth):
        moved = jnp.concatenate([jnp.zeros((offset, widened.shape[1]), jnp.float32), widened[:-offset]], axis=0)
        before = jnp.concatenate([jnp.full((offset,), -1, jnp.int32), owner[:-offset]], axis=0)
        total = total + jnp.where((before == owner)[:, None], moved, 0.0) * weights[depth - 1 - offset]
    return jax.nn.silu(total)

def reference(tokens, stretch_prompt, last_fill, ln1_gain, w_qk, w_vz, w_ba, conv_qk, conv_value, decay_log, dt_bias, norm_gain, w_out, ln2_gain, w_sgate, shared_weights):
    row_count = tokens.shape[0]
    groups = VH // KH
    normed = scaled_rows(tokens, ln1_gain).astype(jnp.bfloat16)
    proj_qk = jnp.dot(normed, w_qk.reshape(D, 2 * KH * DK), preferred_element_type=jnp.float32).astype(jnp.bfloat16)
    proj_vz = jnp.dot(normed, w_vz.reshape(D, 2 * VH * DV), preferred_element_type=jnp.float32).astype(jnp.bfloat16)
    proj_ba = jnp.dot(normed, w_ba.reshape(D, 2 * VH), preferred_element_type=jnp.float32).astype(jnp.bfloat16)
    owner = jnp.repeat(stretch_prompt, STRETCH)
    mixed_qk = causal_mix(proj_qk, conv_qk.reshape(CONV, 2 * KH * DK), owner)
    mixed_value = causal_mix(proj_vz[:, :VH * DV], conv_value, owner)
    query = unit_rows(mixed_qk[:, :KH * DK].reshape(row_count, KH, DK)) * DK ** (-0.5)
    keys = unit_rows(mixed_qk[:, KH * DK:].reshape(row_count, KH, DK))
    values = mixed_value.reshape(row_count, VH, DV)
    gate_inputs = proj_ba.astype(jnp.float32)
    beta = jax.nn.sigmoid(gate_inputs[:, :VH])
    rate = -jnp.exp(decay_log) * jax.nn.softplus(gate_inputs[:, VH:] + dt_bias)
    earlier = jnp.concatenate([jnp.full((1,), -1, jnp.int32), stretch_prompt[:-1]])
    later = jnp.concatenate([stretch_prompt[1:], jnp.full((1,), -1, jnp.int32)])
    starts = stretch_prompt != earlier
    ends = stretch_prompt != later
    per_stretch = STRETCH // BLOCK
    block_count = row_count // BLOCK
    fresh = ((jnp.arange(per_stretch) == 0)[None, :] & starts[:, None]).reshape(block_count)

    def one_head(head_index):
        key_index = head_index // groups
        head_query = lax.dynamic_index_in_dim(query, key_index, 1, False).reshape(block_count, BLOCK, DK)
        head_keys = lax.dynamic_index_in_dim(keys, key_index, 1, False).reshape(block_count, BLOCK, DK)
        head_values = lax.dynamic_index_in_dim(values, head_index, 1, False).reshape(block_count, BLOCK, DV)
        head_beta = lax.dynamic_index_in_dim(beta, head_index, 1, False).reshape(block_count, BLOCK)
        head_rate = lax.dynamic_index_in_dim(rate, head_index, 1, False).reshape(block_count, BLOCK)
        base, probe, carry_map, carry_add = block_terms(head_query, head_keys, head_values, head_beta, head_rate)

        def advance(state, inputs):
            block_base, block_probe, block_map, block_add, block_fresh = inputs
            opening = jnp.where(block_fresh, 0.0, state)
            produced = block_base + jnp.einsum('id,vd->iv', block_probe, opening, precision=HIGHEST)
            return (matmul_high(opening, block_map) + block_add, produced)
        unused, produced = lax.scan(advance, jnp.zeros((DV, DK), jnp.float32), (base, probe, carry_map, carry_add, fresh))
        return produced.reshape(row_count, DV)
    recurrent = jnp.transpose(lax.map(one_head, jnp.arange(VH, dtype=jnp.int32)), (1, 0, 2))
    fill = jnp.where(ends, last_fill, STRETCH)
    kept = (jnp.arange(STRETCH)[None, :] < fill[:, None]).reshape(row_count)
    recurrent = jnp.where(kept[:, None, None], recurrent, 0.0)
    gating = proj_vz[:, VH * DV:].astype(jnp.float32).reshape(row_count, VH, DV)
    gated = (scaled_rows(recurrent, norm_gain) * jax.nn.silu(gating)).reshape(row_count, VH * DV).astype(jnp.bfloat16)
    width = VH // N_HEAD * DV
    total = jnp.zeros((row_count, D), jnp.float32)
    for group in range(N_HEAD):
        partial_sum = jnp.dot(gated[:, group * width:(group + 1) * width], w_out[group * width:(group + 1) * width], preferred_element_type=jnp.float32)
        total = total + lax.optimization_barrier(partial_sum.astype(jnp.bfloat16)).astype(jnp.float32)
    attention_out = total.astype(jnp.bfloat16)
    residual = (tokens.astype(jnp.float32) + attention_out.astype(jnp.float32)).astype(jnp.bfloat16)
    normed_two = scaled_rows(residual, ln2_gain).astype(jnp.bfloat16)
    expert_gate = jax.nn.sigmoid(jnp.dot(normed_two, w_sgate, preferred_element_type=jnp.float32))
    gate_part = jnp.dot(normed_two, shared_weights[0].T, preferred_element_type=jnp.float32)
    up_part = jnp.dot(normed_two, shared_weights[1].T, preferred_element_type=jnp.float32)
    hidden = (jax.nn.silu(gate_part) * up_part).astype(jnp.bfloat16)
    expert = jnp.dot(hidden, shared_weights[2], preferred_element_type=jnp.float32)
    layer_out = (residual.astype(jnp.float32) + expert_gate[:, None] * expert).astype(jnp.bfloat16)
    return (attention_out, layer_out)
```

```python
import jax
import jax.numpy as jnp
from jax import lax
from jax.experimental import pallas as pl
from jax.experimental.pallas import tpu as pltpu
from jax.sharding import Mesh
from jax.sharding import PartitionSpec as P

F32 = jnp.float32
BF16 = jnp.bfloat16
EPSILON = 1e-06
DK = 128
STRETCH = 512
ROWS = 128
CHUNKS = 8
HEADS = 4
KEYS = 2
NZ, NX, NY, NC = 8, 4, 4, 2
LEAD = 16
COL_V = 256
COL_Q = 768
COL_BA = 1024
COL_Z = 1152
COL_END = 1664
PLACES = {
    (0, 0): (0, 0),
    (0, 1): (0, 1),
    (1, 0): (1, 0),
    (3, 0): (1, 1),
    (1, 1): (1, 2),
    (3, 1): (1, 3),
    (2, 0): (2, 0),
    (2, 1): (2, 1),
}


def dot(left, right, contract=((1,), (0,))):
    return lax.dot_general(left, right, (contract, ((), ())), preferred_element_type=F32)


def silu(value):
    return value * (0.5 * jnp.tanh(0.5 * value) + 0.5)


def sigmoid(value):
    return 0.5 * jnp.tanh(0.5 * value) + 0.5


def scaled_rows(inputs, scaling):
    widened = inputs.astype(F32)
    spread = jnp.mean(widened * widened, axis=-1, keepdims=True)
    return widened * lax.rsqrt(spread + EPSILON) * scaling.astype(F32)


def turn(value, axis, steps, count):
    return lax.ppermute(value, axis, [(i, (i + steps) % count) for i in range(count)])


def push(value, axis, steps, count):
    return lax.ppermute(value, axis, [(i, i + steps) for i in range(count - steps)])


def mixed_rows(ref, chunk, first, last, taps, reset):
    start = pl.multiple_of(chunk * ROWS, ROWS)
    rows = ref[pl.ds(start, ROWS + LEAD), first:last].astype(F32)
    lead = jnp.where(reset, 0.0, rows[:LEAD])
    rows = jnp.concatenate([lead, rows[LEAD:]], axis=0)
    total = rows[LEAD:] * taps[3:4]
    for offset in (1, 2, 3):
        total = total + rows[LEAD - offset : LEAD - offset + ROWS] * taps[3 - offset : 4 - offset]
    return silu(total)


def unit_heads(value):
    parts = []
    for head in range(value.shape[1] // DK):
        part = value[:, head * DK : (head + 1) * DK]
        parts.append(part * lax.rsqrt(jnp.sum(part * part, axis=-1, keepdims=True) + EPSILON))
    return parts


def fetch_rows(scal, pieces, scratch, sems, first, last):
    copies = []
    for place, ((steps, other), (piece, block)) in enumerate(PLACES.items()):
        row = lax.rem(scal[0] + steps, NY)
        core = scal[1] if other == 0 else 1 - scal[1]
        chunk = row * NC + core
        start = pl.multiple_of(chunk * ROWS + LEAD, LEAD)
        copy = pltpu.make_async_copy(
            pieces[piece].at[pl.ds(block * ROWS, ROWS), pl.ds(first, last - first)],
            scratch.at[pl.ds(start, ROWS), :],
            sems.at[place],
        )
        copy.start()
        copies.append(copy)
    for copy in copies:
        copy.wait()


def is_reset(scal, chunk):
    first = jnp.logical_and(chunk == 0, scal[2] > 0)
    second = jnp.logical_and(chunk == CHUNKS // 2, scal[3] > 0)
    return jnp.logical_or(first, second)


def iota2(axis):
    return lax.broadcasted_iota(jnp.int32, (ROWS, ROWS), axis)


def inverse_rest(strict):
    row, col = iota2(0), iota2(1)
    near = jnp.logical_and(row // 2 == col // 2, row != col)
    rest = jnp.where(near, -strict, 0.0)
    span = 2
    while span < ROWS:
        wide = 2 * span
        inside = (row // wide == col // wide) & (row % wide >= span) & (col % wide < span)
        below = jnp.where(inside, strict, 0.0)
        half = below + dot(below.astype(BF16), rest.astype(BF16))
        rest = rest - half - dot(rest.astype(BF16), half.astype(BF16))
        span = wide
    return rest


def state_kernel(
    scal, piece_a, piece_b, piece_c, tail, taps, decay, bias,
    xend, xs, vs, khat, logs, raw, rest, kturn, values, betas, state, sems,
):
    raw[0:LEAD, :] = tail[...]
    fetch_rows(scal, (piece_a, piece_b, piece_c), raw, sems, 0, COL_Z)
    row, col = iota2(0), iota2(1)
    strict = row > col
    summing = (row >= col).astype(F32)

    def prepare(chunk):
        reset = is_reset(scal, chunk)
        mixed = mixed_rows(raw, chunk, 0, COL_Q, taps, reset)
        start = pl.multiple_of(chunk * ROWS + LEAD, LEAD)
        ba = raw[pl.ds(start, ROWS), COL_BA:COL_Z].astype(F32)
        beta = sigmoid(ba)
        inner = ba + bias[...]
        soft = jnp.maximum(inner, 0.0) + jnp.log1p(jnp.exp(-jnp.abs(inner)))
        rate = -jnp.exp(decay[...]) * soft
        log = lax.dot_general(
            summing, rate, (((1,), (0,)), ((), ())),
            precision=lax.Precision.HIGHEST, preferred_element_type=F32,
        )
        log_turned = log.T
        betas[chunk] = beta
        logs[chunk] = log
        unit = unit_heads(mixed[:, :COL_V])
        for key in range(KEYS):
            key_rows = unit[key].astype(BF16)
            khat[chunk, key] = key_rows
            kturn[chunk, key] = unit[key].T.astype(BF16)
            products = dot(key_rows, key_rows, ((1,), (1,)))
            for half in range(2):
                head = 2 * key + half
                beta_col = beta[:, head : head + 1]
                spread = log[:, HEADS + head : HEADS + head + 1] - log_turned[HEADS + head : HEADS + head + 1, :]
                weight = jnp.exp(jnp.minimum(spread, 0.0))
                lower = jnp.where(strict, products * beta_col * weight, 0.0)
                rest[chunk, head] = inverse_rest(lower).astype(BF16)
                value = mixed[:, COL_V + head * DK : COL_V + (head + 1) * DK]
                values[chunk, head] = value * beta_col

    def prepare_two(pair, unused):
        prepare(2 * pair)
        prepare(2 * pair + 1)
        return unused

    lax.fori_loop(0, CHUNKS // 2, prepare_two, 0)

    opening = jnp.where(scal[2] > 0, 0.0, 1.0)
    identity = jnp.where(row == col, opening, 0.0)
    for key in range(KEYS):
        for half in range(2):
            state[key, :, 2 * half * DK : (2 * half + 1) * DK] = jnp.zeros((DK, DK), F32)
            state[key, :, (2 * half + 1) * DK : (2 * half + 2) * DK] = identity

    def advance(chunk, unused):
        reset = jnp.logical_and(chunk == CHUNKS // 2, scal[3] > 0)
        keep = jnp.where(reset, 0.0, 1.0)
        beta = betas[chunk]
        log = logs[chunk]
        growth = jnp.exp(log)
        last = log[ROWS - 1 : ROWS, :]
        shrink = jnp.exp(last - log)
        whole = jnp.exp(last)
        for key in range(KEYS):
            held = state[key] * keep
            held_low = held.astype(BF16)
            xs[chunk, key] = held_low
            seen = dot(khat[chunk, key], held_low)
            updates = []
            scales = []
            for half in range(2):
                head = 2 * key + half
                at = HEADS + head
                factor = beta[:, head : head + 1] * growth[:, at : at + 1]
                part = seen[:, 2 * half * DK : (2 * half + 2) * DK] * factor
                wanted = jnp.concatenate([values[chunk, head] - part[:, :DK], -part[:, DK:]], axis=1)
                solved = wanted + dot(rest[chunk, head], wanted.astype(BF16))
                vs[chunk, head] = solved.astype(BF16)
                updates.append((solved * shrink[:, at : at + 1]).astype(BF16))
                scales.append(jnp.broadcast_to(whole[:, at : at + 1], (1, 2 * DK)))
            scale = jnp.concatenate(scales, axis=1)
            state[key] = held * scale + dot(kturn[chunk, key], jnp.concatenate(updates, axis=1))
        return unused

    lax.fori_loop(0, CHUNKS, advance, 0)
    for key in range(KEYS):
        for half in range(2):
            xend[2 * key + half] = state[key, :, 2 * half * DK : (2 * half + 2) * DK].astype(BF16)


def state_call(scal, pieces, tail, taps, decay, bias):
    vmem = pl.BlockSpec(memory_space=pltpu.VMEM)
    hbm = pl.BlockSpec(memory_space=pl.ANY)
    return pl.pallas_call(
        state_kernel,
        out_shape=(
            jax.ShapeDtypeStruct((HEADS, DK, 2 * DK), BF16),
            jax.ShapeDtypeStruct((CHUNKS, KEYS, DK, 4 * DK), BF16),
            jax.ShapeDtypeStruct((CHUNKS, HEADS, ROWS, 2 * DK), BF16),
            jax.ShapeDtypeStruct((CHUNKS, KEYS, ROWS, DK), BF16),
            jax.ShapeDtypeStruct((CHUNKS, ROWS, 128), F32),
        ),
        in_specs=[pl.BlockSpec(memory_space=pltpu.SMEM), hbm, hbm, hbm] + [vmem] * 4,
        out_specs=[vmem] * 5,
        scratch_shapes=[
            pltpu.VMEM((LEAD + CHUNKS * ROWS, COL_Z), BF16),
            pltpu.VMEM((CHUNKS, HEADS, ROWS, ROWS), BF16),
            pltpu.VMEM((CHUNKS, KEYS, DK, ROWS), BF16),
            pltpu.VMEM((CHUNKS, HEADS, ROWS, DK), F32),
            pltpu.VMEM((CHUNKS, ROWS, 128), F32),
            pltpu.VMEM((KEYS, DK, 4 * DK), F32),
            pltpu.SemaphoreType.DMA((CHUNKS,)),
        ],
        compiler_params=pltpu.CompilerParams(vmem_limit_bytes=40 * 1024 * 1024),
        cost_estimate=pl.CostEstimate(flops=6_000_000_000, bytes_accessed=20_000_000, transcendentals=0),
        name="state",
    )(scal, *pieces, tail, taps, decay, bias)


def read_kernel(
    scal, piece_a, piece_b, piece_c, tail, taps, xs, vs, khat, logs, out, raw, sems,
):
    raw[0:LEAD, :] = tail[...]
    fetch_rows(scal, (piece_a, piece_b, piece_c), raw, sems, COL_Q, COL_BA)
    inclusive = iota2(0) >= iota2(1)

    def one(chunk, unused):
        mixed = mixed_rows(raw, chunk, 0, COL_BA - COL_Q, taps, is_reset(scal, chunk))
        unit = unit_heads(mixed)
        log = logs[chunk]
        log_turned = log.T
        growth = jnp.exp(log)
        steps = lax.rem(chunk // NC - scal[0] + NY, NY)
        other = jnp.bitwise_xor(lax.rem(chunk, NC), scal[1])
        for key in range(KEYS):
            query = (unit[key] * DK ** (-0.5)).astype(BF16)
            seen = dot(query, xs[chunk, key])
            products = dot(query, khat[chunk, key], ((1,), (1,)))
            for half in range(2):
                head = 2 * key + half
                at = HEADS + head
                spread = log[:, at : at + 1] - log_turned[at : at + 1, :]
                scores = jnp.where(inclusive, products * jnp.exp(jnp.minimum(spread, 0.0)), 0.0)
                found = seen[:, 2 * half * DK : (2 * half + 2) * DK] * growth[:, at : at + 1]
                found = found + dot(scores.astype(BF16), vs[chunk, head])
                out[other, steps, head] = found.astype(BF16)
        return unused

    lax.fori_loop(0, CHUNKS, one, 0)


def read_call(scal, pieces, tail, taps, xs, vs, khat, logs):
    vmem = pl.BlockSpec(memory_space=pltpu.VMEM)
    hbm = pl.BlockSpec(memory_space=pl.ANY)
    return pl.pallas_call(
        read_kernel,
        out_shape=jax.ShapeDtypeStruct((NC, NY, HEADS, ROWS, 2 * DK), BF16),
        in_specs=[pl.BlockSpec(memory_space=pltpu.SMEM), hbm, hbm, hbm] + [vmem] * 6,
        out_specs=vmem,
        scratch_shapes=[
            pltpu.VMEM((LEAD + CHUNKS * ROWS, COL_BA - COL_Q), BF16),
            pltpu.SemaphoreType.DMA((CHUNKS,)),
        ],
        compiler_params=pltpu.CompilerParams(vmem_limit_bytes=40 * 1024 * 1024),
        cost_estimate=pl.CostEstimate(flops=3_000_000_000, bytes_accessed=20_000_000, transcendentals=0),
        name="read",
    )(scal, *pieces, tail, taps, xs, vs, khat, logs)


def after(late, early):
    moved = dot(late[:, DK:], early)
    if early.shape[1] == DK:
        return moved + late[:, :DK].astype(F32)
    return jnp.concatenate([moved[:, :DK] + late[:, :DK].astype(F32), moved[:, DK:]], axis=1)


def row_kernel(parts, leads):
    held = parts[0]
    leads[0] = held
    for place in range(1, NX):
        held = after(parts[place], held).astype(BF16)
        leads[place] = held


def pair_kernel(near, far, both):
    both[...] = after(near[...], far[...]).astype(BF16)


def open_kernel(pair, far, leads, out):
    opening = after(pair[...], far[...]).astype(BF16)
    out[0] = opening
    for place in range(1, NX):
        out[place] = after(leads[place - 1], opening).astype(BF16)


def small_call(kernel, out_shape, *args):
    return pl.pallas_call(
        kernel,
        out_shape=jax.ShapeDtypeStruct(out_shape, BF16),
        cost_estimate=pl.CostEstimate(flops=100_000_000, bytes_accessed=1_000_000, transcendentals=0),
        name="link",
    )(*args)


def out_kernel(other, scal, found, gates, opening, gain, w_out, out):
    steps = pl.program_id(0)
    row = lax.rem(scal[0] + steps, NY)
    core = scal[1] if other == 0 else 1 - scal[1]
    chunk = row * NC + core
    first = lax.rem(chunk, STRETCH // ROWS) * ROWS
    fill = jnp.where(chunk < CHUNKS // 2, scal[4], scal[5])
    within = lax.broadcasted_iota(jnp.int32, (ROWS, 1), 0) + first
    kept = within < fill
    parts = []
    for head in range(HEADS):
        both = found[head]
        value = both[:, :DK].astype(F32) + dot(both[:, DK:], opening[head])
        value = jnp.where(kept, value, 0.0)
        gate = gates[:, head * DK : (head + 1) * DK].astype(F32)
        spread = jnp.mean(value * value, axis=-1, keepdims=True)
        parts.append((value * lax.rsqrt(spread + EPSILON) * gain[...] * silu(gate)).astype(BF16))
    out[...] = dot(jnp.concatenate(parts, axis=1), w_out[...]).astype(BF16)


def out_call(other, scal, found, gates, opening, gain, w_out):
    width = w_out.shape[1]
    return pl.pallas_call(
        lambda *refs: out_kernel(other, *refs),
        grid=(NY,),
        out_shape=jax.ShapeDtypeStruct((NY, ROWS, width), BF16),
        in_specs=[
            pl.BlockSpec(memory_space=pltpu.SMEM),
            pl.BlockSpec((None, None, HEADS, ROWS, 2 * DK), lambda i: (other, i, 0, 0, 0)),
            pl.BlockSpec((None, ROWS, HEADS * DK), lambda i: (i, 0, 0)),
            pl.BlockSpec((HEADS, DK, DK), lambda i: (0, 0, 0)),
            pl.BlockSpec((1, DK), lambda i: (0, 0)),
            pl.BlockSpec((HEADS * DK, width), lambda i: (0, 0)),
        ],
        out_specs=pl.BlockSpec((None, ROWS, width), lambda i: (i, 0, 0)),
        compiler_params=pltpu.CompilerParams(vmem_limit_bytes=40 * 1024 * 1024),
        cost_estimate=pl.CostEstimate(flops=1_200_000_000, bytes_accessed=6_000_000, transcendentals=0),
        name="out",
    )(scal, found, gates, opening, gain, w_out)


def per_device(
    tokens,
    stretch_prompt,
    last_fill,
    ln1_gain,
    w_qk,
    w_vz,
    w_ba,
    conv_qk,
    conv_value,
    decay_log,
    dt_bias,
    norm_gain,
    w_out,
    ln2_gain,
    w_sgate,
    shared_weights,
):
    width = tokens.shape[1]
    place_y = lax.axis_index("y")
    place_core = lax.axis_index("core")
    device = lax.axis_index("z") * NX + lax.axis_index("x")
    normed = scaled_rows(tokens, ln1_gain).astype(BF16)

    below = turn(normed, "y", 1, NY)
    above = turn(normed, "y", -1, NY)
    beside = turn(normed, "core", 1, NC)
    across_up = turn(below[: ROWS // 2], "y", 1, NY)
    across_down = turn(above[ROWS // 2 :], "y", -1, NY)
    middle = jnp.concatenate([above, below], axis=0)
    middle_beside = turn(middle, "core", 1, NC)
    across = jnp.concatenate([across_up, across_down], axis=0)
    across_beside = turn(across, "core", 1, NC)

    weight = jnp.concatenate(
        [
            w_qk[:, 1, :],
            w_vz[:, 0, :],
            w_qk[:, 0, :],
            w_ba.reshape(width, 2 * HEADS),
            jnp.zeros((width, COL_Z - COL_BA - 2 * HEADS), BF16),
            w_vz[:, 1, :],
        ],
        axis=1,
    )

    def project(rows):
        return jnp.dot(rows, weight, preferred_element_type=F32).astype(BF16)

    pieces = (
        project(jnp.concatenate([normed, beside], axis=0)),
        project(jnp.concatenate([middle, middle_beside], axis=0)),
        project(jnp.concatenate([across, across_beside], axis=0)),
    )

    ends = [None] * (NY * NC)
    for (steps, other), (piece, block) in PLACES.items():
        ends[steps * NC + other] = pieces[piece][(block + 1) * ROWS - LEAD : (block + 1) * ROWS, :COL_BA]
    last_place = lax.rem(NY - 1 - place_y + NY, NY) * NC + (NC - 1 - place_core)
    tail = push(lax.dynamic_index_in_dim(jnp.stack(ends), last_place, 0, False), ("z", "x"), 1, NZ * NX)

    first_slot = device * 2
    before = jnp.concatenate([jnp.full((1,), -1, jnp.int32), stretch_prompt])
    later = jnp.concatenate([stretch_prompt, jnp.full((1,), -1, jnp.int32)])
    current = lax.dynamic_slice_in_dim(stretch_prompt, first_slot, 2)
    starts = current != lax.dynamic_slice_in_dim(before, first_slot, 2)
    finishes = current != lax.dynamic_slice_in_dim(later, first_slot + 1, 2)
    fill = jnp.where(finishes, lax.dynamic_slice_in_dim(last_fill, first_slot, 2), STRETCH)
    scal = jnp.concatenate(
        [jnp.stack([place_y, place_core]).astype(jnp.int32), starts.astype(jnp.int32), fill]
    )

    taps_qk = conv_qk.astype(F32)
    taps_kv = jnp.concatenate([taps_qk[:, 1, :], conv_value.astype(F32)], axis=1)
    pad = ((HEADS, 128 - 2 * HEADS),)
    decay = jnp.pad(decay_log, pad)[None, :]
    bias = jnp.pad(dt_bias, pad)[None, :]
    tail_all = jnp.pad(tail, ((0, 0), (0, COL_Z - COL_BA)))
    xend, xs, vs, khat, logs = state_call(scal, pieces, tail_all, taps_kv, decay, bias)

    parts = lax.all_to_all(xend, "x", 0, 0, tiled=True)
    leads = small_call(row_kernel, (NX, DK, 2 * DK), parts)
    near = push(leads[NX - 1], "z", 1, NZ)
    far = push(leads[NX - 1], "z", 2, NZ)
    both = small_call(pair_kernel, (DK, 2 * DK), near, far)
    farther = push(both[:, :DK], "z", 2, NZ)
    openings = small_call(open_kernel, (NX, DK, DK), both, farther, leads)
    opening = lax.all_to_all(openings, "x", 0, 0, tiled=True)

    found = read_call(scal, pieces, tail[:, COL_Q:], taps_qk[:, 0, :], xs, vs, khat, logs)

    def gates_of(other):
        picked = []
        for steps in range(NY):
            piece, block = PLACES[(steps, other)]
            picked.append(pieces[piece][block * ROWS : (block + 1) * ROWS, COL_Z:])
        return jnp.stack(picked)

    gain = norm_gain.astype(F32)[None, :]
    given = out_call(1, scal, found, gates_of(1), opening, gain, w_out)
    received = turn(given, "core", 1, NC)
    own = out_call(0, scal, found, gates_of(0), opening, gain, w_out)

    def add(left, right):
        return (left.astype(F32) + right.astype(F32)).astype(BF16)

    summed = add(own, received)
    half = width // 2
    pass_up = turn(summed[2, :, :half], "y", 1, NY)
    pass_down = turn(summed[2, :, half:], "y", -1, NY)
    up = jnp.concatenate([add(summed[1, :, :half], pass_up), summed[1, :, half:]], axis=1)
    down = jnp.concatenate([summed[3, :, :half], add(summed[3, :, half:], pass_down)], axis=1)
    got_up = turn(up, "y", 1, NY)
    got_down = turn(down, "y", -1, NY)
    attention_out = (summed[0].astype(F32) + got_up.astype(F32) + got_down.astype(F32)).astype(BF16)

    residual = add(tokens, attention_out)
    normed_two = scaled_rows(residual, ln2_gain).astype(BF16)
    expert_gate = jax.nn.sigmoid(jnp.dot(normed_two, w_sgate, preferred_element_type=F32))
    gathered = lax.all_gather(shared_weights, ("y", "core"), axis=1, tiled=True)
    gate_part = jnp.einsum("rd,fd->rf", normed_two, gathered[0], preferred_element_type=F32)
    up_part = jnp.einsum("rd,fd->rf", normed_two, gathered[1], preferred_element_type=F32)
    hidden = (jax.nn.silu(gate_part) * up_part).astype(BF16)
    expert = jnp.dot(hidden, gathered[2], preferred_element_type=F32)
    layer_out = (residual.astype(F32) + expert_gate[:, None] * expert).astype(BF16)
    return (attention_out, layer_out)


def solution(mesh):
    fine = Mesh(mesh.devices.reshape(NZ, NX, NY, NC), ("z", "x", "y", "core"))
    rows = P(("z", "x", "y", "core"), None)
    head = ("y", "core")
    return jax.shard_map(
        per_device,
        mesh=fine,
        in_specs=(
            rows,
            P(),
            P(),
            P(),
            P(None, None, head),
            P(None, None, head),
            P(None, None, head),
            P(None, None, head),
            P(None, head),
            P(head),
            P(head),
            P(),
            P(head, None),
            P(),
            P(),
            P(None, head, None),
        ),
        out_specs=(rows, rows),
        check_vma=False,
    )
```

```python
import itertools

import jax
import jax.numpy as jnp
from jax import lax
from jax.experimental import pallas as pl
from jax.experimental.pallas import tpu as pltpu
from jax.sharding import Mesh
from jax.sharding import PartitionSpec as P

F32 = jnp.float32
BF16 = jnp.bfloat16
EPSILON = 1e-06
DK = 128
STRETCH = 512
ROWS = 128
CHUNKS = 8
HEADS = 4
KEYS = 2
NZ, NX, NY, NC = 8, 4, 4, 2
LEAD = 16
COL_K = 256
COL_V = 512
COL_BA = 1024
COL_END = 1152
MIB = 1024 * 1024
PLACES = {
    (0, 0): (0, 0),
    (0, 1): (0, 1),
    (1, 0): (1, 0),
    (3, 0): (1, 1),
    (1, 1): (1, 2),
    (3, 1): (1, 3),
    (2, 0): (2, 0),
    (2, 1): (2, 1),
}


def dot(left, right, contract=((1,), (0,))):
    return lax.dot_general(left, right, (contract, ((), ())), preferred_element_type=F32)


def silu(value):
    return value * (0.5 * jnp.tanh(0.5 * value) + 0.5)


def sigmoid(value):
    return 0.5 * jnp.tanh(0.5 * value) + 0.5


def scaled_rows(inputs, scaling):
    widened = inputs.astype(F32)
    spread = jnp.mean(widened * widened, axis=-1, keepdims=True)
    return widened * lax.rsqrt(spread + EPSILON) * scaling.astype(F32)


def hold(value):
    return pltpu.with_memory_space_constraint(value, pltpu.HBM)


def turn(value, axis, steps, count):
    return lax.ppermute(value, axis, [(i, (i + steps) % count) for i in range(count)])


def push(value, axis, steps, count):
    return lax.ppermute(value, axis, [(i, i + steps) for i in range(count - steps)])


def mixed_rows(ref, chunk, first, last, taps, reset):
    start = chunk * ROWS
    rows = ref[pl.ds(start, ROWS + LEAD), first:last].astype(F32)
    if reset is not False:
        rows = jnp.concatenate([jnp.where(reset, 0.0, rows[:LEAD]), rows[LEAD:]], axis=0)
    total = rows[LEAD:] * taps[3:4]
    for offset in (1, 2, 3):
        total = total + rows[LEAD - offset : LEAD - offset + ROWS] * taps[3 - offset : 4 - offset]
    return silu(total)


def unit_heads(value):
    parts = []
    for head in range(value.shape[1] // DK):
        part = value[:, head * DK : (head + 1) * DK]
        parts.append(part * lax.rsqrt(jnp.sum(part * part, axis=-1, keepdims=True) + EPSILON))
    return parts


def fetch_rows(scal, pieces, scratch, sems, first, last, target):
    copies = []
    for (steps, other), (piece, block) in PLACES.items():
        row = lax.rem(scal[0] + steps, NY)
        core = scal[1] if other == 0 else 1 - scal[1]
        chunk = row * NC + core
        start = pl.multiple_of(chunk * ROWS + LEAD, LEAD)
        copy = pltpu.make_async_copy(
            pieces[piece].at[pl.ds(block * ROWS, ROWS), pl.ds(first, last - first)],
            scratch.at[pl.ds(start, ROWS), pl.ds(target, last - first)],
            sems.at[len(copies)],
        )
        copy.start()
        copies.append(copy)
    for copy in copies:
        copy.wait()


def is_reset(scal, chunk):
    if isinstance(chunk, int):
        return scal[2 + chunk * 2 // CHUNKS] > 0 if chunk % (CHUNKS // 2) == 0 else False
    first = jnp.logical_and(chunk == 0, scal[2] > 0)
    second = jnp.logical_and(chunk == CHUNKS // 2, scal[3] > 0)
    return jnp.logical_or(first, second)


def iota2(axis):
    return lax.broadcasted_iota(jnp.int32, (ROWS, ROWS), axis)


def odd_blocks(value, span):
    return jnp.concatenate([value[at : at + span] for at in range(span, ROWS, 2 * span)], axis=0)


def with_even(even, odd, span):
    parts = []
    for place, at in enumerate(range(0, ROWS, 2 * span)):
        block = odd[place * span : (place + 1) * span]
        parts.append(jnp.zeros_like(block) if even is None else even[at : at + span])
        parts.append(block)
    return jnp.concatenate(parts, axis=0)


def inverse_rests(stricts, level):
    rests = [jnp.where(level == 1, -strict, 0.0) for strict in stricts]
    for step in (2, 3):
        lows = [rest.astype(BF16) for rest in rests]
        belows = [jnp.where(level == step, strict, 0.0) for strict in stricts]
        halves = [below + dot(below.astype(BF16), low) for below, low in zip(belows, lows)]
        yield
        rests = [rest - half - dot(low, half.astype(BF16)) for rest, half, low in zip(rests, halves, lows)]
        yield
    for step in (4, 5, 6, 7):
        span = 1 << (step - 1)
        here = odd_blocks(level, span) == step
        lows = [rest.astype(BF16) for rest in rests]
        odds = [odd_blocks(rest, span) for rest in rests]
        belows = [jnp.where(here, odd_blocks(strict, span), 0.0) for strict in stricts]
        halves = [below + dot(below.astype(BF16), low) for below, low in zip(belows, lows)]
        yield
        wides = [with_even(None, half, span).astype(BF16) for half in halves]
        odds = [odd - half - dot(odd.astype(BF16), wide) for odd, half, wide in zip(odds, halves, wides)]
        rests = [with_even(rest, odd, span) for rest, odd in zip(rests, odds)]
        yield
    return rests


def block_levels():
    row, col = iota2(0), iota2(1)
    apart = jnp.where(row > col, jnp.bitwise_xor(row, col), 0)
    level = jnp.zeros((ROWS, ROWS), jnp.int32)
    for step in range(7):
        level = level + (apart >= (1 << step)).astype(jnp.int32)
    return level


def state_kernel(
    scal, piece_a, piece_b, piece_c, tail, taps, decay, bias,
    xend, xs_out, vs_out, khat_out, logs_out,
    raw, rest, kturn, values, betas, state, xs, vs, khat, logs, sems, out_sems,
):
    raw[0:LEAD, 0:COL_BA] = tail[...]
    fetch_rows(scal, (piece_a, piece_b, piece_c), raw, sems, COL_K, COL_END, COL_K)
    row, col = iota2(0), iota2(1)
    strict = row > col
    summing = (row >= col).astype(F32)
    level = block_levels()

    def prepare(chunk):
        reset = is_reset(scal, chunk)
        mixed = mixed_rows(raw, chunk, COL_K, COL_BA, taps, reset)
        start = chunk * ROWS + LEAD
        ba = raw[pl.ds(start, ROWS), COL_BA:COL_END].astype(F32)
        beta = sigmoid(ba)
        inner = ba + bias[...]
        soft = jnp.maximum(inner, 0.0) + jnp.log1p(jnp.exp(-jnp.abs(inner)))
        rate = -jnp.exp(decay[...]) * soft
        log = lax.dot_general(
            summing, rate, (((1,), (0,)), ((), ())),
            precision=lax.Precision.HIGHEST, preferred_element_type=F32,
        )
        log_turned = log.T
        betas[chunk] = beta
        logs[chunk] = log
        unit = unit_heads(mixed[:, : KEYS * DK])
        lowers = []
        for key in range(KEYS):
            key_rows = unit[key].astype(BF16)
            khat[chunk, key] = key_rows
            kturn[chunk, key] = unit[key].T.astype(BF16)
            products = dot(key_rows, key_rows, ((1,), (1,)))
            for half in range(2):
                head = 2 * key + half
                beta_col = beta[:, head : head + 1]
                spread = log[:, HEADS + head : HEADS + head + 1] - log_turned[HEADS + head : HEADS + head + 1, :]
                weight = jnp.exp(jnp.minimum(spread, 0.0))
                lower = jnp.where(strict, products * beta_col * weight, 0.0)
                lowers.append(lower)
                value = mixed[:, (KEYS + head) * DK : (KEYS + head + 1) * DK]
                values[chunk, head] = value * beta_col
        return lowers

    def prepare_all(chunks):
        lowers = []
        for chunk in chunks:
            lowers += prepare(chunk)
            yield
        found = yield from inverse_rests(lowers, level)
        for place, value in enumerate(found):
            rest[chunks[place // HEADS], place % HEADS] = value.astype(BF16)

    opening = jnp.where(scal[2] > 0, 0.0, 1.0)
    identity = jnp.where(row == col, opening, 0.0)
    for key in range(KEYS):
        for half in range(2):
            state[key, :, 2 * half * DK : (2 * half + 1) * DK] = jnp.zeros((DK, DK), F32)
            state[key, :, (2 * half + 1) * DK : (2 * half + 2) * DK] = identity

    def advance(chunk):
        beta = betas[chunk]
        log = logs[chunk]
        growth = jnp.exp(log)
        last = log[ROWS - 1 : ROWS, :]
        shrink = jnp.exp(last - log)
        whole = jnp.exp(last)
        held = [state[key] for key in range(KEYS)]
        if chunk == CHUNKS // 2:
            held = [jnp.where(scal[3] > 0, 0.0, value) for value in held]
        lows = [value.astype(BF16) for value in held]
        for key in range(KEYS):
            xs[chunk, key] = lows[key]
        seen = [dot(khat[chunk, key], lows[key]) for key in range(KEYS)]
        yield
        wanted = []
        for head in range(HEADS):
            at = HEADS + head
            half = head % 2
            factor = beta[:, head : head + 1] * growth[:, at : at + 1]
            part = seen[head // 2][:, 2 * half * DK : (2 * half + 2) * DK] * factor
            wanted.append(jnp.concatenate([values[chunk, head] - part[:, :DK], -part[:, DK:]], axis=1))
        solved = [
            value + dot(rest[chunk, head], value.astype(BF16)) for head, value in enumerate(wanted)
        ]
        yield
        updates = []
        scales = []
        for head in range(HEADS):
            at = HEADS + head
            vs[chunk, head] = solved[head].astype(BF16)
            updates.append((solved[head] * shrink[:, at : at + 1]).astype(BF16))
            scales.append(jnp.broadcast_to(whole[:, at : at + 1], (1, 2 * DK)))
        for key in range(KEYS):
            scale = jnp.concatenate(scales[2 * key : 2 * key + 2], axis=1)
            update = jnp.concatenate(updates[2 * key : 2 * key + 2], axis=1)
            state[key] = held[key] * scale + dot(kturn[chunk, key], update)
        for copy in copies_out(chunk):
            copy.start()
        yield

    def advance_all(chunks):
        for chunk in chunks:
            yield from advance(chunk)

    def copies_out(chunk):
        return [
            pltpu.make_async_copy(held.at[chunk], target.at[chunk], out_sems.at[place, chunk])
            for place, (held, target) in enumerate(((xs, xs_out), (vs, vs_out), (khat, khat_out), (logs, logs_out)))
        ]

    early, late = list(range(CHUNKS // 2)), list(range(CHUNKS // 2, CHUNKS))
    for unused in prepare_all(early):
        pass
    for unused in itertools.zip_longest(prepare_all(late), advance_all(early)):
        pass
    for unused in advance_all(late):
        pass
    for key in range(KEYS):
        for half in range(2):
            xend[2 * key + half] = state[key, :, 2 * half * DK : (2 * half + 2) * DK].astype(BF16)
    for chunk in range(CHUNKS):
        for copy in copies_out(chunk):
            copy.wait()


def state_call(scal, pieces, tail, taps, decay, bias):
    vmem = pl.BlockSpec(memory_space=pltpu.VMEM)
    hbm = pl.BlockSpec(memory_space=pltpu.HBM)
    return pl.pallas_call(
        state_kernel,
        out_shape=(
            jax.ShapeDtypeStruct((HEADS, DK, 2 * DK), BF16),
            pltpu.HBM((CHUNKS, KEYS, DK, 4 * DK), BF16),
            pltpu.HBM((CHUNKS, HEADS, ROWS, 2 * DK), BF16),
            pltpu.HBM((CHUNKS, KEYS, ROWS, DK), BF16),
            pltpu.HBM((CHUNKS, ROWS, 128), F32),
        ),
        in_specs=[pl.BlockSpec(memory_space=pltpu.SMEM), hbm, hbm, hbm] + [vmem] * 4,
        out_specs=[vmem] + [hbm] * 4,
        scratch_shapes=[
            pltpu.VMEM((LEAD + CHUNKS * ROWS, COL_END), BF16),
            pltpu.VMEM((CHUNKS, HEADS, ROWS, ROWS), BF16),
            pltpu.VMEM((CHUNKS, KEYS, DK, ROWS), BF16),
            pltpu.VMEM((CHUNKS, HEADS, ROWS, DK), F32),
            pltpu.VMEM((CHUNKS, ROWS, 128), F32),
            pltpu.VMEM((KEYS, DK, 4 * DK), F32),
            pltpu.VMEM((CHUNKS, KEYS, DK, 4 * DK), BF16),
            pltpu.VMEM((CHUNKS, HEADS, ROWS, 2 * DK), BF16),
            pltpu.VMEM((CHUNKS, KEYS, ROWS, DK), BF16),
            pltpu.VMEM((CHUNKS, ROWS, 128), F32),
            pltpu.SemaphoreType.DMA((CHUNKS,)),
            pltpu.SemaphoreType.DMA((4, CHUNKS)),
        ],
        compiler_params=pltpu.CompilerParams(vmem_limit_bytes=40 * MIB),
        cost_estimate=pl.CostEstimate(flops=6_000_000_000, bytes_accessed=20_000_000, transcendentals=0),
        name="state",
    )(scal, *map(hold, pieces), tail, taps, decay, bias)


def read_kernel(
    scal, piece_a, piece_b, piece_c, tail, taps, xs, vs, khat, logs, out, raw, sems,
):
    step = pl.program_id(0)

    @pl.when(step == 0)
    def _():
        raw[0:LEAD, :] = tail[...]
        fetch_rows(scal, (piece_a, piece_b, piece_c), raw, sems, 0, COL_K, 0)

    inclusive = iota2(0) >= iota2(1)
    queries, weights, growths = [], [], []
    for core in range(NC):
        chunk = NC * step + core
        start = pl.multiple_of(chunk * ROWS, ROWS)
        reset = is_reset(scal, chunk) if core == 0 else False
        mixed = mixed_rows(raw.at[pl.ds(start, ROWS + LEAD)], 0, 0, COL_K, taps, reset)
        queries += [(value * DK ** (-0.5)).astype(BF16) for value in unit_heads(mixed)]
        log = logs[core]
        log_turned = log.T
        growth = jnp.exp(log)
        for head in range(HEADS):
            at = HEADS + head
            growths.append(growth[:, at : at + 1])
            spread = log[:, at : at + 1] - log_turned[at : at + 1, :]
            weights.append(jnp.where(inclusive, jnp.exp(jnp.minimum(spread, 0.0)), 0.0))
    pairs = [(core, key) for core in range(NC) for key in range(KEYS)]
    products = [dot(queries[i], khat[core, key], ((1,), (1,))) for i, (core, key) in enumerate(pairs)]
    seen = [dot(queries[i], xs[core, key]) for i, (core, key) in enumerate(pairs)]
    for core in range(NC):
        other = jnp.bitwise_xor(core, scal[1])
        for head in range(HEADS):
            pair = core * KEYS + head // 2
            half = head % 2
            scores = (products[pair] * weights[core * HEADS + head]).astype(BF16)
            found = seen[pair][:, 2 * half * DK : (2 * half + 2) * DK] * growths[core * HEADS + head]
            out[other, head] = (found + dot(scores, vs[core, head])).astype(BF16)


def read_call(scal, pieces, tail, taps, xs, vs, khat, logs):
    hbm = pl.BlockSpec(memory_space=pltpu.HBM)
    return pl.pallas_call(
        read_kernel,
        out_shape=pltpu.HBM((NC, NY, HEADS, ROWS, 2 * DK), BF16),
        grid_spec=pltpu.PrefetchScalarGridSpec(
            num_scalar_prefetch=1,
            grid=(CHUNKS // NC,),
            in_specs=[
                hbm,
                hbm,
                hbm,
                pl.BlockSpec((LEAD, COL_K), lambda c, scal: (0, 0)),
                pl.BlockSpec((4, COL_K), lambda c, scal: (0, 0)),
                pl.BlockSpec((NC, KEYS, DK, 4 * DK), lambda c, scal: (c, 0, 0, 0)),
                pl.BlockSpec((NC, HEADS, ROWS, 2 * DK), lambda c, scal: (c, 0, 0, 0)),
                pl.BlockSpec((NC, KEYS, ROWS, DK), lambda c, scal: (c, 0, 0, 0)),
                pl.BlockSpec((NC, ROWS, 128), lambda c, scal: (c, 0, 0)),
            ],
            out_specs=pl.BlockSpec(
                (NC, None, HEADS, ROWS, 2 * DK),
                lambda c, scal: (0, lax.rem(c - scal[0] + NY, NY), 0, 0, 0),
            ),
            scratch_shapes=[
                pltpu.VMEM((LEAD + CHUNKS * ROWS, COL_K), BF16),
                pltpu.SemaphoreType.DMA((CHUNKS,)),
            ],
        ),
        compiler_params=pltpu.CompilerParams(vmem_limit_bytes=32 * MIB),
        cost_estimate=pl.CostEstimate(flops=3_000_000_000, bytes_accessed=20_000_000, transcendentals=0),
        name="read",
    )(scal, *map(hold, pieces), tail, taps, hold(xs), hold(vs), hold(khat), hold(logs))


def norm_kernel(tokens, gain, out):
    out[...] = scaled_rows(tokens[...], gain[...][None, :]).astype(BF16)


def norm_call(tokens, gain):
    vmem = pl.BlockSpec(memory_space=pltpu.VMEM)
    return pl.pallas_call(
        norm_kernel,
        out_shape=jax.ShapeDtypeStruct(tokens.shape, BF16),
        in_specs=[vmem, vmem],
        out_specs=vmem,
        cost_estimate=pl.CostEstimate(flops=1_000_000, bytes_accessed=1_000_000, transcendentals=0),
        name="norm",
    )(tokens, gain)


def after(late, early):
    moved = dot(late[:, DK:], early)
    if early.shape[1] == DK:
        return moved + late[:, :DK].astype(F32)
    return jnp.concatenate([moved[:, :DK] + late[:, :DK].astype(F32), moved[:, DK:]], axis=1)


def row_kernel(parts, leads, whole, sums):
    held = parts[0]
    leads[0] = held
    for place in range(1, NX):
        held = after(parts[place], held).astype(BF16)
        if place < NX - 1:
            leads[place] = held
    whole[...] = held
    sums[...] = held[:, :DK]


def row_call(parts):
    vmem = pl.BlockSpec(memory_space=pltpu.VMEM)
    return pl.pallas_call(
        row_kernel,
        out_shape=(
            jax.ShapeDtypeStruct((NX - 1, DK, 2 * DK), BF16),
            jax.ShapeDtypeStruct((DK, 2 * DK), BF16),
            jax.ShapeDtypeStruct((DK, DK), BF16),
        ),
        in_specs=[vmem],
        out_specs=[vmem] * 3,
        cost_estimate=pl.CostEstimate(flops=100_000_000, bytes_accessed=1_000_000, transcendentals=0),
        name="rows",
    )(parts)


def open_kernel(one, two, three, four, leads, out):
    opening = four[...]
    for earlier in (three, two, one):
        opening = after(earlier[...], opening).astype(BF16)
    out[0] = opening
    for place in range(1, NX):
        out[place] = after(leads[place - 1], opening).astype(BF16)


def open_call(earlier, leads):
    vmem = pl.BlockSpec(memory_space=pltpu.VMEM)
    return pl.pallas_call(
        open_kernel,
        out_shape=jax.ShapeDtypeStruct((NX, DK, DK), BF16),
        in_specs=[vmem] * 5,
        out_specs=vmem,
        cost_estimate=pl.CostEstimate(flops=100_000_000, bytes_accessed=1_000_000, transcendentals=0),
        name="open",
    )(*earlier, leads)


def out_kernel(other, scal, found, gates, opening, gain, w_out, out):
    rows = []
    moved = [
        [dot(found[block, head][:, DK:], opening[head]) for head in range(HEADS)]
        for block in range(2)
    ]
    for block in range(2):
        steps = 2 * pl.program_id(0) + block
        core = scal[1] if other == 0 else 1 - scal[1]
        chunk = lax.rem(scal[0] + steps, NY) * NC + core
        first = lax.rem(chunk, STRETCH // ROWS) * ROWS
        fill = jnp.where(chunk < CHUNKS // 2, scal[4], scal[5])
        within = lax.broadcasted_iota(jnp.int32, (ROWS, 1), 0) + first
        kept = within < fill
        parts = []
        for head in range(HEADS):
            value = found[block, head][:, :DK].astype(F32) + moved[block][head]
            value = jnp.where(kept, value, 0.0)
            gate = gates[block, :, head * DK : (head + 1) * DK].astype(F32)
            spread = jnp.mean(value * value, axis=-1, keepdims=True)
            parts.append((value * lax.rsqrt(spread + EPSILON) * gain[...] * silu(gate)).astype(BF16))
        rows.append(jnp.concatenate(parts, axis=1))
    total = dot(jnp.concatenate(rows, axis=0), w_out[...]).astype(BF16)
    out[...] = total.reshape(out.shape)


def out_call(other, scal, found, gates, opening, gain, w_out):
    width = w_out.shape[1]
    return pl.pallas_call(
        lambda *refs: out_kernel(other, *refs),
        grid=(NY // 2,),
        out_shape=jax.ShapeDtypeStruct((NY, ROWS, width), BF16),
        in_specs=[
            pl.BlockSpec(memory_space=pltpu.SMEM),
            pl.BlockSpec((None, 2, HEADS, ROWS, 2 * DK), lambda i: (other, i, 0, 0, 0)),
            pl.BlockSpec((2, ROWS, HEADS * DK), lambda i: (i, 0, 0)),
            pl.BlockSpec((HEADS, DK, DK), lambda i: (0, 0, 0)),
            pl.BlockSpec((1, DK), lambda i: (0, 0)),
            pl.BlockSpec((HEADS * DK, width), lambda i: (0, 0)),
        ],
        out_specs=pl.BlockSpec((2, ROWS, width), lambda i: (i, 0, 0)),
        compiler_params=pltpu.CompilerParams(vmem_limit_bytes=32 * MIB),
        cost_estimate=pl.CostEstimate(flops=1_200_000_000, bytes_accessed=6_000_000, transcendentals=0),
        name="out",
    )(scal, hold(found), hold(gates), opening, gain, hold(w_out))


def expert_kernel(
    summed, got_up, got_down, tokens, gain, w_sgate, shared, attention, layer, weights, sems
):
    copies = [pltpu.make_async_copy(shared.at[i], weights.at[i], sems.at[i]) for i in range(3)]
    for copy in copies:
        copy.start()
    total = summed[...].astype(F32) + got_up[...].astype(F32) + got_down[...].astype(F32)
    total = total.astype(BF16)
    attention[...] = total
    residual = (tokens[...].astype(F32) + total.astype(F32)).astype(BF16)
    normed = scaled_rows(residual, gain[...][None, :]).astype(BF16)
    weighed = normed.astype(F32) * w_sgate[...][None, :].astype(F32)
    gate = sigmoid(jnp.sum(weighed, axis=-1, keepdims=True))
    copies[0].wait()
    gate_part = dot(normed, weights[0], ((1,), (1,)))
    copies[1].wait()
    up_part = dot(normed, weights[1], ((1,), (1,)))
    hidden = (silu(gate_part) * up_part).astype(BF16)
    copies[2].wait()
    layer[...] = (residual.astype(F32) + gate * dot(hidden, weights[2])).astype(BF16)


def expert_call(summed, got_up, got_down, tokens, gain, w_sgate, shared):
    vmem = pl.BlockSpec(memory_space=pltpu.VMEM)
    return pl.pallas_call(
        expert_kernel,
        out_shape=(jax.ShapeDtypeStruct(tokens.shape, BF16),) * 2,
        in_specs=[vmem] * 6 + [pl.BlockSpec(memory_space=pltpu.HBM)],
        out_specs=[vmem] * 2,
        scratch_shapes=[pltpu.VMEM(shared.shape, BF16), pltpu.SemaphoreType.DMA((3,))],
        compiler_params=pltpu.CompilerParams(vmem_limit_bytes=32 * MIB),
        cost_estimate=pl.CostEstimate(flops=800_000_000, bytes_accessed=9_000_000, transcendentals=0),
        name="expert",
    )(summed, got_up, got_down, tokens, gain, w_sgate, hold(shared))


def per_device(
    tokens,
    stretch_prompt,
    last_fill,
    ln1_gain,
    w_qk,
    w_vz,
    w_ba,
    conv_qk,
    conv_value,
    decay_log,
    dt_bias,
    norm_gain,
    w_out,
    ln2_gain,
    w_sgate,
    shared_weights,
):
    width = tokens.shape[1]
    place_y = lax.axis_index("y")
    place_core = lax.axis_index("core")
    device = lax.axis_index("z") * NX + lax.axis_index("x")
    normed = norm_call(tokens, ln1_gain)

    below = turn(normed, "y", 1, NY)
    above = turn(normed, "y", -1, NY)
    beside = turn(normed, "core", 1, NC)
    flat_vz = w_vz.reshape(width, -1)
    half_vz = flat_vz.shape[1] // 2
    weight = jnp.concatenate(
        [
            w_qk.reshape(width, -1),
            flat_vz[:, :half_vz],
            jnp.pad(w_ba.reshape(width, -1), ((0, 0), (0, 128 - 2 * HEADS))),
        ],
        axis=1,
    )
    weight_z = flat_vz[:, half_vz:]

    def project(weight, *parts):
        rows = jnp.concatenate(parts, axis=0)
        return jnp.dot(rows, weight, preferred_element_type=F32).astype(BF16)

    low, high, weight = lax.optimization_barrier(
        (below[: ROWS // 2], above[ROWS // 2 :], weight)
    )
    across_up = turn(low, "y", 1, NY)
    across_down = turn(high, "y", -1, NY)
    piece_a = project(weight, normed, beside)
    above_beside = turn(above, "core", 1, NC)
    below_beside = turn(below, "core", 1, NC)
    piece_b = project(weight, above, below, above_beside, below_beside)
    across_up, across_down, piece_b = lax.optimization_barrier((across_up, across_down, piece_b))
    across = jnp.concatenate([across_up, across_down], axis=0)
    across_beside = turn(across, "core", 1, NC)
    piece_c = project(weight, across, across_beside)
    pieces = (piece_a, piece_b, piece_c)
    shared_weights, tied = lax.optimization_barrier((shared_weights, across))
    gathered = lax.all_gather(shared_weights, ("y", "core"), axis=1, tiled=True)

    first_slot = device * 2
    before = jnp.concatenate([jnp.full((1,), -1, jnp.int32), stretch_prompt])
    later = jnp.concatenate([stretch_prompt, jnp.full((1,), -1, jnp.int32)])
    current = lax.dynamic_slice_in_dim(stretch_prompt, first_slot, 2)
    starts = current != lax.dynamic_slice_in_dim(before, first_slot, 2)
    finishes = current != lax.dynamic_slice_in_dim(later, first_slot + 1, 2)
    fill = jnp.where(finishes, lax.dynamic_slice_in_dim(last_fill, first_slot, 2), STRETCH)
    scal = jnp.concatenate(
        [jnp.stack([place_y, place_core]).astype(jnp.int32), starts.astype(jnp.int32), fill]
    )

    last_place = (NY - 1 - place_y) * NC + (NC - 1 - place_core)
    ends = piece_a[ROWS - LEAD : ROWS, :COL_BA]
    for (steps, other), (piece, block) in PLACES.items():
        rows = pieces[piece][(block + 1) * ROWS - LEAD : (block + 1) * ROWS, :COL_BA]
        ends = jnp.where(last_place == steps * NC + other, rows, ends)
    tail = push(ends, ("z", "x"), 1, NZ * NX)

    def gates(*parts):
        rows = jnp.concatenate(parts, axis=0)
        gate = jnp.dot(rows, weight_z, preferred_element_type=F32).astype(BF16)
        return gate.reshape(NY, ROWS, -1)

    gates_beside = gates(beside, above_beside, across_beside, below_beside)
    gates_own = gates(normed, above, tied, below)
    tail, gates_own = lax.optimization_barrier((tail, gates_own))
    taps_qk = conv_qk.astype(F32)
    taps_kv = jnp.concatenate([taps_qk[:, 1, :], conv_value.astype(F32)], axis=1)
    pad = ((HEADS, 128 - 2 * HEADS),)
    decay = jnp.pad(decay_log, pad)[None, :]
    bias = jnp.pad(dt_bias, pad)[None, :]
    xend, xs, vs, khat, logs = state_call(scal, pieces, tail, taps_kv, decay, bias)

    parts = lax.all_to_all(xend, "x", 0, 0, tiled=True)
    parts, gates_beside = lax.optimization_barrier((parts, gates_beside))
    leads, whole, sums = row_call(parts)
    earlier = [push(whole if steps < 4 else sums, "z", steps, NZ) for steps in (1, 2, 3, 4)]
    openings = open_call(earlier, leads)
    opening = lax.all_to_all(openings, "x", 0, 0, tiled=True)

    found = read_call(scal, pieces, tail[:, :COL_K], taps_qk[:, 0, :], xs, vs, khat, logs)

    gain = norm_gain.astype(F32)[None, :]
    given = out_call(1, scal, found, gates_beside, opening, gain, w_out)
    received = turn(given, "core", 1, NC)
    own = out_call(0, scal, found, gates_own, opening, gain, w_out)

    def add(left, right):
        return (left.astype(F32) + right.astype(F32)).astype(BF16)

    summed = add(own, received)
    half = width // 2
    pass_up = turn(summed[2, :, :half], "y", 1, NY)
    pass_down = turn(summed[2, :, half:], "y", -1, NY)
    up = jnp.concatenate([add(summed[1, :, :half], pass_up), summed[1, :, half:]], axis=1)
    down = jnp.concatenate([summed[3, :, :half], add(summed[3, :, half:], pass_down)], axis=1)
    got_up = turn(up, "y", 1, NY)
    got_down = turn(down, "y", -1, NY)
    return expert_call(
        summed[0], got_up, got_down, tokens, ln2_gain, w_sgate, gathered
    )


def solution(mesh):
    fine = Mesh(mesh.devices.reshape(NZ, NX, NY, NC), ("z", "x", "y", "core"))
    rows = P(("z", "x", "y", "core"), None)
    head = ("y", "core")
    return jax.shard_map(
        per_device,
        mesh=fine,
        in_specs=(
            rows,
            P(),
            P(),
            P(),
            P(None, None, head),
            P(None, None, head),
            P(None, None, head),
            P(None, None, head),
            P(None, head),
            P(head),
            P(head),
            P(),
            P(head, None),
            P(),
            P(),
            P(None, head, None),
        ),
        out_specs=(rows, rows),
        check_vma=False,
    )
```

```python
import itertools

import jax
import jax.numpy as jnp
from jax import lax
from jax.experimental import pallas as pl
from jax.experimental.pallas import tpu as pltpu
from jax.sharding import Mesh
from jax.sharding import PartitionSpec as P

F32 = jnp.float32
BF16 = jnp.bfloat16
EPSILON = 1e-06
DK = 128
STRETCH = 512
ROWS = 128
CHUNKS = 8
HEADS = 4
KEYS = 2
NZ, NX, NY, NC = 8, 4, 4, 2
LEAD = 16
COL_K = 256
COL_V = 512
COL_BA = 1024
COL_END = 1152
MIB = 1024 * 1024
PLACES = {
    (0, 0): (0, 0),
    (0, 1): (0, 1),
    (1, 0): (1, 0),
    (3, 0): (1, 1),
    (1, 1): (1, 2),
    (3, 1): (1, 3),
    (2, 0): (2, 0),
    (2, 1): (2, 1),
}


def dot(left, right, contract=((1,), (0,))):
    return lax.dot_general(left, right, (contract, ((), ())), preferred_element_type=F32)


def silu(value):
    return value * (0.5 * jnp.tanh(0.5 * value) + 0.5)


def sigmoid(value):
    return 0.5 * jnp.tanh(0.5 * value) + 0.5


def scaled_rows(inputs, scaling):
    widened = inputs.astype(F32)
    spread = jnp.mean(widened * widened, axis=-1, keepdims=True)
    return widened * lax.rsqrt(spread + EPSILON) * scaling.astype(F32)


def hold(value):
    return pltpu.with_memory_space_constraint(value, pltpu.HBM)


def turn(value, axis, steps, count):
    return lax.ppermute(value, axis, [(i, (i + steps) % count) for i in range(count)])


def push(value, axis, steps, count):
    return lax.ppermute(value, axis, [(i, i + steps) for i in range(count - steps)])


def mixed_rows(ref, chunk, first, last, taps, reset):
    start = chunk * ROWS
    rows = ref[pl.ds(start, ROWS + LEAD), first:last].astype(F32)
    if reset is not False:
        rows = jnp.concatenate([jnp.where(reset, 0.0, rows[:LEAD]), rows[LEAD:]], axis=0)
    total = rows[LEAD:] * taps[3:4]
    for offset in (1, 2, 3):
        total = total + rows[LEAD - offset : LEAD - offset + ROWS] * taps[3 - offset : 4 - offset]
    return silu(total)


def unit_heads(value):
    parts = []
    for head in range(value.shape[1] // DK):
        part = value[:, head * DK : (head + 1) * DK]
        parts.append(part * lax.rsqrt(jnp.sum(part * part, axis=-1, keepdims=True) + EPSILON))
    return parts


def fetch_rows(scal, pieces, scratch, sems, first, last, target):
    copies = []
    for (steps, other), (piece, block) in PLACES.items():
        row = lax.rem(scal[0] + steps, NY)
        core = scal[1] if other == 0 else 1 - scal[1]
        chunk = row * NC + core
        start = pl.multiple_of(chunk * ROWS + LEAD, LEAD)
        copy = pltpu.make_async_copy(
            pieces[piece].at[pl.ds(block * ROWS, ROWS), pl.ds(first, last - first)],
            scratch.at[pl.ds(start, ROWS), pl.ds(target, last - first)],
            sems.at[len(copies)],
        )
        copy.start()
        copies.append(copy)
    for copy in copies:
        copy.wait()


def is_reset(scal, chunk):
    if isinstance(chunk, int):
        return scal[2 + chunk * 2 // CHUNKS] > 0 if chunk % (CHUNKS // 2) == 0 else False
    first = jnp.logical_and(chunk == 0, scal[2] > 0)
    second = jnp.logical_and(chunk == CHUNKS // 2, scal[3] > 0)
    return jnp.logical_or(first, second)


def iota2(axis):
    return lax.broadcasted_iota(jnp.int32, (ROWS, ROWS), axis)


def odd_blocks(value, span):
    return jnp.concatenate([value[at : at + span] for at in range(span, ROWS, 2 * span)], axis=0)


def with_even(even, odd, span):
    parts = []
    for place, at in enumerate(range(0, ROWS, 2 * span)):
        block = odd[place * span : (place + 1) * span]
        parts.append(jnp.zeros_like(block) if even is None else even[at : at + span])
        parts.append(block)
    return jnp.concatenate(parts, axis=0)


def inverse_rests(stricts, level):
    rests = [jnp.where(level == 1, -strict, 0.0) for strict in stricts]
    for step in (2, 3):
        lows = [rest.astype(BF16) for rest in rests]
        belows = [jnp.where(level == step, strict, 0.0) for strict in stricts]
        halves = [below + dot(below.astype(BF16), low) for below, low in zip(belows, lows)]
        yield
        rests = [rest - half - dot(low, half.astype(BF16)) for rest, half, low in zip(rests, halves, lows)]
        yield
    for step in (4, 5, 6, 7):
        span = 1 << (step - 1)
        here = odd_blocks(level, span) == step
        lows = [rest.astype(BF16) for rest in rests]
        odds = [odd_blocks(rest, span) for rest in rests]
        belows = [jnp.where(here, odd_blocks(strict, span), 0.0) for strict in stricts]
        halves = [below + dot(below.astype(BF16), low) for below, low in zip(belows, lows)]
        yield
        wides = [with_even(None, half, span).astype(BF16) for half in halves]
        odds = [odd - half - dot(odd.astype(BF16), wide) for odd, half, wide in zip(odds, halves, wides)]
        rests = [with_even(rest, odd, span) for rest, odd in zip(rests, odds)]
        yield
    return rests


def block_levels():
    row, col = iota2(0), iota2(1)
    apart = jnp.where(row > col, jnp.bitwise_xor(row, col), 0)
    level = jnp.zeros((ROWS, ROWS), jnp.int32)
    for step in range(7):
        level = level + (apart >= (1 << step)).astype(jnp.int32)
    return level


def state_kernel(
    scal, piece_a, piece_b, piece_c, tail, taps, decay, bias,
    xend, xs_out, vs_out, khat_out, logs_out,
    raw, rest, kturn, values, betas, state, xs, vs, khat, logs, sems, out_sems,
):
    raw[0:LEAD, 0:COL_BA] = tail[...]
    fetch_rows(scal, (piece_a, piece_b, piece_c), raw, sems, COL_K, COL_END, COL_K)
    row, col = iota2(0), iota2(1)
    strict = row > col
    summing = (row >= col).astype(F32)
    level = block_levels()

    def prepare(chunk):
        reset = is_reset(scal, chunk)
        mixed = mixed_rows(raw, chunk, COL_K, COL_BA, taps, reset)
        start = chunk * ROWS + LEAD
        ba = raw[pl.ds(start, ROWS), COL_BA:COL_END].astype(F32)
        beta = sigmoid(ba)
        inner = ba + bias[...]
        soft = jnp.maximum(inner, 0.0) + jnp.log1p(jnp.exp(-jnp.abs(inner)))
        rate = -jnp.exp(decay[...]) * soft
        log = lax.dot_general(
            summing, rate, (((1,), (0,)), ((), ())),
            precision=lax.Precision.HIGHEST, preferred_element_type=F32,
        )
        log_turned = log.T
        betas[chunk] = beta
        logs[chunk] = log
        unit = unit_heads(mixed[:, : KEYS * DK])
        lowers = []
        for key in range(KEYS):
            key_rows = unit[key].astype(BF16)
            khat[chunk, key] = key_rows
            kturn[chunk, key] = unit[key].T.astype(BF16)
            products = dot(key_rows, key_rows, ((1,), (1,)))
            for half in range(2):
                head = 2 * key + half
                beta_col = beta[:, head : head + 1]
                spread = log[:, HEADS + head : HEADS + head + 1] - log_turned[HEADS + head : HEADS + head + 1, :]
                weight = jnp.exp(jnp.minimum(spread, 0.0))
                lower = jnp.where(strict, products * beta_col * weight, 0.0)
                lowers.append(lower)
                value = mixed[:, (KEYS + head) * DK : (KEYS + head + 1) * DK]
                values[chunk, head] = value * beta_col
        return lowers

    def prepare_all(chunks):
        lowers = []
        for chunk in chunks:
            lowers += prepare(chunk)
            yield
        found = yield from inverse_rests(lowers, level)
        for place, value in enumerate(found):
            rest[chunks[place // HEADS], place % HEADS] = value.astype(BF16)

    opening = jnp.where(scal[2] > 0, 0.0, 1.0)
    identity = jnp.where(row == col, opening, 0.0)
    for key in range(KEYS):
        for half in range(2):
            state[key, :, 2 * half * DK : (2 * half + 1) * DK] = jnp.zeros((DK, DK), F32)
            state[key, :, (2 * half + 1) * DK : (2 * half + 2) * DK] = identity

    def advance(chunk):
        beta = betas[chunk]
        log = logs[chunk]
        growth = jnp.exp(log)
        last = log[ROWS - 1 : ROWS, :]
        shrink = jnp.exp(last - log)
        whole = jnp.exp(last)
        held = [state[key] for key in range(KEYS)]
        if chunk == CHUNKS // 2:
            held = [jnp.where(scal[3] > 0, 0.0, value) for value in held]
        lows = [value.astype(BF16) for value in held]
        for key in range(KEYS):
            xs[chunk, key] = lows[key]
        seen = [dot(khat[chunk, key], lows[key]) for key in range(KEYS)]
        yield
        wanted = []
        for head in range(HEADS):
            at = HEADS + head
            half = head % 2
            factor = beta[:, head : head + 1] * growth[:, at : at + 1]
            part = seen[head // 2][:, 2 * half * DK : (2 * half + 2) * DK] * factor
            wanted.append(jnp.concatenate([values[chunk, head] - part[:, :DK], -part[:, DK:]], axis=1))
        solved = [
            value + dot(rest[chunk, head], value.astype(BF16)) for head, value in enumerate(wanted)
        ]
        yield
        updates = []
        scales = []
        for head in range(HEADS):
            at = HEADS + head
            vs[chunk, head] = solved[head].astype(BF16)
            updates.append((solved[head] * shrink[:, at : at + 1]).astype(BF16))
            scales.append(jnp.broadcast_to(whole[:, at : at + 1], (1, 2 * DK)))
        for key in range(KEYS):
            scale = jnp.concatenate(scales[2 * key : 2 * key + 2], axis=1)
            update = jnp.concatenate(updates[2 * key : 2 * key + 2], axis=1)
            state[key] = held[key] * scale + dot(kturn[chunk, key], update)
        for copy in copies_out(chunk):
            copy.start()
        yield

    def advance_all(chunks):
        for chunk in chunks:
            yield from advance(chunk)

    def copies_out(chunk):
        return [
            pltpu.make_async_copy(held.at[chunk], target.at[chunk], out_sems.at[place, chunk])
            for place, (held, target) in enumerate(((xs, xs_out), (vs, vs_out), (khat, khat_out), (logs, logs_out)))
        ]

    early, late = list(range(CHUNKS // 2)), list(range(CHUNKS // 2, CHUNKS))
    for unused in prepare_all(early):
        pass
    for unused in itertools.zip_longest(prepare_all(late), advance_all(early)):
        pass
    for unused in advance_all(late):
        pass
    for key in range(KEYS):
        for half in range(2):
            xend[2 * key + half] = state[key, :, 2 * half * DK : (2 * half + 2) * DK].astype(BF16)
    for chunk in range(CHUNKS):
        for copy in copies_out(chunk):
            copy.wait()


def state_call(scal, pieces, tail, taps, decay, bias):
    vmem = pl.BlockSpec(memory_space=pltpu.VMEM)
    hbm = pl.BlockSpec(memory_space=pltpu.HBM)
    return pl.pallas_call(
        state_kernel,
        out_shape=(
            jax.ShapeDtypeStruct((HEADS, DK, 2 * DK), BF16),
            pltpu.HBM((CHUNKS, KEYS, DK, 4 * DK), BF16),
            pltpu.HBM((CHUNKS, HEADS, ROWS, 2 * DK), BF16),
            pltpu.HBM((CHUNKS, KEYS, ROWS, DK), BF16),
            pltpu.HBM((CHUNKS, ROWS, 128), F32),
        ),
        in_specs=[pl.BlockSpec(memory_space=pltpu.SMEM), hbm, hbm, hbm] + [vmem] * 4,
        out_specs=[vmem] + [hbm] * 4,
        scratch_shapes=[
            pltpu.VMEM((LEAD + CHUNKS * ROWS, COL_END), BF16),
            pltpu.VMEM((CHUNKS, HEADS, ROWS, ROWS), BF16),
            pltpu.VMEM((CHUNKS, KEYS, DK, ROWS), BF16),
            pltpu.VMEM((CHUNKS, HEADS, ROWS, DK), F32),
            pltpu.VMEM((CHUNKS, ROWS, 128), F32),
            pltpu.VMEM((KEYS, DK, 4 * DK), F32),
            pltpu.VMEM((CHUNKS, KEYS, DK, 4 * DK), BF16),
            pltpu.VMEM((CHUNKS, HEADS, ROWS, 2 * DK), BF16),
            pltpu.VMEM((CHUNKS, KEYS, ROWS, DK), BF16),
            pltpu.VMEM((CHUNKS, ROWS, 128), F32),
            pltpu.SemaphoreType.DMA((CHUNKS,)),
            pltpu.SemaphoreType.DMA((4, CHUNKS)),
        ],
        compiler_params=pltpu.CompilerParams(vmem_limit_bytes=40 * MIB),
        cost_estimate=pl.CostEstimate(flops=6_000_000_000, bytes_accessed=20_000_000, transcendentals=0),
        name="state",
    )(scal, *map(hold, pieces), tail, taps, decay, bias)


def read_kernel(
    scal, piece_a, piece_b, piece_c, tail, taps, xs, vs, khat, logs, out, raw, sems
):
    step = pl.program_id(0)

    @pl.when(step == 0)
    def _():
        raw[0:LEAD, :] = tail[...]
        fetch_rows(scal, (piece_a, piece_b, piece_c), raw, sems, 0, COL_K, 0)

    inclusive = iota2(0) >= iota2(1)
    queries, weights, growths = [], [], []
    for core in range(NC):
        chunk = NC * step + core
        start = pl.multiple_of(chunk * ROWS, ROWS)
        reset = is_reset(scal, chunk) if core == 0 else False
        mixed = mixed_rows(raw.at[pl.ds(start, ROWS + LEAD)], 0, 0, COL_K, taps, reset)
        queries += [(value * DK ** (-0.5)).astype(BF16) for value in unit_heads(mixed)]
        log = logs[core]
        log_turned = log.T
        growth = jnp.exp(log)
        for head in range(HEADS):
            at = HEADS + head
            growths.append(growth[:, at : at + 1])
            spread = log[:, at : at + 1] - log_turned[at : at + 1, :]
            weights.append(jnp.where(inclusive, jnp.exp(jnp.minimum(spread, 0.0)), 0.0))
    pairs = [(core, key) for core in range(NC) for key in range(KEYS)]
    products = [dot(queries[i], khat[core, key], ((1,), (1,))) for i, (core, key) in enumerate(pairs)]
    seen = [dot(queries[i], xs[core, key]) for i, (core, key) in enumerate(pairs)]
    for core in range(NC):
        other = jnp.bitwise_xor(core, scal[1])
        for head in range(HEADS):
            pair = core * KEYS + head // 2
            half = head % 2
            scores = (products[pair] * weights[core * HEADS + head]).astype(BF16)
            found = seen[pair][:, 2 * half * DK : (2 * half + 2) * DK] * growths[core * HEADS + head]
            out[other, head] = (found + dot(scores, vs[core, head])).astype(BF16)


def read_call(scal, pieces, tail, taps, xs, vs, khat, logs):
    hbm = pl.BlockSpec(memory_space=pltpu.HBM)
    return pl.pallas_call(
        read_kernel,
        out_shape=pltpu.HBM((NC, NY, HEADS, ROWS, 2 * DK), BF16),
        grid_spec=pltpu.PrefetchScalarGridSpec(
            num_scalar_prefetch=1,
            grid=(CHUNKS // NC,),
            in_specs=[
                hbm,
                hbm,
                hbm,
                pl.BlockSpec((LEAD, COL_K), lambda c, scal: (0, 0)),
                pl.BlockSpec((4, COL_K), lambda c, scal: (0, 0)),
                pl.BlockSpec((NC, KEYS, DK, 4 * DK), lambda c, scal: (c, 0, 0, 0)),
                pl.BlockSpec((NC, HEADS, ROWS, 2 * DK), lambda c, scal: (c, 0, 0, 0)),
                pl.BlockSpec((NC, KEYS, ROWS, DK), lambda c, scal: (c, 0, 0, 0)),
                pl.BlockSpec((NC, ROWS, 128), lambda c, scal: (c, 0, 0)),
            ],
            out_specs=pl.BlockSpec(
                (NC, None, HEADS, ROWS, 2 * DK),
                lambda c, scal: (0, lax.rem(c - scal[0] + NY, NY), 0, 0, 0),
            ),
            scratch_shapes=[
                pltpu.VMEM((LEAD + CHUNKS * ROWS, COL_K), BF16),
                pltpu.SemaphoreType.DMA((CHUNKS,)),
            ],
        ),
        compiler_params=pltpu.CompilerParams(vmem_limit_bytes=32 * MIB),
        cost_estimate=pl.CostEstimate(flops=3_000_000_000, bytes_accessed=10_000_000, transcendentals=0),
        name="read",
    )(scal, *map(hold, pieces), tail, taps, hold(xs), hold(vs), hold(khat), hold(logs))


def norm_kernel(tokens, gain, out):
    out[...] = scaled_rows(tokens[...], gain[...][None, :]).astype(BF16)


def norm_call(tokens, gain):
    vmem = pl.BlockSpec(memory_space=pltpu.VMEM)
    return pl.pallas_call(
        norm_kernel,
        out_shape=jax.ShapeDtypeStruct(tokens.shape, BF16),
        in_specs=[vmem, vmem],
        out_specs=vmem,
        cost_estimate=pl.CostEstimate(flops=1_000_000, bytes_accessed=1_000_000, transcendentals=0),
        name="norm",
    )(tokens, gain)


def after(late, early):
    moved = dot(late[:, DK:], early)
    if early.shape[1] == DK:
        return moved + late[:, :DK].astype(F32)
    return jnp.concatenate([moved[:, :DK] + late[:, :DK].astype(F32), moved[:, DK:]], axis=1)


def row_kernel(parts, leads, whole, sums):
    held = parts[0]
    leads[0] = held
    for place in range(1, NX):
        held = after(parts[place], held).astype(BF16)
        if place < NX - 1:
            leads[place] = held
    whole[...] = held
    sums[...] = held[:, :DK]


def row_call(parts):
    vmem = pl.BlockSpec(memory_space=pltpu.VMEM)
    return pl.pallas_call(
        row_kernel,
        out_shape=(
            jax.ShapeDtypeStruct((NX - 1, DK, 2 * DK), BF16),
            jax.ShapeDtypeStruct((DK, 2 * DK), BF16),
            jax.ShapeDtypeStruct((DK, DK), BF16),
        ),
        in_specs=[vmem],
        out_specs=[vmem] * 3,
        cost_estimate=pl.CostEstimate(flops=100_000_000, bytes_accessed=1_000_000, transcendentals=0),
        name="rows",
    )(parts)


def open_kernel(one, two, three, four, leads, out):
    opening = four[...]
    for earlier in (three, two, one):
        opening = after(earlier[...], opening).astype(BF16)
    out[0] = opening
    for place in range(1, NX):
        out[place] = after(leads[place - 1], opening).astype(BF16)


def open_call(earlier, leads):
    vmem = pl.BlockSpec(memory_space=pltpu.VMEM)
    return pl.pallas_call(
        open_kernel,
        out_shape=jax.ShapeDtypeStruct((NX, DK, DK), BF16),
        in_specs=[vmem] * 5,
        out_specs=vmem,
        cost_estimate=pl.CostEstimate(flops=100_000_000, bytes_accessed=1_000_000, transcendentals=0),
        name="open",
    )(*earlier, leads)


def out_kernel(other, scal, found, gates, opening, gain, w_out, out):
    rows = []
    moved = [
        [dot(found[block, head][:, DK:], opening[head]) for head in range(HEADS)]
        for block in range(2)
    ]
    for block in range(2):
        steps = 2 * pl.program_id(0) + block
        core = scal[1] if other == 0 else 1 - scal[1]
        chunk = lax.rem(scal[0] + steps, NY) * NC + core
        first = lax.rem(chunk, STRETCH // ROWS) * ROWS
        fill = jnp.where(chunk < CHUNKS // 2, scal[4], scal[5])
        within = lax.broadcasted_iota(jnp.int32, (ROWS, 1), 0) + first
        kept = within < fill
        parts = []
        for head in range(HEADS):
            value = found[block, head][:, :DK].astype(F32) + moved[block][head]
            value = jnp.where(kept, value, 0.0)
            gate = gates[block, :, head * DK : (head + 1) * DK].astype(F32)
            spread = jnp.mean(value * value, axis=-1, keepdims=True)
            parts.append((value * lax.rsqrt(spread + EPSILON) * gain[...] * silu(gate)).astype(BF16))
        rows.append(jnp.concatenate(parts, axis=1))
    total = dot(jnp.concatenate(rows, axis=0), w_out[...]).astype(BF16)
    out[...] = total.reshape(out.shape)


def out_call(other, scal, found, gates, opening, gain, w_out):
    width = w_out.shape[1]
    return pl.pallas_call(
        lambda *refs: out_kernel(other, *refs),
        grid=(NY // 2,),
        out_shape=jax.ShapeDtypeStruct((NY, ROWS, width), BF16),
        in_specs=[
            pl.BlockSpec(memory_space=pltpu.SMEM),
            pl.BlockSpec((None, 2, HEADS, ROWS, 2 * DK), lambda i: (other, i, 0, 0, 0)),
            pl.BlockSpec((2, ROWS, HEADS * DK), lambda i: (i, 0, 0)),
            pl.BlockSpec((HEADS, DK, DK), lambda i: (0, 0, 0)),
            pl.BlockSpec((1, DK), lambda i: (0, 0)),
            pl.BlockSpec((HEADS * DK, width), lambda i: (0, 0)),
        ],
        out_specs=pl.BlockSpec((2, ROWS, width), lambda i: (i, 0, 0)),
        compiler_params=pltpu.CompilerParams(vmem_limit_bytes=32 * MIB),
        cost_estimate=pl.CostEstimate(flops=1_200_000_000, bytes_accessed=6_000_000, transcendentals=0),
        name="out",
    )(scal, hold(found), hold(gates), opening, gain, hold(w_out))


def sum_kernel(own, received, rows, pass_up, pass_down, free_up, free_down, more_up, more_down):
    half = own.shape[2] // 2
    total = own[2].astype(F32) + received[2].astype(F32)
    pass_up[...] = total[:, :half].astype(BF16)
    pass_down[...] = total[:, half:].astype(BF16)
    total = own[1].astype(F32) + received[1].astype(F32)
    more_up[...] = total[:, :half].astype(BF16)
    free_up[...] = total[:, half:].astype(BF16)
    total = own[3].astype(F32) + received[3].astype(F32)
    free_down[...] = total[:, :half].astype(BF16)
    more_down[...] = total[:, half:].astype(BF16)
    rows[...] = (own[0].astype(F32) + received[0].astype(F32)).astype(BF16)


def sum_call(own, received):
    vmem = pl.BlockSpec(memory_space=pltpu.VMEM)
    width = own.shape[2]
    half = jax.ShapeDtypeStruct((ROWS, width // 2), BF16)
    return pl.pallas_call(
        sum_kernel,
        out_shape=(jax.ShapeDtypeStruct((ROWS, width), BF16),) + (half,) * 6,
        in_specs=[vmem] * 2,
        out_specs=[vmem] * 7,
        compiler_params=pltpu.CompilerParams(vmem_limit_bytes=16 * MIB),
        cost_estimate=pl.CostEstimate(flops=1_000_000, bytes_accessed=6_000_000, transcendentals=0),
        name="sum",
    )(own, received)


def expert_kernel(
    rows, more_up, free_up, free_down, more_down, tokens, gain, w_sgate, shared,
    attention, layer, weights, sems,
):
    copies = [pltpu.make_async_copy(shared.at[i], weights.at[i], sems.at[i]) for i in range(3)]
    for copy in copies:
        copy.start()
    ups = jnp.concatenate([more_up[...], free_up[...]], axis=1)
    downs = jnp.concatenate([free_down[...], more_down[...]], axis=1)
    total = rows[...].astype(F32) + ups.astype(F32) + downs.astype(F32)
    total = total.astype(BF16)
    attention[...] = total
    residual = (tokens[...].astype(F32) + total.astype(F32)).astype(BF16)
    normed = scaled_rows(residual, gain[...][None, :]).astype(BF16)
    weighed = normed.astype(F32) * w_sgate[...][None, :].astype(F32)
    gate = sigmoid(jnp.sum(weighed, axis=-1, keepdims=True))
    copies[0].wait()
    gate_part = dot(normed, weights[0], ((1,), (1,)))
    copies[1].wait()
    up_part = dot(normed, weights[1], ((1,), (1,)))
    hidden = (silu(gate_part) * up_part).astype(BF16)
    copies[2].wait()
    layer[...] = (residual.astype(F32) + gate * dot(hidden, weights[2])).astype(BF16)


def expert_call(rows, more_up, free_up, free_down, more_down, tokens, gain, w_sgate, shared):
    vmem = pl.BlockSpec(memory_space=pltpu.VMEM)
    return pl.pallas_call(
        expert_kernel,
        out_shape=(jax.ShapeDtypeStruct(tokens.shape, BF16),) * 2,
        in_specs=[vmem] * 8 + [pl.BlockSpec(memory_space=pltpu.HBM)],
        out_specs=[vmem] * 2,
        scratch_shapes=[pltpu.VMEM(shared.shape, BF16), pltpu.SemaphoreType.DMA((3,))],
        compiler_params=pltpu.CompilerParams(vmem_limit_bytes=32 * MIB),
        cost_estimate=pl.CostEstimate(flops=800_000_000, bytes_accessed=9_000_000, transcendentals=0),
        name="expert",
    )(rows, more_up, free_up, free_down, more_down, tokens, gain, w_sgate, hold(shared))


def per_device(
    tokens,
    stretch_prompt,
    last_fill,
    ln1_gain,
    w_qk,
    w_vz,
    w_ba,
    conv_qk,
    conv_value,
    decay_log,
    dt_bias,
    norm_gain,
    w_out,
    ln2_gain,
    w_sgate,
    shared_weights,
):
    width = tokens.shape[1]
    place_y = lax.axis_index("y")
    place_core = lax.axis_index("core")
    device = lax.axis_index("z") * NX + lax.axis_index("x")
    normed = norm_call(tokens, ln1_gain)

    below = turn(normed, "y", 1, NY)
    above = turn(normed, "y", -1, NY)
    beside = turn(normed, "core", 1, NC)
    flat_vz = w_vz.reshape(width, -1)
    half_vz = flat_vz.shape[1] // 2
    weight = jnp.concatenate(
        [
            w_qk.reshape(width, -1),
            flat_vz[:, :half_vz],
            jnp.pad(w_ba.reshape(width, -1), ((0, 0), (0, 128 - 2 * HEADS))),
        ],
        axis=1,
    )
    weight_z = flat_vz[:, half_vz:]

    def project(weight, *parts):
        rows = jnp.concatenate(parts, axis=0)
        return jnp.dot(rows, weight, preferred_element_type=F32).astype(BF16)

    piece_a = project(weight, normed, beside)
    below, above, piece_a = lax.optimization_barrier((below, above, piece_a))
    across_up = turn(below[: ROWS // 2], "y", 1, NY)
    across_down = turn(above[ROWS // 2 :], "y", -1, NY)
    above_beside = turn(above, "core", 1, NC)
    below_beside = turn(below, "core", 1, NC)
    above, below, above_beside, below_beside = lax.optimization_barrier(
        (above, below, above_beside, below_beside)
    )
    piece_b = project(weight, above, below, above_beside, below_beside)
    across_up, across_down, piece_b = lax.optimization_barrier((across_up, across_down, piece_b))
    across = jnp.concatenate([across_up, across_down], axis=0)
    across_beside = turn(across, "core", 1, NC)
    piece_c = project(weight, across, across_beside)
    shared_weights, piece_c = lax.optimization_barrier((shared_weights, piece_c))
    pieces = (piece_a, piece_b, piece_c)
    gathered = lax.all_gather(shared_weights, ("y", "core"), axis=1, tiled=True)

    first_slot = device * 2
    before = jnp.concatenate([jnp.full((1,), -1, jnp.int32), stretch_prompt])
    later = jnp.concatenate([stretch_prompt, jnp.full((1,), -1, jnp.int32)])
    current = lax.dynamic_slice_in_dim(stretch_prompt, first_slot, 2)
    starts = current != lax.dynamic_slice_in_dim(before, first_slot, 2)
    finishes = current != lax.dynamic_slice_in_dim(later, first_slot + 1, 2)
    fill = jnp.where(finishes, lax.dynamic_slice_in_dim(last_fill, first_slot, 2), STRETCH)
    scal = jnp.concatenate(
        [jnp.stack([place_y, place_core]).astype(jnp.int32), starts.astype(jnp.int32), fill]
    )

    last_place = (NY - 1 - place_y) * NC + (NC - 1 - place_core)
    ends = piece_a[ROWS - LEAD : ROWS, :COL_BA]
    for (steps, other), (piece, block) in PLACES.items():
        rows = pieces[piece][(block + 1) * ROWS - LEAD : (block + 1) * ROWS, :COL_BA]
        ends = jnp.where(last_place == steps * NC + other, rows, ends)
    tail = push(ends, ("z", "x"), 1, NZ * NX)

    def gates(*parts):
        rows = jnp.concatenate(parts, axis=0)
        gate = jnp.dot(rows, weight_z, preferred_element_type=F32).astype(BF16)
        return gate.reshape(NY, ROWS, -1)

    gates_beside = gates(beside, above_beside, across_beside, below_beside)
    gates_own = gates(normed, above, across, below)
    tail, gates_own = lax.optimization_barrier((tail, gates_own))
    taps_qk = conv_qk.astype(F32)
    taps_kv = jnp.concatenate([taps_qk[:, 1, :], conv_value.astype(F32)], axis=1)
    pad = ((HEADS, 128 - 2 * HEADS),)
    decay = jnp.pad(decay_log, pad)[None, :]
    bias = jnp.pad(dt_bias, pad)[None, :]
    xend, xs, vs, khat, logs = state_call(scal, pieces, tail, taps_kv, decay, bias)

    parts = lax.all_to_all(xend, "x", 0, 0, tiled=True)
    given = (tail[:, :COL_K], taps_qk[:, 0, :], xs, vs, khat, logs)
    parts, gates_beside = lax.optimization_barrier((parts, gates_beside))
    leads, whole, sums = row_call(parts)
    earlier = [push(whole if steps < 4 else sums, "z", steps, NZ) for steps in (1, 2, 3, 4)]
    openings = open_call(earlier, leads)
    opening = lax.all_to_all(openings, "x", 0, 0, tiled=True)

    found = read_call(scal, pieces, *given)

    gain = norm_gain.astype(F32)[None, :]
    lent = out_call(1, scal, found, gates_beside, opening, gain, w_out)
    received = turn(lent, "core", 1, NC)
    own = out_call(0, scal, found, gates_own, opening, gain, w_out)

    own_rows, pass_up, pass_down, free_up, free_down, more_up, more_down = sum_call(own, received)
    pass_up = turn(pass_up, "y", 1, NY)
    pass_down = turn(pass_down, "y", -1, NY)
    free_up = turn(free_up, "y", 1, NY)
    free_down = turn(free_down, "y", -1, NY)
    more_up = turn((more_up.astype(F32) + pass_up.astype(F32)).astype(BF16), "y", 1, NY)
    more_down = turn((more_down.astype(F32) + pass_down.astype(F32)).astype(BF16), "y", -1, NY)
    return expert_call(
        own_rows, more_up, free_up, free_down, more_down, tokens, ln2_gain, w_sgate, gathered
    )


def solution(mesh):
    fine = Mesh(mesh.devices.reshape(NZ, NX, NY, NC), ("z", "x", "y", "core"))
    rows = P(("z", "x", "y", "core"), None)
    head = ("y", "core")
    return jax.shard_map(
        per_device,
        mesh=fine,
        in_specs=(
            rows,
            P(),
            P(),
            P(),
            P(None, None, head),
            P(None, None, head),
            P(None, None, head),
            P(None, None, head),
            P(None, head),
            P(head),
            P(head),
            P(),
            P(head, None),
            P(),
            P(),
            P(None, head, None),
        ),
        out_specs=(rows, rows),
        check_vma=False,
    )
```

```python
import itertools

import jax
import jax.numpy as jnp
from jax import lax
from jax.experimental import pallas as pl
from jax.experimental.pallas import tpu as pltpu
from jax.sharding import Mesh
from jax.sharding import PartitionSpec as P

F32 = jnp.float32
BF16 = jnp.bfloat16
EPSILON = 1e-06
DK = 128
STRETCH = 512
ROWS = 128
CHUNKS = 8
HEADS = 4
KEYS = 2
NZ, NX, NY, NC = 8, 4, 4, 2
LEAD = 16
COL_K = 256
COL_V = 512
COL_BA = 1024
COL_END = 1152
MIB = 1024 * 1024
PLACES = {
    (0, 0): (0, 0),
    (0, 1): (0, 1),
    (1, 0): (1, 0),
    (3, 0): (1, 1),
    (1, 1): (1, 2),
    (3, 1): (1, 3),
    (2, 0): (2, 0),
    (2, 1): (2, 1),
}


def dot(left, right, contract=((1,), (0,))):
    return lax.dot_general(left, right, (contract, ((), ())), preferred_element_type=F32)


def silu(value):
    return value * (0.5 * jnp.tanh(0.5 * value) + 0.5)


def sigmoid(value):
    return 0.5 * jnp.tanh(0.5 * value) + 0.5


def scaled_rows(inputs, scaling):
    widened = inputs.astype(F32)
    spread = jnp.mean(widened * widened, axis=-1, keepdims=True)
    return widened * lax.rsqrt(spread + EPSILON) * scaling.astype(F32)


def hold(value):
    return pltpu.with_memory_space_constraint(value, pltpu.HBM)


def turn(value, axis, steps, count):
    return lax.ppermute(value, axis, [(i, (i + steps) % count) for i in range(count)])


def push(value, axis, steps, count):
    return lax.ppermute(value, axis, [(i, i + steps) for i in range(count - steps)])


def mixed_rows(ref, chunk, first, last, taps, reset):
    start = chunk * ROWS
    rows = ref[pl.ds(start, ROWS + LEAD), first:last].astype(F32)
    if reset is not False:
        rows = jnp.concatenate([jnp.where(reset, 0.0, rows[:LEAD]), rows[LEAD:]], axis=0)
    total = rows[LEAD:] * taps[3:4]
    for offset in (1, 2, 3):
        total = total + rows[LEAD - offset : LEAD - offset + ROWS] * taps[3 - offset : 4 - offset]
    return silu(total)


def unit_heads(value):
    parts = []
    for head in range(value.shape[1] // DK):
        part = value[:, head * DK : (head + 1) * DK]
        parts.append(part * lax.rsqrt(jnp.sum(part * part, axis=-1, keepdims=True) + EPSILON))
    return parts


def fetch_rows(scal, pieces, scratch, sems, first, last, target):
    copies = []
    for (steps, other), (piece, block) in PLACES.items():
        row = lax.rem(scal[0] + steps, NY)
        core = scal[1] if other == 0 else 1 - scal[1]
        chunk = row * NC + core
        start = pl.multiple_of(chunk * ROWS + LEAD, LEAD)
        copy = pltpu.make_async_copy(
            pieces[piece].at[pl.ds(block * ROWS, ROWS), pl.ds(first, last - first)],
            scratch.at[pl.ds(start, ROWS), pl.ds(target, last - first)],
            sems.at[len(copies)],
        )
        copy.start()
        copies.append(copy)
    for copy in copies:
        copy.wait()


def is_reset(scal, chunk):
    if isinstance(chunk, int):
        return scal[2 + chunk * 2 // CHUNKS] > 0 if chunk % (CHUNKS // 2) == 0 else False
    first = jnp.logical_and(chunk == 0, scal[2] > 0)
    second = jnp.logical_and(chunk == CHUNKS // 2, scal[3] > 0)
    return jnp.logical_or(first, second)


def iota2(axis):
    return lax.broadcasted_iota(jnp.int32, (ROWS, ROWS), axis)


def odd_blocks(value, span):
    return jnp.concatenate([value[at : at + span] for at in range(span, ROWS, 2 * span)], axis=0)


def with_even(even, odd, span):
    parts = []
    for place, at in enumerate(range(0, ROWS, 2 * span)):
        block = odd[place * span : (place + 1) * span]
        parts.append(jnp.zeros_like(block) if even is None else even[at : at + span])
        parts.append(block)
    return jnp.concatenate(parts, axis=0)


def inverse_rests(stricts, level):
    rests = [jnp.where(level == 1, -strict, 0.0) for strict in stricts]
    for step in (2, 3):
        lows = [rest.astype(BF16) for rest in rests]
        belows = [jnp.where(level == step, strict, 0.0) for strict in stricts]
        halves = [below + dot(below.astype(BF16), low) for below, low in zip(belows, lows)]
        yield
        rests = [rest - half - dot(low, half.astype(BF16)) for rest, half, low in zip(rests, halves, lows)]
        yield
    for step in (4, 5, 6, 7):
        span = 1 << (step - 1)
        here = odd_blocks(level, span) == step
        lows = [rest.astype(BF16) for rest in rests]
        odds = [odd_blocks(rest, span) for rest in rests]
        belows = [jnp.where(here, odd_blocks(strict, span), 0.0) for strict in stricts]
        halves = [below + dot(below.astype(BF16), low) for below, low in zip(belows, lows)]
        yield
        wides = [with_even(None, half, span).astype(BF16) for half in halves]
        odds = [odd - half - dot(odd.astype(BF16), wide) for odd, half, wide in zip(odds, halves, wides)]
        rests = [with_even(rest, odd, span) for rest, odd in zip(rests, odds)]
        yield
    return rests


def block_levels():
    row, col = iota2(0), iota2(1)
    apart = jnp.where(row > col, jnp.bitwise_xor(row, col), 0)
    level = jnp.zeros((ROWS, ROWS), jnp.int32)
    for step in range(7):
        level = level + (apart >= (1 << step)).astype(jnp.int32)
    return level


def state_kernel(
    scal, piece_a, piece_b, piece_c, tail, taps, decay, bias,
    xend, xs_out, vs_out, khat_out, logs_out,
    raw, rest, kturn, values, betas, state, xs, vs, khat, logs, sems, out_sems,
):
    raw[0:LEAD, 0:COL_BA] = tail[...]
    fetch_rows(scal, (piece_a, piece_b, piece_c), raw, sems, COL_K, COL_END, COL_K)
    row, col = iota2(0), iota2(1)
    strict = row > col
    summing = (row >= col).astype(F32)
    level = block_levels()

    def prepare(chunk):
        reset = is_reset(scal, chunk)
        mixed = mixed_rows(raw, chunk, COL_K, COL_BA, taps, reset)
        start = chunk * ROWS + LEAD
        ba = raw[pl.ds(start, ROWS), COL_BA:COL_END].astype(F32)
        beta = sigmoid(ba)
        inner = ba + bias[...]
        soft = jnp.maximum(inner, 0.0) + jnp.log1p(jnp.exp(-jnp.abs(inner)))
        rate = -jnp.exp(decay[...]) * soft
        log = lax.dot_general(
            summing, rate, (((1,), (0,)), ((), ())),
            precision=lax.Precision.HIGHEST, preferred_element_type=F32,
        )
        log_turned = log.T
        betas[chunk] = beta
        logs[chunk] = log
        unit = unit_heads(mixed[:, : KEYS * DK])
        lowers = []
        for key in range(KEYS):
            key_rows = unit[key].astype(BF16)
            khat[chunk, key] = key_rows
            kturn[chunk, key] = unit[key].T.astype(BF16)
            products = dot(key_rows, key_rows, ((1,), (1,)))
            for half in range(2):
                head = 2 * key + half
                beta_col = beta[:, head : head + 1]
                spread = log[:, HEADS + head : HEADS + head + 1] - log_turned[HEADS + head : HEADS + head + 1, :]
                weight = jnp.exp(jnp.minimum(spread, 0.0))
                lower = jnp.where(strict, products * beta_col * weight, 0.0)
                lowers.append(lower)
                value = mixed[:, (KEYS + head) * DK : (KEYS + head + 1) * DK]
                values[chunk, head] = value * beta_col
        return lowers

    def prepare_all(chunks):
        lowers = []
        for chunk in chunks:
            lowers += prepare(chunk)
            yield
        found = yield from inverse_rests(lowers, level)
        for place, value in enumerate(found):
            rest[chunks[place // HEADS], place % HEADS] = value.astype(BF16)

    opening = jnp.where(scal[2] > 0, 0.0, 1.0)
    identity = jnp.where(row == col, opening, 0.0)
    for key in range(KEYS):
        for half in range(2):
            state[key, :, 2 * half * DK : (2 * half + 1) * DK] = jnp.zeros((DK, DK), F32)
            state[key, :, (2 * half + 1) * DK : (2 * half + 2) * DK] = identity

    def advance(chunk):
        beta = betas[chunk]
        log = logs[chunk]
        growth = jnp.exp(log)
        last = log[ROWS - 1 : ROWS, :]
        shrink = jnp.exp(last - log)
        whole = jnp.exp(last)
        held = [state[key] for key in range(KEYS)]
        if chunk == CHUNKS // 2:
            held = [jnp.where(scal[3] > 0, 0.0, value) for value in held]
        lows = [value.astype(BF16) for value in held]
        for key in range(KEYS):
            xs[chunk, key] = lows[key]
        seen = [dot(khat[chunk, key], lows[key]) for key in range(KEYS)]
        yield
        wanted = []
        for head in range(HEADS):
            at = HEADS + head
            half = head % 2
            factor = beta[:, head : head + 1] * growth[:, at : at + 1]
            part = seen[head // 2][:, 2 * half * DK : (2 * half + 2) * DK] * factor
            wanted.append(jnp.concatenate([values[chunk, head] - part[:, :DK], -part[:, DK:]], axis=1))
        solved = [
            value + dot(rest[chunk, head], value.astype(BF16)) for head, value in enumerate(wanted)
        ]
        yield
        updates = []
        scales = []
        for head in range(HEADS):
            at = HEADS + head
            vs[chunk, head] = solved[head].astype(BF16)
            updates.append((solved[head] * shrink[:, at : at + 1]).astype(BF16))
            scales.append(jnp.broadcast_to(whole[:, at : at + 1], (1, 2 * DK)))
        for key in range(KEYS):
            scale = jnp.concatenate(scales[2 * key : 2 * key + 2], axis=1)
            update = jnp.concatenate(updates[2 * key : 2 * key + 2], axis=1)
            state[key] = held[key] * scale + dot(kturn[chunk, key], update)
        for copy in copies_out(chunk):
            copy.start()
        yield

    def advance_all(chunks):
        for chunk in chunks:
            yield from advance(chunk)

    def copies_out(chunk):
        return [
            pltpu.make_async_copy(held.at[chunk], target.at[chunk], out_sems.at[place, chunk])
            for place, (held, target) in enumerate(((xs, xs_out), (vs, vs_out), (khat, khat_out), (logs, logs_out)))
        ]

    early, late = list(range(CHUNKS // 2)), list(range(CHUNKS // 2, CHUNKS))
    for unused in prepare_all(early):
        pass
    for unused in itertools.zip_longest(prepare_all(late), advance_all(early)):
        pass
    for unused in advance_all(late):
        pass
    for key in range(KEYS):
        for half in range(2):
            xend[2 * key + half] = state[key, :, 2 * half * DK : (2 * half + 2) * DK].astype(BF16)
    for chunk in range(CHUNKS):
        for copy in copies_out(chunk):
            copy.wait()


def state_call(scal, pieces, tail, taps, decay, bias):
    vmem = pl.BlockSpec(memory_space=pltpu.VMEM)
    hbm = pl.BlockSpec(memory_space=pltpu.HBM)
    return pl.pallas_call(
        state_kernel,
        out_shape=(
            jax.ShapeDtypeStruct((HEADS, DK, 2 * DK), BF16),
            pltpu.HBM((CHUNKS, KEYS, DK, 4 * DK), BF16),
            pltpu.HBM((CHUNKS, HEADS, ROWS, 2 * DK), BF16),
            pltpu.HBM((CHUNKS, KEYS, ROWS, DK), BF16),
            pltpu.HBM((CHUNKS, ROWS, 128), F32),
        ),
        in_specs=[pl.BlockSpec(memory_space=pltpu.SMEM), hbm, hbm, hbm] + [vmem] * 4,
        out_specs=[vmem] + [hbm] * 4,
        scratch_shapes=[
            pltpu.VMEM((LEAD + CHUNKS * ROWS, COL_END), BF16),
            pltpu.VMEM((CHUNKS, HEADS, ROWS, ROWS), BF16),
            pltpu.VMEM((CHUNKS, KEYS, DK, ROWS), BF16),
            pltpu.VMEM((CHUNKS, HEADS, ROWS, DK), F32),
            pltpu.VMEM((CHUNKS, ROWS, 128), F32),
            pltpu.VMEM((KEYS, DK, 4 * DK), F32),
            pltpu.VMEM((CHUNKS, KEYS, DK, 4 * DK), BF16),
            pltpu.VMEM((CHUNKS, HEADS, ROWS, 2 * DK), BF16),
            pltpu.VMEM((CHUNKS, KEYS, ROWS, DK), BF16),
            pltpu.VMEM((CHUNKS, ROWS, 128), F32),
            pltpu.SemaphoreType.DMA((CHUNKS,)),
            pltpu.SemaphoreType.DMA((4, CHUNKS)),
        ],
        compiler_params=pltpu.CompilerParams(vmem_limit_bytes=40 * MIB),
        cost_estimate=pl.CostEstimate(flops=6_000_000_000, bytes_accessed=20_000_000, transcendentals=0),
        name="state",
    )(scal, *map(hold, pieces), tail, taps, decay, bias)


def read_kernel(
    scal, piece_a, piece_b, piece_c, tail, taps, xs, vs, khat, logs, out, raw, sems
):
    step = pl.program_id(0)

    @pl.when(step == 0)
    def _():
        raw[0:LEAD, :] = tail[...]
        fetch_rows(scal, (piece_a, piece_b, piece_c), raw, sems, 0, COL_K, 0)

    inclusive = iota2(0) >= iota2(1)
    queries, weights, growths = [], [], []
    for core in range(NC):
        chunk = NC * step + core
        start = pl.multiple_of(chunk * ROWS, ROWS)
        reset = is_reset(scal, chunk) if core == 0 else False
        mixed = mixed_rows(raw.at[pl.ds(start, ROWS + LEAD)], 0, 0, COL_K, taps, reset)
        queries += [(value * DK ** (-0.5)).astype(BF16) for value in unit_heads(mixed)]
        log = logs[core]
        log_turned = log.T
        growth = jnp.exp(log)
        for head in range(HEADS):
            at = HEADS + head
            growths.append(growth[:, at : at + 1])
            spread = log[:, at : at + 1] - log_turned[at : at + 1, :]
            weights.append(jnp.where(inclusive, jnp.exp(jnp.minimum(spread, 0.0)), 0.0))
    pairs = [(core, key) for core in range(NC) for key in range(KEYS)]
    products = [dot(queries[i], khat[core, key], ((1,), (1,))) for i, (core, key) in enumerate(pairs)]
    seen = [dot(queries[i], xs[core, key]) for i, (core, key) in enumerate(pairs)]
    for core in range(NC):
        other = jnp.bitwise_xor(core, scal[1])
        for head in range(HEADS):
            pair = core * KEYS + head // 2
            half = head % 2
            scores = (products[pair] * weights[core * HEADS + head]).astype(BF16)
            found = seen[pair][:, 2 * half * DK : (2 * half + 2) * DK] * growths[core * HEADS + head]
            out[other, head] = (found + dot(scores, vs[core, head])).astype(BF16)


def read_call(scal, pieces, tail, taps, xs, vs, khat, logs):
    hbm = pl.BlockSpec(memory_space=pltpu.HBM)
    return pl.pallas_call(
        read_kernel,
        out_shape=pltpu.HBM((NC, NY, HEADS, ROWS, 2 * DK), BF16),
        grid_spec=pltpu.PrefetchScalarGridSpec(
            num_scalar_prefetch=1,
            grid=(CHUNKS // NC,),
            in_specs=[
                hbm,
                hbm,
                hbm,
                pl.BlockSpec((LEAD, COL_K), lambda c, scal: (0, 0)),
                pl.BlockSpec((4, COL_K), lambda c, scal: (0, 0)),
                pl.BlockSpec((NC, KEYS, DK, 4 * DK), lambda c, scal: (c, 0, 0, 0)),
                pl.BlockSpec((NC, HEADS, ROWS, 2 * DK), lambda c, scal: (c, 0, 0, 0)),
                pl.BlockSpec((NC, KEYS, ROWS, DK), lambda c, scal: (c, 0, 0, 0)),
                pl.BlockSpec((NC, ROWS, 128), lambda c, scal: (c, 0, 0)),
            ],
            out_specs=pl.BlockSpec(
                (NC, None, HEADS, ROWS, 2 * DK),
                lambda c, scal: (0, lax.rem(c - scal[0] + NY, NY), 0, 0, 0),
            ),
            scratch_shapes=[
                pltpu.VMEM((LEAD + CHUNKS * ROWS, COL_K), BF16),
                pltpu.SemaphoreType.DMA((CHUNKS,)),
            ],
        ),
        compiler_params=pltpu.CompilerParams(vmem_limit_bytes=32 * MIB),
        cost_estimate=pl.CostEstimate(flops=3_000_000_000, bytes_accessed=10_000_000, transcendentals=0),
        name="read",
    )(scal, *map(hold, pieces), tail, taps, hold(xs), hold(vs), hold(khat), hold(logs))


def norm_kernel(tokens, gain, out):
    out[...] = scaled_rows(tokens[...], gain[...][None, :]).astype(BF16)


def norm_call(tokens, gain):
    vmem = pl.BlockSpec(memory_space=pltpu.VMEM)
    return pl.pallas_call(
        norm_kernel,
        out_shape=jax.ShapeDtypeStruct(tokens.shape, BF16),
        in_specs=[vmem, vmem],
        out_specs=vmem,
        cost_estimate=pl.CostEstimate(flops=1_000_000, bytes_accessed=1_000_000, transcendentals=0),
        name="norm",
    )(tokens, gain)


def after(late, early):
    moved = dot(late[:, DK:], early)
    if early.shape[1] == DK:
        return moved + late[:, :DK].astype(F32)
    return jnp.concatenate([moved[:, :DK] + late[:, :DK].astype(F32), moved[:, DK:]], axis=1)


def row_kernel(parts, leads, whole, sums):
    held = parts[0]
    leads[0] = held
    for place in range(1, NX):
        held = after(parts[place], held).astype(BF16)
        if place < NX - 1:
            leads[place] = held
    whole[...] = held
    sums[...] = held[:, :DK]


def row_call(parts):
    vmem = pl.BlockSpec(memory_space=pltpu.VMEM)
    return pl.pallas_call(
        row_kernel,
        out_shape=(
            jax.ShapeDtypeStruct((NX - 1, DK, 2 * DK), BF16),
            jax.ShapeDtypeStruct((DK, 2 * DK), BF16),
            jax.ShapeDtypeStruct((DK, DK), BF16),
        ),
        in_specs=[vmem],
        out_specs=[vmem] * 3,
        cost_estimate=pl.CostEstimate(flops=100_000_000, bytes_accessed=1_000_000, transcendentals=0),
        name="rows",
    )(parts)


def open_kernel(one, two, three, four, leads, out):
    opening = four[...]
    for earlier in (three, two, one):
        opening = after(earlier[...], opening).astype(BF16)
    out[0] = opening
    for place in range(1, NX):
        out[place] = after(leads[place - 1], opening).astype(BF16)


def open_call(earlier, leads):
    vmem = pl.BlockSpec(memory_space=pltpu.VMEM)
    return pl.pallas_call(
        open_kernel,
        out_shape=jax.ShapeDtypeStruct((NX, DK, DK), BF16),
        in_specs=[vmem] * 5,
        out_specs=vmem,
        cost_estimate=pl.CostEstimate(flops=100_000_000, bytes_accessed=1_000_000, transcendentals=0),
        name="open",
    )(*earlier, leads)


def out_kernel(other, scal, found, gates, opening, gain, w_out, out):
    rows = []
    moved = [
        [dot(found[block, head][:, DK:], opening[head]) for head in range(HEADS)]
        for block in range(2)
    ]
    for block in range(2):
        steps = 2 * pl.program_id(0) + block
        core = scal[1] if other == 0 else 1 - scal[1]
        chunk = lax.rem(scal[0] + steps, NY) * NC + core
        first = lax.rem(chunk, STRETCH // ROWS) * ROWS
        fill = jnp.where(chunk < CHUNKS // 2, scal[4], scal[5])
        within = lax.broadcasted_iota(jnp.int32, (ROWS, 1), 0) + first
        kept = within < fill
        parts = []
        for head in range(HEADS):
            value = found[block, head][:, :DK].astype(F32) + moved[block][head]
            value = jnp.where(kept, value, 0.0)
            gate = gates[block, :, head * DK : (head + 1) * DK].astype(F32)
            spread = jnp.mean(value * value, axis=-1, keepdims=True)
            parts.append((value * lax.rsqrt(spread + EPSILON) * gain[...] * silu(gate)).astype(BF16))
        rows.append(jnp.concatenate(parts, axis=1))
    total = dot(jnp.concatenate(rows, axis=0), w_out[...]).astype(BF16)
    out[...] = total.reshape(out.shape)


def out_call(other, scal, found, gates, opening, gain, w_out):
    width = w_out.shape[1]
    return pl.pallas_call(
        lambda *refs: out_kernel(other, *refs),
        grid=(NY // 2,),
        out_shape=jax.ShapeDtypeStruct((NY, ROWS, width), BF16),
        in_specs=[
            pl.BlockSpec(memory_space=pltpu.SMEM),
            pl.BlockSpec((None, 2, HEADS, ROWS, 2 * DK), lambda i: (other, i, 0, 0, 0)),
            pl.BlockSpec((2, ROWS, HEADS * DK), lambda i: (i, 0, 0)),
            pl.BlockSpec((HEADS, DK, DK), lambda i: (0, 0, 0)),
            pl.BlockSpec((1, DK), lambda i: (0, 0)),
            pl.BlockSpec((HEADS * DK, width), lambda i: (0, 0)),
        ],
        out_specs=pl.BlockSpec((2, ROWS, width), lambda i: (i, 0, 0)),
        compiler_params=pltpu.CompilerParams(vmem_limit_bytes=32 * MIB),
        cost_estimate=pl.CostEstimate(flops=1_200_000_000, bytes_accessed=6_000_000, transcendentals=0),
        name="out",
    )(scal, hold(found), hold(gates), opening, gain, w_out)


def sum_kernel(own, received, rows, pass_up, pass_down, free_up, free_down, more_up, more_down):
    half = own.shape[2] // 2
    total = own[2].astype(F32) + received[2].astype(F32)
    pass_up[...] = total[:, :half].astype(BF16)
    pass_down[...] = total[:, half:].astype(BF16)
    total = own[1].astype(F32) + received[1].astype(F32)
    more_up[...] = total[:, :half].astype(BF16)
    free_up[...] = total[:, half:].astype(BF16)
    total = own[3].astype(F32) + received[3].astype(F32)
    free_down[...] = total[:, :half].astype(BF16)
    more_down[...] = total[:, half:].astype(BF16)
    rows[...] = (own[0].astype(F32) + received[0].astype(F32)).astype(BF16)


def sum_call(own, received):
    vmem = pl.BlockSpec(memory_space=pltpu.VMEM)
    width = own.shape[2]
    half = jax.ShapeDtypeStruct((ROWS, width // 2), BF16)
    return pl.pallas_call(
        sum_kernel,
        out_shape=(jax.ShapeDtypeStruct((ROWS, width), BF16),) + (half,) * 6,
        in_specs=[vmem] * 2,
        out_specs=[vmem] * 7,
        compiler_params=pltpu.CompilerParams(vmem_limit_bytes=16 * MIB),
        cost_estimate=pl.CostEstimate(flops=1_000_000, bytes_accessed=6_000_000, transcendentals=0),
        name="sum",
    )(own, received)


def expert_kernel(
    rows, more_up, free_up, free_down, more_down, tokens, gain, w_sgate, shared,
    attention, layer, weights, sems,
):
    size = shared.shape[1] // 4
    copies = [
        [
            pltpu.make_async_copy(
                shared.at[place, pl.ds(part * size, size)],
                weights.at[place, pl.ds(part * size, size)],
                sems.at[4 * place + part],
            )
            for part in range(4)
        ]
        for place in range(3)
    ]
    for place in range(3):
        for copy in copies[place]:
            copy.start()
    ups = jnp.concatenate([more_up[...], free_up[...]], axis=1)
    downs = jnp.concatenate([free_down[...], more_down[...]], axis=1)
    total = rows[...].astype(F32) + ups.astype(F32) + downs.astype(F32)
    total = total.astype(BF16)
    attention[...] = total
    residual = (tokens[...].astype(F32) + total.astype(F32)).astype(BF16)
    normed = scaled_rows(residual, gain[...][None, :]).astype(BF16)
    weighed = normed.astype(F32) * w_sgate[...][None, :].astype(F32)
    gate = sigmoid(jnp.sum(weighed, axis=-1, keepdims=True))
    for copy in copies[0]:
        copy.wait()
    gate_part = dot(normed, weights[0], ((1,), (1,)))
    for copy in copies[1]:
        copy.wait()
    up_part = dot(normed, weights[1], ((1,), (1,)))
    hidden = (silu(gate_part) * up_part).astype(BF16)
    for copy in copies[2]:
        copy.wait()
    layer[...] = (residual.astype(F32) + gate * dot(hidden, weights[2])).astype(BF16)


def expert_call(rows, more_up, free_up, free_down, more_down, tokens, gain, w_sgate, shared):
    vmem = pl.BlockSpec(memory_space=pltpu.VMEM)
    return pl.pallas_call(
        expert_kernel,
        out_shape=(jax.ShapeDtypeStruct(tokens.shape, BF16),) * 2,
        in_specs=[vmem] * 8 + [pl.BlockSpec(memory_space=pltpu.HBM)],
        out_specs=[vmem] * 2,
        scratch_shapes=[pltpu.VMEM(shared.shape, BF16), pltpu.SemaphoreType.DMA((12,))],
        compiler_params=pltpu.CompilerParams(vmem_limit_bytes=32 * MIB),
        cost_estimate=pl.CostEstimate(flops=800_000_000, bytes_accessed=9_000_000, transcendentals=0),
        name="expert",
    )(rows, more_up, free_up, free_down, more_down, tokens, gain, w_sgate, hold(shared))


def per_device(
    tokens,
    stretch_prompt,
    last_fill,
    ln1_gain,
    w_qk,
    w_vz,
    w_ba,
    conv_qk,
    conv_value,
    decay_log,
    dt_bias,
    norm_gain,
    w_out,
    ln2_gain,
    w_sgate,
    shared_weights,
):
    width = tokens.shape[1]
    place_y = lax.axis_index("y")
    place_core = lax.axis_index("core")
    device = lax.axis_index("z") * NX + lax.axis_index("x")
    normed = norm_call(tokens, ln1_gain)

    below = turn(normed, "y", 1, NY)
    above = turn(normed, "y", -1, NY)
    beside = turn(normed, "core", 1, NC)
    flat_vz = w_vz.reshape(width, -1)
    half_vz = flat_vz.shape[1] // 2
    weight = jnp.concatenate(
        [
            w_qk.reshape(width, -1),
            flat_vz[:, :half_vz],
            jnp.pad(w_ba.reshape(width, -1), ((0, 0), (0, 128 - 2 * HEADS))),
        ],
        axis=1,
    )
    weight_z = flat_vz[:, half_vz:]

    def project(weight, *parts):
        rows = jnp.concatenate(parts, axis=0)
        return jnp.dot(rows, weight, preferred_element_type=F32).astype(BF16)

    piece_a = project(weight, normed, beside)
    below, above, piece_a = lax.optimization_barrier((below, above, piece_a))
    across_up = turn(below[: ROWS // 2], "y", 1, NY)
    across_down = turn(above[ROWS // 2 :], "y", -1, NY)
    above_beside = turn(above, "core", 1, NC)
    below_beside = turn(below, "core", 1, NC)
    above, below, above_beside, below_beside = lax.optimization_barrier(
        (above, below, above_beside, below_beside)
    )
    piece_b = project(weight, above, below, above_beside, below_beside)
    across_up, across_down, piece_b = lax.optimization_barrier((across_up, across_down, piece_b))
    across = jnp.concatenate([across_up, across_down], axis=0)
    across_beside = turn(across, "core", 1, NC)
    piece_c = project(weight, across, across_beside)
    shared_weights, piece_c = lax.optimization_barrier((shared_weights, piece_c))
    pieces = (piece_a, piece_b, piece_c)
    gathered = lax.all_gather(shared_weights, ("y", "core"), axis=1, tiled=True)

    first_slot = device * 2
    before = jnp.concatenate([jnp.full((1,), -1, jnp.int32), stretch_prompt])
    later = jnp.concatenate([stretch_prompt, jnp.full((1,), -1, jnp.int32)])
    current = lax.dynamic_slice_in_dim(stretch_prompt, first_slot, 2)
    starts = current != lax.dynamic_slice_in_dim(before, first_slot, 2)
    finishes = current != lax.dynamic_slice_in_dim(later, first_slot + 1, 2)
    fill = jnp.where(finishes, lax.dynamic_slice_in_dim(last_fill, first_slot, 2), STRETCH)
    scal = jnp.concatenate(
        [jnp.stack([place_y, place_core]).astype(jnp.int32), starts.astype(jnp.int32), fill]
    )

    last_place = (NY - 1 - place_y) * NC + (NC - 1 - place_core)
    ends = piece_a[ROWS - LEAD : ROWS, :COL_BA]
    for (steps, other), (piece, block) in PLACES.items():
        rows = pieces[piece][(block + 1) * ROWS - LEAD : (block + 1) * ROWS, :COL_BA]
        ends = jnp.where(last_place == steps * NC + other, rows, ends)
    tail = push(ends, ("z", "x"), 1, NZ * NX)

    def gates(*parts):
        rows = jnp.concatenate(parts, axis=0)
        gate = jnp.dot(rows, weight_z, preferred_element_type=F32).astype(BF16)
        return gate.reshape(NY, ROWS, -1)

    gates_beside = gates(beside, above_beside, across_beside, below_beside)
    gates_own = gates(normed, above, across, below)
    tail, gates_own = lax.optimization_barrier((tail, gates_own))
    taps_qk = conv_qk.astype(F32)
    taps_kv = jnp.concatenate([taps_qk[:, 1, :], conv_value.astype(F32)], axis=1)
    pad = ((HEADS, 128 - 2 * HEADS),)
    decay = jnp.pad(decay_log, pad)[None, :]
    bias = jnp.pad(dt_bias, pad)[None, :]
    xend, xs, vs, khat, logs = state_call(scal, pieces, tail, taps_kv, decay, bias)

    parts = lax.all_to_all(xend, "x", 0, 0, tiled=True)
    given = (tail[:, :COL_K], taps_qk[:, 0, :], xs, vs, khat, logs)
    parts, gates_beside = lax.optimization_barrier((parts, gates_beside))
    leads, whole, sums = row_call(parts)
    earlier = [push(whole if steps < 4 else sums, "z", steps, NZ) for steps in (1, 2, 3, 4)]
    openings = open_call(earlier, leads)
    opening = lax.all_to_all(openings, "x", 0, 0, tiled=True)

    found = read_call(scal, pieces, *given)

    gain = norm_gain.astype(F32)[None, :]
    lent = out_call(1, scal, found, gates_beside, opening, gain, w_out)
    received = turn(lent, "core", 1, NC)
    own = out_call(0, scal, found, gates_own, opening, gain, w_out)

    own_rows, pass_up, pass_down, free_up, free_down, more_up, more_down = sum_call(own, received)
    pass_up = turn(pass_up, "y", 1, NY)
    pass_down = turn(pass_down, "y", -1, NY)
    free_up = turn(free_up, "y", 1, NY)
    free_down = turn(free_down, "y", -1, NY)
    more_up = turn((more_up.astype(F32) + pass_up.astype(F32)).astype(BF16), "y", 1, NY)
    more_down = turn((more_down.astype(F32) + pass_down.astype(F32)).astype(BF16), "y", -1, NY)
    return expert_call(
        own_rows, more_up, free_up, free_down, more_down, tokens, ln2_gain, w_sgate, gathered
    )


def solution(mesh):
    fine = Mesh(mesh.devices.reshape(NZ, NX, NY, NC), ("z", "x", "y", "core"))
    rows = P(("z", "x", "y", "core"), None)
    head = ("y", "core")
    return jax.shard_map(
        per_device,
        mesh=fine,
        in_specs=(
            rows,
            P(),
            P(),
            P(),
            P(None, None, head),
            P(None, None, head),
            P(None, None, head),
            P(None, None, head),
            P(None, head),
            P(head),
            P(head),
            P(),
            P(head, None),
            P(),
            P(),
            P(None, head, None),
        ),
        out_specs=(rows, rows),
        check_vma=False,
    )
```

```python
import itertools

import jax
import jax.numpy as jnp
from jax import lax
from jax.experimental import pallas as pl
from jax.experimental.pallas import tpu as pltpu
from jax.sharding import Mesh
from jax.sharding import PartitionSpec as P

F32 = jnp.float32
BF16 = jnp.bfloat16
EPSILON = 1e-06
DK = 128
STRETCH = 512
ROWS = 128
CHUNKS = 8
HEADS = 4
KEYS = 2
NZ, NX, NY, NC = 8, 4, 4, 2
LEAD = 16
COL_K = 256
COL_V = 512
COL_BA = 1024
COL_END = 1152
MIB = 1024 * 1024
PLACES = {
    (0, 0): (0, 0),
    (0, 1): (0, 1),
    (1, 0): (1, 0),
    (3, 0): (1, 1),
    (1, 1): (1, 2),
    (3, 1): (1, 3),
    (2, 0): (2, 0),
    (2, 1): (2, 1),
}


def dot(left, right, contract=((1,), (0,))):
    return lax.dot_general(left, right, (contract, ((), ())), preferred_element_type=F32)


def silu(value):
    return value * (0.5 * jnp.tanh(0.5 * value) + 0.5)


def sigmoid(value):
    return 0.5 * jnp.tanh(0.5 * value) + 0.5


def scaled_rows(inputs, scaling):
    widened = inputs.astype(F32)
    spread = jnp.mean(widened * widened, axis=-1, keepdims=True)
    return widened * lax.rsqrt(spread + EPSILON) * scaling.astype(F32)


def hold(value):
    return pltpu.with_memory_space_constraint(value, pltpu.HBM)


def turn(value, axis, steps, count):
    return lax.ppermute(value, axis, [(i, (i + steps) % count) for i in range(count)])


def push(value, axis, steps, count):
    return lax.ppermute(value, axis, [(i, i + steps) for i in range(count - steps)])


def mixed_rows(ref, chunk, first, last, taps, reset):
    start = chunk * ROWS if isinstance(chunk, int) else pl.multiple_of(chunk * ROWS, ROWS)
    rows = ref[pl.ds(start, ROWS + LEAD), first:last].astype(F32)
    if reset is not False:
        rows = jnp.concatenate([jnp.where(reset, 0.0, rows[:LEAD]), rows[LEAD:]], axis=0)
    total = rows[LEAD:] * taps[3:4]
    for offset in (1, 2, 3):
        total = total + rows[LEAD - offset : LEAD - offset + ROWS] * taps[3 - offset : 4 - offset]
    return silu(total)


def unit_heads(value):
    parts = []
    for head in range(value.shape[1] // DK):
        part = value[:, head * DK : (head + 1) * DK]
        parts.append(part * lax.rsqrt(jnp.sum(part * part, axis=-1, keepdims=True) + EPSILON))
    return parts


def fetch_rows(scal, pieces, scratch, sems, first, last, target):
    copies = []
    for (steps, other), (piece, block) in PLACES.items():
        row = lax.rem(scal[0] + steps, NY)
        core = scal[1] if other == 0 else 1 - scal[1]
        chunk = row * NC + core
        start = pl.multiple_of(chunk * ROWS + LEAD, LEAD)
        copy = pltpu.make_async_copy(
            pieces[piece].at[pl.ds(block * ROWS, ROWS), pl.ds(first, last - first)],
            scratch.at[pl.ds(start, ROWS), pl.ds(target, last - first)],
            sems.at[len(copies)],
        )
        copy.start()
        copies.append(copy)
    for copy in copies:
        copy.wait()


def is_reset(scal, chunk):
    if isinstance(chunk, int):
        return scal[2 + chunk * 2 // CHUNKS] > 0 if chunk % (CHUNKS // 2) == 0 else False
    first = jnp.logical_and(chunk == 0, scal[2] > 0)
    second = jnp.logical_and(chunk == CHUNKS // 2, scal[3] > 0)
    return jnp.logical_or(first, second)


def iota2(axis):
    return lax.broadcasted_iota(jnp.int32, (ROWS, ROWS), axis)


def odd_blocks(value, span):
    return jnp.concatenate([value[at : at + span] for at in range(span, ROWS, 2 * span)], axis=0)


def with_even(even, odd, span):
    parts = []
    for place, at in enumerate(range(0, ROWS, 2 * span)):
        block = odd[place * span : (place + 1) * span]
        parts.append(jnp.zeros_like(block) if even is None else even[at : at + span])
        parts.append(block)
    return jnp.concatenate(parts, axis=0)


def inverse_rests(stricts, level):
    rests = [jnp.where(level == 1, -strict, 0.0) for strict in stricts]
    for step in (2, 3):
        lows = [rest.astype(BF16) for rest in rests]
        belows = [jnp.where(level == step, strict, 0.0) for strict in stricts]
        halves = [below + dot(below.astype(BF16), low) for below, low in zip(belows, lows)]
        yield
        rests = [rest - half - dot(low, half.astype(BF16)) for rest, half, low in zip(rests, halves, lows)]
        yield
    for step in (4, 5, 6, 7):
        span = 1 << (step - 1)
        here = odd_blocks(level, span) == step
        lows = [rest.astype(BF16) for rest in rests]
        odds = [odd_blocks(rest, span) for rest in rests]
        belows = [jnp.where(here, odd_blocks(strict, span), 0.0) for strict in stricts]
        halves = [below + dot(below.astype(BF16), low) for below, low in zip(belows, lows)]
        yield
        wides = [with_even(None, half, span).astype(BF16) for half in halves]
        odds = [odd - half - dot(odd.astype(BF16), wide) for odd, half, wide in zip(odds, halves, wides)]
        rests = [with_even(rest, odd, span) for rest, odd in zip(rests, odds)]
        yield
    return rests


def block_levels():
    row, col = iota2(0), iota2(1)
    apart = jnp.where(row > col, jnp.bitwise_xor(row, col), 0)
    level = jnp.zeros((ROWS, ROWS), jnp.int32)
    for step in range(7):
        level = level + (apart >= (1 << step)).astype(jnp.int32)
    return level


def state_kernel(
    scal, piece_a, piece_b, piece_c, tail, taps, decay, bias,
    xend, xs_out, vs_out, khat_out, logs_out,
    raw, rest, kturn, values, betas, state, xs, vs, khat, logs, sems, out_sems,
):
    raw[0:LEAD, 0:COL_BA] = tail[...]
    fetch_rows(scal, (piece_a, piece_b, piece_c), raw, sems, COL_K, COL_END, COL_K)
    row, col = iota2(0), iota2(1)
    strict = row > col
    summing = (row >= col).astype(F32)
    level = block_levels()

    def prepare(chunk):
        reset = is_reset(scal, chunk)
        mixed = mixed_rows(raw, chunk, COL_K, COL_BA, taps, reset)
        start = chunk * ROWS + LEAD
        start = start if isinstance(chunk, int) else pl.multiple_of(start, LEAD)
        ba = raw[pl.ds(start, ROWS), COL_BA:COL_END].astype(F32)
        beta = sigmoid(ba)
        inner = ba + bias[...]
        soft = jnp.maximum(inner, 0.0) + jnp.log1p(jnp.exp(-jnp.abs(inner)))
        rate = -jnp.exp(decay[...]) * soft
        log = lax.dot_general(
            summing, rate, (((1,), (0,)), ((), ())),
            precision=lax.Precision.HIGHEST, preferred_element_type=F32,
        )
        log_turned = log.T
        betas[chunk] = beta
        logs[chunk] = log
        unit = unit_heads(mixed[:, : KEYS * DK])
        lowers = []
        for key in range(KEYS):
            key_rows = unit[key].astype(BF16)
            khat[chunk, key] = key_rows
            kturn[chunk, key] = unit[key].T.astype(BF16)
            products = dot(key_rows, key_rows, ((1,), (1,)))
            for half in range(2):
                head = 2 * key + half
                beta_col = beta[:, head : head + 1]
                spread = log[:, HEADS + head : HEADS + head + 1] - log_turned[HEADS + head : HEADS + head + 1, :]
                weight = jnp.exp(jnp.minimum(spread, 0.0))
                lower = jnp.where(strict, products * beta_col * weight, 0.0)
                lowers.append(lower)
                value = mixed[:, (KEYS + head) * DK : (KEYS + head + 1) * DK]
                values[chunk, head] = value * beta_col
        return lowers

    def prepare_all(chunks):
        lowers = []
        for chunk in chunks:
            lowers += prepare(chunk)
            yield
        found = yield from inverse_rests(lowers, level)
        for place, value in enumerate(found):
            rest[chunks[place // HEADS], place % HEADS] = value.astype(BF16)

    opening = jnp.where(scal[2] > 0, 0.0, 1.0)
    identity = jnp.where(row == col, opening, 0.0)
    for key in range(KEYS):
        for half in range(2):
            state[key, :, 2 * half * DK : (2 * half + 1) * DK] = jnp.zeros((DK, DK), F32)
            state[key, :, (2 * half + 1) * DK : (2 * half + 2) * DK] = identity

    def advance(chunk):
        beta = betas[chunk]
        log = logs[chunk]
        growth = jnp.exp(log)
        last = log[ROWS - 1 : ROWS, :]
        shrink = jnp.exp(last - log)
        whole = jnp.exp(last)
        held = [state[key] for key in range(KEYS)]
        fresh = jnp.logical_and(chunk == CHUNKS // 2, scal[3] > 0)
        held = [jnp.where(fresh, 0.0, value) for value in held]
        lows = [value.astype(BF16) for value in held]
        for key in range(KEYS):
            xs[chunk, key] = lows[key]
        seen = [dot(khat[chunk, key], lows[key]) for key in range(KEYS)]
        yield
        wanted = []
        for head in range(HEADS):
            at = HEADS + head
            half = head % 2
            factor = beta[:, head : head + 1] * growth[:, at : at + 1]
            part = seen[head // 2][:, 2 * half * DK : (2 * half + 2) * DK] * factor
            wanted.append(jnp.concatenate([values[chunk, head] - part[:, :DK], -part[:, DK:]], axis=1))
        solved = [
            value + dot(rest[chunk, head], value.astype(BF16)) for head, value in enumerate(wanted)
        ]
        yield
        updates = []
        scales = []
        for head in range(HEADS):
            at = HEADS + head
            vs[chunk, head] = solved[head].astype(BF16)
            updates.append((solved[head] * shrink[:, at : at + 1]).astype(BF16))
            scales.append(jnp.broadcast_to(whole[:, at : at + 1], (1, 2 * DK)))
        for key in range(KEYS):
            scale = jnp.concatenate(scales[2 * key : 2 * key + 2], axis=1)
            update = jnp.concatenate(updates[2 * key : 2 * key + 2], axis=1)
            state[key] = held[key] * scale + dot(kturn[chunk, key], update)
        for copy in copies_out(chunk):
            copy.start()
        yield

    def advance_all(chunks):
        for chunk in chunks:
            yield from advance(chunk)

    def copies_out(chunk):
        return [
            pltpu.make_async_copy(held.at[chunk], target.at[chunk], out_sems.at[place, chunk])
            for place, (held, target) in enumerate(((xs, xs_out), (vs, vs_out), (khat, khat_out), (logs, logs_out)))
        ]

    def both(pair, unused):
        chain = advance_all((2 * pair - 2, 2 * pair - 1))
        for place, also_unused in enumerate(prepare_all((2 * pair, 2 * pair + 1))):
            if place % 2 == 1:
                next(chain, None)
        for also_unused in chain:
            pass
        return unused

    def last(chunk, unused):
        for also_unused in advance(chunk):
            pass
        return unused

    for unused in prepare_all((0, 1)):
        pass
    lax.fori_loop(1, CHUNKS // 2, both, 0)
    lax.fori_loop(CHUNKS - 2, CHUNKS, last, 0)
    for key in range(KEYS):
        for half in range(2):
            xend[2 * key + half] = state[key, :, 2 * half * DK : (2 * half + 2) * DK].astype(BF16)
    for chunk in range(CHUNKS):
        for copy in copies_out(chunk):
            copy.wait()


def state_call(scal, pieces, tail, taps, decay, bias):
    vmem = pl.BlockSpec(memory_space=pltpu.VMEM)
    hbm = pl.BlockSpec(memory_space=pltpu.HBM)
    return pl.pallas_call(
        state_kernel,
        out_shape=(
            jax.ShapeDtypeStruct((HEADS, DK, 2 * DK), BF16),
            pltpu.HBM((CHUNKS, KEYS, DK, 4 * DK), BF16),
            pltpu.HBM((CHUNKS, HEADS, ROWS, 2 * DK), BF16),
            pltpu.HBM((CHUNKS, KEYS, ROWS, DK), BF16),
            pltpu.HBM((CHUNKS, ROWS, 128), F32),
        ),
        in_specs=[pl.BlockSpec(memory_space=pltpu.SMEM), hbm, hbm, hbm] + [vmem] * 4,
        out_specs=[vmem] + [hbm] * 4,
        scratch_shapes=[
            pltpu.VMEM((LEAD + CHUNKS * ROWS, COL_END), BF16),
            pltpu.VMEM((CHUNKS, HEADS, ROWS, ROWS), BF16),
            pltpu.VMEM((CHUNKS, KEYS, DK, ROWS), BF16),
            pltpu.VMEM((CHUNKS, HEADS, ROWS, DK), F32),
            pltpu.VMEM((CHUNKS, ROWS, 128), F32),
            pltpu.VMEM((KEYS, DK, 4 * DK), F32),
            pltpu.VMEM((CHUNKS, KEYS, DK, 4 * DK), BF16),
            pltpu.VMEM((CHUNKS, HEADS, ROWS, 2 * DK), BF16),
            pltpu.VMEM((CHUNKS, KEYS, ROWS, DK), BF16),
            pltpu.VMEM((CHUNKS, ROWS, 128), F32),
            pltpu.SemaphoreType.DMA((CHUNKS,)),
            pltpu.SemaphoreType.DMA((4, CHUNKS)),
        ],
        compiler_params=pltpu.CompilerParams(vmem_limit_bytes=40 * MIB),
        cost_estimate=pl.CostEstimate(flops=6_000_000_000, bytes_accessed=20_000_000, transcendentals=0),
        name="state",
    )(scal, *map(hold, pieces), tail, taps, decay, bias)


def read_kernel(
    scal, piece_a, piece_b, piece_c, tail, taps, xs, vs, khat, logs, out, raw, sems
):
    step = pl.program_id(0)

    @pl.when(step == 0)
    def _():
        raw[0:LEAD, :] = tail[...]
        fetch_rows(scal, (piece_a, piece_b, piece_c), raw, sems, 0, COL_K, 0)

    inclusive = iota2(0) >= iota2(1)
    queries, weights, growths = [], [], []
    for core in range(NC):
        chunk = NC * step + core
        start = pl.multiple_of(chunk * ROWS, ROWS)
        reset = is_reset(scal, chunk) if core == 0 else False
        mixed = mixed_rows(raw.at[pl.ds(start, ROWS + LEAD)], 0, 0, COL_K, taps, reset)
        queries += [(value * DK ** (-0.5)).astype(BF16) for value in unit_heads(mixed)]
        log = logs[core]
        log_turned = log.T
        growth = jnp.exp(log)
        for head in range(HEADS):
            at = HEADS + head
            growths.append(growth[:, at : at + 1])
            spread = log[:, at : at + 1] - log_turned[at : at + 1, :]
            weights.append(jnp.where(inclusive, jnp.exp(jnp.minimum(spread, 0.0)), 0.0))
    pairs = [(core, key) for core in range(NC) for key in range(KEYS)]
    products = [dot(queries[i], khat[core, key], ((1,), (1,))) for i, (core, key) in enumerate(pairs)]
    seen = [dot(queries[i], xs[core, key]) for i, (core, key) in enumerate(pairs)]
    for core in range(NC):
        other = jnp.bitwise_xor(core, scal[1])
        for head in range(HEADS):
            pair = core * KEYS + head // 2
            half = head % 2
            scores = (products[pair] * weights[core * HEADS + head]).astype(BF16)
            found = seen[pair][:, 2 * half * DK : (2 * half + 2) * DK] * growths[core * HEADS + head]
            out[other, head] = (found + dot(scores, vs[core, head])).astype(BF16)


def read_call(scal, pieces, tail, taps, xs, vs, khat, logs):
    hbm = pl.BlockSpec(memory_space=pltpu.HBM)
    return pl.pallas_call(
        read_kernel,
        out_shape=pltpu.HBM((NC, NY, HEADS, ROWS, 2 * DK), BF16),
        grid_spec=pltpu.PrefetchScalarGridSpec(
            num_scalar_prefetch=1,
            grid=(CHUNKS // NC,),
            in_specs=[
                hbm,
                hbm,
                hbm,
                pl.BlockSpec((LEAD, COL_K), lambda c, scal: (0, 0)),
                pl.BlockSpec((4, COL_K), lambda c, scal: (0, 0)),
                pl.BlockSpec((NC, KEYS, DK, 4 * DK), lambda c, scal: (c, 0, 0, 0)),
                pl.BlockSpec((NC, HEADS, ROWS, 2 * DK), lambda c, scal: (c, 0, 0, 0)),
                pl.BlockSpec((NC, KEYS, ROWS, DK), lambda c, scal: (c, 0, 0, 0)),
                pl.BlockSpec((NC, ROWS, 128), lambda c, scal: (c, 0, 0)),
            ],
            out_specs=pl.BlockSpec(
                (NC, None, HEADS, ROWS, 2 * DK),
                lambda c, scal: (0, lax.rem(c - scal[0] + NY, NY), 0, 0, 0),
            ),
            scratch_shapes=[
                pltpu.VMEM((LEAD + CHUNKS * ROWS, COL_K), BF16),
                pltpu.SemaphoreType.DMA((CHUNKS,)),
            ],
        ),
        compiler_params=pltpu.CompilerParams(vmem_limit_bytes=32 * MIB),
        cost_estimate=pl.CostEstimate(flops=3_000_000_000, bytes_accessed=10_000_000, transcendentals=0),
        name="read",
    )(scal, *map(hold, pieces), tail, taps, hold(xs), hold(vs), hold(khat), hold(logs))


def norm_kernel(tokens, gain, out):
    out[...] = scaled_rows(tokens[...], gain[...][None, :]).astype(BF16)


def norm_call(tokens, gain):
    vmem = pl.BlockSpec(memory_space=pltpu.VMEM)
    return pl.pallas_call(
        norm_kernel,
        out_shape=jax.ShapeDtypeStruct(tokens.shape, BF16),
        in_specs=[vmem, vmem],
        out_specs=vmem,
        cost_estimate=pl.CostEstimate(flops=1_000_000, bytes_accessed=1_000_000, transcendentals=0),
        name="norm",
    )(tokens, gain)


def after(late, early):
    moved = dot(late[:, DK:], early)
    if early.shape[1] == DK:
        return moved + late[:, :DK].astype(F32)
    return jnp.concatenate([moved[:, :DK] + late[:, :DK].astype(F32), moved[:, DK:]], axis=1)


def row_kernel(parts, leads, whole, sums):
    held = parts[0]
    leads[0] = held
    for place in range(1, NX):
        held = after(parts[place], held).astype(BF16)
        if place < NX - 1:
            leads[place] = held
    whole[...] = held
    sums[...] = held[:, :DK]


def row_call(parts):
    vmem = pl.BlockSpec(memory_space=pltpu.VMEM)
    return pl.pallas_call(
        row_kernel,
        out_shape=(
            jax.ShapeDtypeStruct((NX - 1, DK, 2 * DK), BF16),
            jax.ShapeDtypeStruct((DK, 2 * DK), BF16),
            jax.ShapeDtypeStruct((DK, DK), BF16),
        ),
        in_specs=[vmem],
        out_specs=[vmem] * 3,
        cost_estimate=pl.CostEstimate(flops=100_000_000, bytes_accessed=1_000_000, transcendentals=0),
        name="rows",
    )(parts)


def open_kernel(one, two, three, four, leads, out):
    opening = four[...]
    for earlier in (three, two, one):
        opening = after(earlier[...], opening).astype(BF16)
    out[0] = opening
    for place in range(1, NX):
        out[place] = after(leads[place - 1], opening).astype(BF16)


def open_call(earlier, leads):
    vmem = pl.BlockSpec(memory_space=pltpu.VMEM)
    return pl.pallas_call(
        open_kernel,
        out_shape=jax.ShapeDtypeStruct((NX, DK, DK), BF16),
        in_specs=[vmem] * 5,
        out_specs=vmem,
        cost_estimate=pl.CostEstimate(flops=100_000_000, bytes_accessed=1_000_000, transcendentals=0),
        name="open",
    )(*earlier, leads)


def out_kernel(other, scal, found, gates, opening, gain, w_out, out):
    rows = []
    moved = [
        [dot(found[block, head][:, DK:], opening[head]) for head in range(HEADS)]
        for block in range(2)
    ]
    for block in range(2):
        steps = 2 * pl.program_id(0) + block
        core = scal[1] if other == 0 else 1 - scal[1]
        chunk = lax.rem(scal[0] + steps, NY) * NC + core
        first = lax.rem(chunk, STRETCH // ROWS) * ROWS
        fill = jnp.where(chunk < CHUNKS // 2, scal[4], scal[5])
        within = lax.broadcasted_iota(jnp.int32, (ROWS, 1), 0) + first
        kept = within < fill
        parts = []
        for head in range(HEADS):
            value = found[block, head][:, :DK].astype(F32) + moved[block][head]
            value = jnp.where(kept, value, 0.0)
            gate = gates[block, :, head * DK : (head + 1) * DK].astype(F32)
            spread = jnp.mean(value * value, axis=-1, keepdims=True)
            parts.append((value * lax.rsqrt(spread + EPSILON) * gain[...] * silu(gate)).astype(BF16))
        rows.append(jnp.concatenate(parts, axis=1))
    total = dot(jnp.concatenate(rows, axis=0), w_out[...]).astype(BF16)
    out[...] = total.reshape(out.shape)


def out_call(other, scal, found, gates, opening, gain, w_out):
    width = w_out.shape[1]
    return pl.pallas_call(
        lambda *refs: out_kernel(other, *refs),
        grid=(NY // 2,),
        out_shape=jax.ShapeDtypeStruct((NY, ROWS, width), BF16),
        in_specs=[
            pl.BlockSpec(memory_space=pltpu.SMEM),
            pl.BlockSpec((None, 2, HEADS, ROWS, 2 * DK), lambda i: (other, i, 0, 0, 0)),
            pl.BlockSpec((2, ROWS, HEADS * DK), lambda i: (i, 0, 0)),
            pl.BlockSpec((HEADS, DK, DK), lambda i: (0, 0, 0)),
            pl.BlockSpec((1, DK), lambda i: (0, 0)),
            pl.BlockSpec((HEADS * DK, width), lambda i: (0, 0)),
        ],
        out_specs=pl.BlockSpec((2, ROWS, width), lambda i: (i, 0, 0)),
        compiler_params=pltpu.CompilerParams(vmem_limit_bytes=32 * MIB),
        cost_estimate=pl.CostEstimate(flops=1_200_000_000, bytes_accessed=6_000_000, transcendentals=0),
        name="out",
    )(scal, hold(found), hold(gates), opening, gain, w_out)


def sum_kernel(own, received, rows, pass_up, pass_down, free_up, free_down, more_up, more_down):
    half = own.shape[2] // 2
    total = own[2].astype(F32) + received[2].astype(F32)
    pass_up[...] = total[:, :half].astype(BF16)
    pass_down[...] = total[:, half:].astype(BF16)
    total = own[1].astype(F32) + received[1].astype(F32)
    more_up[...] = total[:, :half].astype(BF16)
    free_up[...] = total[:, half:].astype(BF16)
    total = own[3].astype(F32) + received[3].astype(F32)
    free_down[...] = total[:, :half].astype(BF16)
    more_down[...] = total[:, half:].astype(BF16)
    rows[...] = (own[0].astype(F32) + received[0].astype(F32)).astype(BF16)


def sum_call(own, received):
    vmem = pl.BlockSpec(memory_space=pltpu.VMEM)
    width = own.shape[2]
    half = jax.ShapeDtypeStruct((ROWS, width // 2), BF16)
    return pl.pallas_call(
        sum_kernel,
        out_shape=(jax.ShapeDtypeStruct((ROWS, width), BF16),) + (half,) * 6,
        in_specs=[vmem] * 2,
        out_specs=[vmem] * 7,
        compiler_params=pltpu.CompilerParams(vmem_limit_bytes=16 * MIB),
        cost_estimate=pl.CostEstimate(flops=1_000_000, bytes_accessed=6_000_000, transcendentals=0),
        name="sum",
    )(own, received)


def expert_kernel(
    rows, more_up, free_up, free_down, more_down, tokens, gain, w_sgate, shared,
    attention, layer, weights, sems,
):
    size = shared.shape[1] // 4
    copies = [
        [
            pltpu.make_async_copy(
                shared.at[place, pl.ds(part * size, size)],
                weights.at[place, pl.ds(part * size, size)],
                sems.at[4 * place + part],
            )
            for part in range(4)
        ]
        for place in range(3)
    ]
    for place in range(3):
        for copy in copies[place]:
            copy.start()
    ups = jnp.concatenate([more_up[...], free_up[...]], axis=1)
    downs = jnp.concatenate([free_down[...], more_down[...]], axis=1)
    total = rows[...].astype(F32) + ups.astype(F32) + downs.astype(F32)
    total = total.astype(BF16)
    attention[...] = total
    residual = (tokens[...].astype(F32) + total.astype(F32)).astype(BF16)
    normed = scaled_rows(residual, gain[...][None, :]).astype(BF16)
    weighed = normed.astype(F32) * w_sgate[...][None, :].astype(F32)
    gate = sigmoid(jnp.sum(weighed, axis=-1, keepdims=True))
    for copy in copies[0]:
        copy.wait()
    gate_part = dot(normed, weights[0], ((1,), (1,)))
    for copy in copies[1]:
        copy.wait()
    up_part = dot(normed, weights[1], ((1,), (1,)))
    hidden = (silu(gate_part) * up_part).astype(BF16)
    for copy in copies[2]:
        copy.wait()
    layer[...] = (residual.astype(F32) + gate * dot(hidden, weights[2])).astype(BF16)


def expert_call(rows, more_up, free_up, free_down, more_down, tokens, gain, w_sgate, shared):
    vmem = pl.BlockSpec(memory_space=pltpu.VMEM)
    return pl.pallas_call(
        expert_kernel,
        out_shape=(jax.ShapeDtypeStruct(tokens.shape, BF16),) * 2,
        in_specs=[vmem] * 8 + [pl.BlockSpec(memory_space=pltpu.HBM)],
        out_specs=[vmem] * 2,
        scratch_shapes=[pltpu.VMEM(shared.shape, BF16), pltpu.SemaphoreType.DMA((12,))],
        compiler_params=pltpu.CompilerParams(vmem_limit_bytes=32 * MIB),
        cost_estimate=pl.CostEstimate(flops=800_000_000, bytes_accessed=9_000_000, transcendentals=0),
        name="expert",
    )(rows, more_up, free_up, free_down, more_down, tokens, gain, w_sgate, hold(shared))


def per_device(
    tokens,
    stretch_prompt,
    last_fill,
    ln1_gain,
    w_qk,
    w_vz,
    w_ba,
    conv_qk,
    conv_value,
    decay_log,
    dt_bias,
    norm_gain,
    w_out,
    ln2_gain,
    w_sgate,
    shared_weights,
):
    width = tokens.shape[1]
    place_y = lax.axis_index("y")
    place_core = lax.axis_index("core")
    device = lax.axis_index("z") * NX + lax.axis_index("x")
    normed = norm_call(tokens, ln1_gain)

    below = turn(normed, "y", 1, NY)
    above = turn(normed, "y", -1, NY)
    beside = turn(normed, "core", 1, NC)
    flat_vz = w_vz.reshape(width, -1)
    half_vz = flat_vz.shape[1] // 2
    weight = jnp.concatenate(
        [
            w_qk.reshape(width, -1),
            flat_vz[:, :half_vz],
            jnp.pad(w_ba.reshape(width, -1), ((0, 0), (0, 128 - 2 * HEADS))),
        ],
        axis=1,
    )
    weight_z = flat_vz[:, half_vz:]

    def project(weight, *parts):
        rows = jnp.concatenate(parts, axis=0)
        return jnp.dot(rows, weight, preferred_element_type=F32).astype(BF16)

    piece_a = project(weight, normed, beside)
    below, above, piece_a = lax.optimization_barrier((below, above, piece_a))
    across_up = turn(below[: ROWS // 2], "y", 1, NY)
    across_down = turn(above[ROWS // 2 :], "y", -1, NY)
    above_beside = turn(above, "core", 1, NC)
    below_beside = turn(below, "core", 1, NC)
    above, below, above_beside, below_beside = lax.optimization_barrier(
        (above, below, above_beside, below_beside)
    )
    piece_b = project(weight, above, below, above_beside, below_beside)
    across_up, across_down, piece_b = lax.optimization_barrier((across_up, across_down, piece_b))
    across = jnp.concatenate([across_up, across_down], axis=0)
    across_beside = turn(across, "core", 1, NC)
    piece_c = project(weight, across, across_beside)
    shared_weights, piece_c = lax.optimization_barrier((shared_weights, piece_c))
    pieces = (piece_a, piece_b, piece_c)
    gathered = lax.all_gather(shared_weights, ("y", "core"), axis=1, tiled=True)

    first_slot = device * 2
    before = jnp.concatenate([jnp.full((1,), -1, jnp.int32), stretch_prompt])
    later = jnp.concatenate([stretch_prompt, jnp.full((1,), -1, jnp.int32)])
    current = lax.dynamic_slice_in_dim(stretch_prompt, first_slot, 2)
    starts = current != lax.dynamic_slice_in_dim(before, first_slot, 2)
    finishes = current != lax.dynamic_slice_in_dim(later, first_slot + 1, 2)
    fill = jnp.where(finishes, lax.dynamic_slice_in_dim(last_fill, first_slot, 2), STRETCH)
    scal = jnp.concatenate(
        [jnp.stack([place_y, place_core]).astype(jnp.int32), starts.astype(jnp.int32), fill]
    )

    last_place = (NY - 1 - place_y) * NC + (NC - 1 - place_core)
    ends = piece_a[ROWS - LEAD : ROWS, :COL_BA]
    for (steps, other), (piece, block) in PLACES.items():
        rows = pieces[piece][(block + 1) * ROWS - LEAD : (block + 1) * ROWS, :COL_BA]
        ends = jnp.where(last_place == steps * NC + other, rows, ends)
    tail = push(ends, ("z", "x"), 1, NZ * NX)

    def gates(*parts):
        rows = jnp.concatenate(parts, axis=0)
        gate = jnp.dot(rows, weight_z, preferred_element_type=F32).astype(BF16)
        return gate.reshape(NY, ROWS, -1)

    gates_beside = gates(beside, above_beside, across_beside, below_beside)
    gates_own = gates(normed, above, across, below)
    tail, gates_own = lax.optimization_barrier((tail, gates_own))
    taps_qk = conv_qk.astype(F32)
    taps_kv = jnp.concatenate([taps_qk[:, 1, :], conv_value.astype(F32)], axis=1)
    pad = ((HEADS, 128 - 2 * HEADS),)
    decay = jnp.pad(decay_log, pad)[None, :]
    bias = jnp.pad(dt_bias, pad)[None, :]
    xend, xs, vs, khat, logs = state_call(scal, pieces, tail, taps_kv, decay, bias)

    parts = lax.all_to_all(xend, "x", 0, 0, tiled=True)
    given = (tail[:, :COL_K], taps_qk[:, 0, :], xs, vs, khat, logs)
    parts, gates_beside = lax.optimization_barrier((parts, gates_beside))
    leads, whole, sums = row_call(parts)
    earlier = [push(whole if steps < 4 else sums, "z", steps, NZ) for steps in (1, 2, 3, 4)]
    openings = open_call(earlier, leads)
    opening = lax.all_to_all(openings, "x", 0, 0, tiled=True)

    found = read_call(scal, pieces, *given)

    gain = norm_gain.astype(F32)[None, :]
    lent = out_call(1, scal, found, gates_beside, opening, gain, w_out)
    received = turn(lent, "core", 1, NC)
    own = out_call(0, scal, found, gates_own, opening, gain, w_out)

    own_rows, pass_up, pass_down, free_up, free_down, more_up, more_down = sum_call(own, received)
    pass_up = turn(pass_up, "y", 1, NY)
    pass_down = turn(pass_down, "y", -1, NY)
    free_up = turn(free_up, "y", 1, NY)
    free_down = turn(free_down, "y", -1, NY)
    more_up = turn((more_up.astype(F32) + pass_up.astype(F32)).astype(BF16), "y", 1, NY)
    more_down = turn((more_down.astype(F32) + pass_down.astype(F32)).astype(BF16), "y", -1, NY)
    return expert_call(
        own_rows, more_up, free_up, free_down, more_down, tokens, ln2_gain, w_sgate, gathered
    )


def solution(mesh):
    fine = Mesh(mesh.devices.reshape(NZ, NX, NY, NC), ("z", "x", "y", "core"))
    rows = P(("z", "x", "y", "core"), None)
    head = ("y", "core")
    return jax.shard_map(
        per_device,
        mesh=fine,
        in_specs=(
            rows,
            P(),
            P(),
            P(),
            P(None, None, head),
            P(None, None, head),
            P(None, None, head),
            P(None, None, head),
            P(None, head),
            P(head),
            P(head),
            P(),
            P(head, None),
            P(),
            P(),
            P(None, head, None),
        ),
        out_specs=(rows, rows),
        check_vma=False,
    )
```

```python
import itertools

import jax
import jax.numpy as jnp
from jax import lax
from jax.experimental import pallas as pl
from jax.experimental.pallas import tpu as pltpu
from jax.sharding import Mesh
from jax.sharding import PartitionSpec as P

F32 = jnp.float32
BF16 = jnp.bfloat16
EPSILON = 1e-06
DK = 128
STRETCH = 512
ROWS = 128
CHUNKS = 8
HEADS = 4
KEYS = 2
NZ, NX, NY, NC = 8, 4, 4, 2
LEAD = 16
COL_K = 256
COL_V = 512
COL_BA = 1024
COL_END = 1152
MIB = 1024 * 1024
PLACES = {
    (0, 0): (0, 0),
    (0, 1): (0, 1),
    (1, 0): (1, 0),
    (3, 0): (1, 1),
    (1, 1): (1, 2),
    (3, 1): (1, 3),
    (2, 0): (2, 0),
    (2, 1): (2, 1),
}


def dot(left, right, contract=((1,), (0,))):
    return lax.dot_general(left, right, (contract, ((), ())), preferred_element_type=F32)


def silu(value):
    return value * (0.5 * jnp.tanh(0.5 * value) + 0.5)


def sigmoid(value):
    return 0.5 * jnp.tanh(0.5 * value) + 0.5


def scaled_rows(inputs, scaling):
    widened = inputs.astype(F32)
    spread = jnp.mean(widened * widened, axis=-1, keepdims=True)
    return widened * lax.rsqrt(spread + EPSILON) * scaling.astype(F32)


def hold(value):
    return pltpu.with_memory_space_constraint(value, pltpu.HBM)


def turn(value, axis, steps, count):
    return lax.ppermute(value, axis, [(i, (i + steps) % count) for i in range(count)])


def push(value, axis, steps, count):
    return lax.ppermute(value, axis, [(i, i + steps) for i in range(count - steps)])


def mixed_rows(ref, chunk, first, last, taps, reset):
    start = chunk * ROWS if isinstance(chunk, int) else pl.multiple_of(chunk * ROWS, ROWS)
    rows = ref[pl.ds(start, ROWS + LEAD), first:last].astype(F32)
    if reset is not False:
        rows = jnp.concatenate([jnp.where(reset, 0.0, rows[:LEAD]), rows[LEAD:]], axis=0)
    total = rows[LEAD:] * taps[3:4]
    for offset in (1, 2, 3):
        total = total + rows[LEAD - offset : LEAD - offset + ROWS] * taps[3 - offset : 4 - offset]
    return silu(total)


def unit_heads(value):
    parts = []
    for head in range(value.shape[1] // DK):
        part = value[:, head * DK : (head + 1) * DK]
        parts.append(part * lax.rsqrt(jnp.sum(part * part, axis=-1, keepdims=True) + EPSILON))
    return parts


def fetch_rows(scal, pieces, scratch, sems, first, last, target):
    copies = []
    for (steps, other), (piece, block) in PLACES.items():
        row = lax.rem(scal[0] + steps, NY)
        core = scal[1] if other == 0 else 1 - scal[1]
        chunk = row * NC + core
        start = pl.multiple_of(chunk * ROWS + LEAD, LEAD)
        copy = pltpu.make_async_copy(
            pieces[piece].at[pl.ds(block * ROWS, ROWS), pl.ds(first, last - first)],
            scratch.at[pl.ds(start, ROWS), pl.ds(target, last - first)],
            sems.at[len(copies)],
        )
        copy.start()
        copies.append(copy)
    for copy in copies:
        copy.wait()


def is_reset(scal, chunk):
    if isinstance(chunk, int):
        return scal[2 + chunk * 2 // CHUNKS] > 0 if chunk % (CHUNKS // 2) == 0 else False
    first = jnp.logical_and(chunk == 0, scal[2] > 0)
    second = jnp.logical_and(chunk == CHUNKS // 2, scal[3] > 0)
    return jnp.logical_or(first, second)


def iota2(axis):
    return lax.broadcasted_iota(jnp.int32, (ROWS, ROWS), axis)


def odd_blocks(value, span):
    return jnp.concatenate([value[at : at + span] for at in range(span, ROWS, 2 * span)], axis=0)


def with_even(even, odd, span):
    parts = []
    for place, at in enumerate(range(0, ROWS, 2 * span)):
        block = odd[place * span : (place + 1) * span]
        parts.append(jnp.zeros_like(block) if even is None else even[at : at + span])
        parts.append(block)
    return jnp.concatenate(parts, axis=0)


def inverse_rests(stricts, level):
    rests = [jnp.where(level == 1, -strict, 0.0) for strict in stricts]
    for step in (2, 3):
        lows = [rest.astype(BF16) for rest in rests]
        belows = [jnp.where(level == step, strict, 0.0) for strict in stricts]
        halves = [below + dot(below.astype(BF16), low) for below, low in zip(belows, lows)]
        yield
        rests = [rest - half - dot(low, half.astype(BF16)) for rest, half, low in zip(rests, halves, lows)]
        yield
    for step in (4, 5, 6, 7):
        span = 1 << (step - 1)
        here = odd_blocks(level, span) == step
        lows = [rest.astype(BF16) for rest in rests]
        odds = [odd_blocks(rest, span) for rest in rests]
        belows = [jnp.where(here, odd_blocks(strict, span), 0.0) for strict in stricts]
        halves = [below + dot(below.astype(BF16), low) for below, low in zip(belows, lows)]
        yield
        wides = [with_even(None, half, span).astype(BF16) for half in halves]
        odds = [odd - half - dot(odd.astype(BF16), wide) for odd, half, wide in zip(odds, halves, wides)]
        rests = [with_even(rest, odd, span) for rest, odd in zip(rests, odds)]
        yield
    return rests


def block_levels():
    row, col = iota2(0), iota2(1)
    apart = jnp.where(row > col, jnp.bitwise_xor(row, col), 0)
    level = jnp.zeros((ROWS, ROWS), jnp.int32)
    for step in range(7):
        level = level + (apart >= (1 << step)).astype(jnp.int32)
    return level


def state_kernel(
    scal, piece_a, piece_b, piece_c, tail, taps, decay, bias,
    xend, xs_out, vs_out, khat_out, logs_out,
    raw, rest, kturn, values, betas, state, xs, vs, khat, logs, sems, out_sems,
):
    raw[0:LEAD, 0:COL_BA] = tail[...]
    fetch_rows(scal, (piece_a, piece_b, piece_c), raw, sems, COL_K, COL_END, COL_K)
    row, col = iota2(0), iota2(1)
    strict = row > col
    summing = (row >= col).astype(F32)
    level = block_levels()

    def prepare(chunk):
        reset = is_reset(scal, chunk)
        mixed = mixed_rows(raw, chunk, COL_K, COL_BA, taps, reset)
        start = chunk * ROWS + LEAD
        start = start if isinstance(chunk, int) else pl.multiple_of(start, LEAD)
        ba = raw[pl.ds(start, ROWS), COL_BA:COL_END].astype(F32)
        beta = sigmoid(ba)
        inner = ba + bias[...]
        soft = jnp.maximum(inner, 0.0) + jnp.log1p(jnp.exp(-jnp.abs(inner)))
        rate = -jnp.exp(decay[...]) * soft
        log = lax.dot_general(
            summing, rate, (((1,), (0,)), ((), ())),
            precision=lax.Precision.HIGHEST, preferred_element_type=F32,
        )
        log_turned = log.T
        betas[chunk] = beta
        logs[chunk] = log
        unit = unit_heads(mixed[:, : KEYS * DK])
        lowers = []
        for key in range(KEYS):
            key_rows = unit[key].astype(BF16)
            khat[chunk, key] = key_rows
            kturn[chunk, key] = unit[key].T.astype(BF16)
            products = dot(key_rows, key_rows, ((1,), (1,)))
            for half in range(2):
                head = 2 * key + half
                beta_col = beta[:, head : head + 1]
                spread = log[:, HEADS + head : HEADS + head + 1] - log_turned[HEADS + head : HEADS + head + 1, :]
                weight = jnp.exp(jnp.minimum(spread, 0.0))
                lower = jnp.where(strict, products * beta_col * weight, 0.0)
                lowers.append(lower)
                value = mixed[:, (KEYS + head) * DK : (KEYS + head + 1) * DK]
                values[chunk, head] = value * beta_col
        return lowers

    def prepare_all(chunks):
        lowers = []
        for chunk in chunks:
            lowers += prepare(chunk)
            yield
        found = yield from inverse_rests(lowers, level)
        for place, value in enumerate(found):
            rest[chunks[place // HEADS], place % HEADS] = value.astype(BF16)

    opening = jnp.where(scal[2] > 0, 0.0, 1.0)
    identity = jnp.where(row == col, opening, 0.0)
    for key in range(KEYS):
        for half in range(2):
            state[key, :, 2 * half * DK : (2 * half + 1) * DK] = jnp.zeros((DK, DK), F32)
            state[key, :, (2 * half + 1) * DK : (2 * half + 2) * DK] = identity

    def advance(chunk):
        beta = betas[chunk]
        log = logs[chunk]
        growth = jnp.exp(log)
        last = log[ROWS - 1 : ROWS, :]
        shrink = jnp.exp(last - log)
        whole = jnp.exp(last)
        held = [state[key] for key in range(KEYS)]
        fresh = jnp.logical_and(chunk == CHUNKS // 2, scal[3] > 0)
        held = [jnp.where(fresh, 0.0, value) for value in held]
        lows = [value.astype(BF16) for value in held]
        for key in range(KEYS):
            xs[chunk, key] = lows[key]
        seen = [dot(khat[chunk, key], lows[key]) for key in range(KEYS)]
        yield
        wanted = []
        for head in range(HEADS):
            at = HEADS + head
            half = head % 2
            factor = beta[:, head : head + 1] * growth[:, at : at + 1]
            part = seen[head // 2][:, 2 * half * DK : (2 * half + 2) * DK] * factor
            wanted.append(jnp.concatenate([values[chunk, head] - part[:, :DK], -part[:, DK:]], axis=1))
        solved = [
            value + dot(rest[chunk, head], value.astype(BF16)) for head, value in enumerate(wanted)
        ]
        yield
        updates = []
        scales = []
        for head in range(HEADS):
            at = HEADS + head
            vs[chunk, head] = solved[head].astype(BF16)
            updates.append((solved[head] * shrink[:, at : at + 1]).astype(BF16))
            scales.append(jnp.broadcast_to(whole[:, at : at + 1], (1, 2 * DK)))
        for key in range(KEYS):
            scale = jnp.concatenate(scales[2 * key : 2 * key + 2], axis=1)
            update = jnp.concatenate(updates[2 * key : 2 * key + 2], axis=1)
            state[key] = held[key] * scale + dot(kturn[chunk, key], update)
        for copy in copies_out(chunk):
            copy.start()
        yield

    def advance_all(chunks):
        for chunk in chunks:
            yield from advance(chunk)

    def copies_out(chunk):
        return [
            pltpu.make_async_copy(held.at[chunk], target.at[chunk], out_sems.at[place, chunk])
            for place, (held, target) in enumerate(((xs, xs_out), (vs, vs_out), (khat, khat_out), (logs, logs_out)))
        ]

    def both(pair, unused):
        chain = advance_all((2 * pair - 2, 2 * pair - 1))
        for place, also_unused in enumerate(prepare_all((2 * pair, 2 * pair + 1))):
            if place % 2 == 1:
                next(chain, None)
        for also_unused in chain:
            pass
        return unused

    def last(chunk, unused):
        for also_unused in advance(chunk):
            pass
        return unused

    for unused in prepare_all((0, 1)):
        pass
    lax.fori_loop(1, CHUNKS // 2, both, 0)
    lax.fori_loop(CHUNKS - 2, CHUNKS, last, 0)
    for key in range(KEYS):
        for half in range(2):
            xend[2 * key + half] = state[key, :, 2 * half * DK : (2 * half + 2) * DK].astype(BF16)
    for chunk in range(CHUNKS):
        for copy in copies_out(chunk):
            copy.wait()


def state_call(scal, pieces, tail, taps, decay, bias):
    vmem = pl.BlockSpec(memory_space=pltpu.VMEM)
    hbm = pl.BlockSpec(memory_space=pltpu.HBM)
    return pl.pallas_call(
        state_kernel,
        out_shape=(
            jax.ShapeDtypeStruct((HEADS, DK, 2 * DK), BF16),
            pltpu.HBM((CHUNKS, KEYS, DK, 4 * DK), BF16),
            pltpu.HBM((CHUNKS, HEADS, ROWS, 2 * DK), BF16),
            pltpu.HBM((CHUNKS, KEYS, ROWS, DK), BF16),
            pltpu.HBM((CHUNKS, ROWS, 128), F32),
        ),
        in_specs=[pl.BlockSpec(memory_space=pltpu.SMEM), hbm, hbm, hbm] + [vmem] * 4,
        out_specs=[vmem] + [hbm] * 4,
        scratch_shapes=[
            pltpu.VMEM((LEAD + CHUNKS * ROWS, COL_END), BF16),
            pltpu.VMEM((CHUNKS, HEADS, ROWS, ROWS), BF16),
            pltpu.VMEM((CHUNKS, KEYS, DK, ROWS), BF16),
            pltpu.VMEM((CHUNKS, HEADS, ROWS, DK), F32),
            pltpu.VMEM((CHUNKS, ROWS, 128), F32),
            pltpu.VMEM((KEYS, DK, 4 * DK), F32),
            pltpu.VMEM((CHUNKS, KEYS, DK, 4 * DK), BF16),
            pltpu.VMEM((CHUNKS, HEADS, ROWS, 2 * DK), BF16),
            pltpu.VMEM((CHUNKS, KEYS, ROWS, DK), BF16),
            pltpu.VMEM((CHUNKS, ROWS, 128), F32),
            pltpu.SemaphoreType.DMA((CHUNKS,)),
            pltpu.SemaphoreType.DMA((4, CHUNKS)),
        ],
        compiler_params=pltpu.CompilerParams(vmem_limit_bytes=40 * MIB),
        cost_estimate=pl.CostEstimate(flops=6_000_000_000, bytes_accessed=20_000_000, transcendentals=0),
        name="state",
    )(scal, *map(hold, pieces), tail, taps, decay, bias)


def read_kernel(
    half, scal, piece_a, piece_b, piece_c, tail, taps, xs, vs, khat, logs, *rest
):
    out, raw, sems = rest[-3:]
    step = pl.program_id(0) + half * CHUNKS // NC // 2

    @pl.when(pl.program_id(0) == 0)
    def _():
        raw[0:LEAD, :] = tail[...]
        fetch_rows(scal, (piece_a, piece_b, piece_c), raw, sems, 0, COL_K, 0)

    inclusive = iota2(0) >= iota2(1)
    queries, weights, growths = [], [], []
    for core in range(NC):
        chunk = NC * step + core
        start = pl.multiple_of(chunk * ROWS, ROWS)
        reset = is_reset(scal, chunk) if core == 0 else False
        mixed = mixed_rows(raw.at[pl.ds(start, ROWS + LEAD)], 0, 0, COL_K, taps, reset)
        queries += [(value * DK ** (-0.5)).astype(BF16) for value in unit_heads(mixed)]
        log = logs[core]
        log_turned = log.T
        growth = jnp.exp(log)
        for head in range(HEADS):
            at = HEADS + head
            growths.append(growth[:, at : at + 1])
            spread = log[:, at : at + 1] - log_turned[at : at + 1, :]
            weights.append(jnp.where(inclusive, jnp.exp(jnp.minimum(spread, 0.0)), 0.0))
    pairs = [(core, key) for core in range(NC) for key in range(KEYS)]
    products = [dot(queries[i], khat[core, key], ((1,), (1,))) for i, (core, key) in enumerate(pairs)]
    seen = [dot(queries[i], xs[core, key]) for i, (core, key) in enumerate(pairs)]
    for core in range(NC):
        other = jnp.bitwise_xor(core, scal[1])
        for head in range(HEADS):
            pair = core * KEYS + head // 2
            half = head % 2
            scores = (products[pair] * weights[core * HEADS + head]).astype(BF16)
            found = seen[pair][:, 2 * half * DK : (2 * half + 2) * DK] * growths[core * HEADS + head]
            out[other, head] = (found + dot(scores, vs[core, head])).astype(BF16)


def read_call(half, scal, pieces, tail, taps, xs, vs, khat, logs, *found):
    hbm = pl.BlockSpec(memory_space=pltpu.HBM)
    skip = half * CHUNKS // NC // 2
    return pl.pallas_call(
        lambda *refs: read_kernel(half, *refs),
        out_shape=pltpu.HBM((NC, NY, HEADS, ROWS, 2 * DK), BF16),
        grid_spec=pltpu.PrefetchScalarGridSpec(
            num_scalar_prefetch=1,
            grid=(CHUNKS // NC // 2,),
            in_specs=[
                hbm,
                hbm,
                hbm,
                pl.BlockSpec((LEAD, COL_K), lambda c, scal: (0, 0)),
                pl.BlockSpec((4, COL_K), lambda c, scal: (0, 0)),
                pl.BlockSpec((NC, KEYS, DK, 4 * DK), lambda c, scal: (c + skip, 0, 0, 0)),
                pl.BlockSpec((NC, HEADS, ROWS, 2 * DK), lambda c, scal: (c + skip, 0, 0, 0)),
                pl.BlockSpec((NC, KEYS, ROWS, DK), lambda c, scal: (c + skip, 0, 0, 0)),
                pl.BlockSpec((NC, ROWS, 128), lambda c, scal: (c + skip, 0, 0)),
            ]
            + [hbm] * len(found),
            out_specs=pl.BlockSpec(
                (NC, None, HEADS, ROWS, 2 * DK),
                lambda c, scal: (0, lax.rem(c + skip - scal[0] + NY, NY), 0, 0, 0),
            ),
            scratch_shapes=[
                pltpu.VMEM((LEAD + CHUNKS * ROWS, COL_K), BF16),
                pltpu.SemaphoreType.DMA((CHUNKS,)),
            ],
        ),
        input_output_aliases={10: 0} if found else {},
        compiler_params=pltpu.CompilerParams(vmem_limit_bytes=32 * MIB),
        cost_estimate=pl.CostEstimate(flops=3_000_000_000, bytes_accessed=10_000_000, transcendentals=0),
        name="read",
    )(scal, *map(hold, pieces), tail, taps, hold(xs), hold(vs), hold(khat), hold(logs), *map(hold, found))


def norm_kernel(tokens, gain, out):
    out[...] = scaled_rows(tokens[...], gain[...][None, :]).astype(BF16)


def norm_call(tokens, gain):
    vmem = pl.BlockSpec(memory_space=pltpu.VMEM)
    return pl.pallas_call(
        norm_kernel,
        out_shape=jax.ShapeDtypeStruct(tokens.shape, BF16),
        in_specs=[vmem, vmem],
        out_specs=vmem,
        cost_estimate=pl.CostEstimate(flops=1_000_000, bytes_accessed=1_000_000, transcendentals=0),
        name="norm",
    )(tokens, gain)


def after(late, early):
    moved = dot(late[:, DK:], early)
    if early.shape[1] == DK:
        return moved + late[:, :DK].astype(F32)
    return jnp.concatenate([moved[:, :DK] + late[:, :DK].astype(F32), moved[:, DK:]], axis=1)


def row_kernel(parts, leads, whole, sums):
    held = parts[0]
    leads[0] = held
    for place in range(1, NX):
        held = after(parts[place], held).astype(BF16)
        if place < NX - 1:
            leads[place] = held
    whole[...] = held
    sums[...] = held[:, :DK]


def row_call(parts):
    vmem = pl.BlockSpec(memory_space=pltpu.VMEM)
    return pl.pallas_call(
        row_kernel,
        out_shape=(
            jax.ShapeDtypeStruct((NX - 1, DK, 2 * DK), BF16),
            jax.ShapeDtypeStruct((DK, 2 * DK), BF16),
            jax.ShapeDtypeStruct((DK, DK), BF16),
        ),
        in_specs=[vmem],
        out_specs=[vmem] * 3,
        cost_estimate=pl.CostEstimate(flops=100_000_000, bytes_accessed=1_000_000, transcendentals=0),
        name="rows",
    )(parts)


def open_kernel(one, two, three, four, leads, out):
    opening = four[...]
    for earlier in (three, two, one):
        opening = after(earlier[...], opening).astype(BF16)
    out[0] = opening
    for place in range(1, NX):
        out[place] = after(leads[place - 1], opening).astype(BF16)


def open_call(earlier, leads):
    vmem = pl.BlockSpec(memory_space=pltpu.VMEM)
    return pl.pallas_call(
        open_kernel,
        out_shape=jax.ShapeDtypeStruct((NX, DK, DK), BF16),
        in_specs=[vmem] * 5,
        out_specs=vmem,
        cost_estimate=pl.CostEstimate(flops=100_000_000, bytes_accessed=1_000_000, transcendentals=0),
        name="open",
    )(*earlier, leads)


def out_kernel(other, scal, found, gates, opening, gain, w_out, out):
    rows = []
    moved = [
        [dot(found[block, head][:, DK:], opening[head]) for head in range(HEADS)]
        for block in range(2)
    ]
    for block in range(2):
        steps = 2 * pl.program_id(0) + block
        core = scal[1] if other == 0 else 1 - scal[1]
        chunk = lax.rem(scal[0] + steps, NY) * NC + core
        first = lax.rem(chunk, STRETCH // ROWS) * ROWS
        fill = jnp.where(chunk < CHUNKS // 2, scal[4], scal[5])
        within = lax.broadcasted_iota(jnp.int32, (ROWS, 1), 0) + first
        kept = within < fill
        parts = []
        for head in range(HEADS):
            value = found[block, head][:, :DK].astype(F32) + moved[block][head]
            value = jnp.where(kept, value, 0.0)
            gate = gates[block, :, head * DK : (head + 1) * DK].astype(F32)
            spread = jnp.mean(value * value, axis=-1, keepdims=True)
            parts.append((value * lax.rsqrt(spread + EPSILON) * gain[...] * silu(gate)).astype(BF16))
        rows.append(jnp.concatenate(parts, axis=1))
    total = dot(jnp.concatenate(rows, axis=0), w_out[...]).astype(BF16)
    out[...] = total.reshape(out.shape)


def out_call(other, scal, found, gates, opening, gain, w_out):
    width = w_out.shape[1]
    return pl.pallas_call(
        lambda *refs: out_kernel(other, *refs),
        grid=(NY // 2,),
        out_shape=jax.ShapeDtypeStruct((NY, ROWS, width), BF16),
        in_specs=[
            pl.BlockSpec(memory_space=pltpu.SMEM),
            pl.BlockSpec((None, 2, HEADS, ROWS, 2 * DK), lambda i: (other, i, 0, 0, 0)),
            pl.BlockSpec((2, ROWS, HEADS * DK), lambda i: (i, 0, 0)),
            pl.BlockSpec((HEADS, DK, DK), lambda i: (0, 0, 0)),
            pl.BlockSpec((1, DK), lambda i: (0, 0)),
            pl.BlockSpec((HEADS * DK, width), lambda i: (0, 0)),
        ],
        out_specs=pl.BlockSpec((2, ROWS, width), lambda i: (i, 0, 0)),
        compiler_params=pltpu.CompilerParams(vmem_limit_bytes=32 * MIB),
        cost_estimate=pl.CostEstimate(flops=1_200_000_000, bytes_accessed=6_000_000, transcendentals=0),
        name="out",
    )(scal, hold(found), hold(gates), opening, gain, w_out)


def sum_kernel(own, received, rows, pass_up, pass_down, free_up, free_down, more_up, more_down):
    half = own.shape[2] // 2
    total = own[2].astype(F32) + received[2].astype(F32)
    pass_up[...] = total[:, :half].astype(BF16)
    pass_down[...] = total[:, half:].astype(BF16)
    total = own[1].astype(F32) + received[1].astype(F32)
    more_up[...] = total[:, :half].astype(BF16)
    free_up[...] = total[:, half:].astype(BF16)
    total = own[3].astype(F32) + received[3].astype(F32)
    free_down[...] = total[:, :half].astype(BF16)
    more_down[...] = total[:, half:].astype(BF16)
    rows[...] = (own[0].astype(F32) + received[0].astype(F32)).astype(BF16)


def sum_call(own, received):
    vmem = pl.BlockSpec(memory_space=pltpu.VMEM)
    width = own.shape[2]
    half = jax.ShapeDtypeStruct((ROWS, width // 2), BF16)
    return pl.pallas_call(
        sum_kernel,
        out_shape=(jax.ShapeDtypeStruct((ROWS, width), BF16),) + (half,) * 6,
        in_specs=[vmem] * 2,
        out_specs=[vmem] * 7,
        compiler_params=pltpu.CompilerParams(vmem_limit_bytes=16 * MIB),
        cost_estimate=pl.CostEstimate(flops=1_000_000, bytes_accessed=6_000_000, transcendentals=0),
        name="sum",
    )(own, received)


def expert_kernel(
    rows, more_up, free_up, free_down, more_down, tokens, gain, w_sgate, shared,
    attention, layer, weights, sems,
):
    size = shared.shape[1] // 4
    copies = [
        [
            pltpu.make_async_copy(
                shared.at[place, pl.ds(part * size, size)],
                weights.at[place, pl.ds(part * size, size)],
                sems.at[4 * place + part],
            )
            for part in range(4)
        ]
        for place in range(3)
    ]
    for place in range(3):
        for copy in copies[place]:
            copy.start()
    ups = jnp.concatenate([more_up[...], free_up[...]], axis=1)
    downs = jnp.concatenate([free_down[...], more_down[...]], axis=1)
    total = rows[...].astype(F32) + ups.astype(F32) + downs.astype(F32)
    total = total.astype(BF16)
    attention[...] = total
    residual = (tokens[...].astype(F32) + total.astype(F32)).astype(BF16)
    normed = scaled_rows(residual, gain[...][None, :]).astype(BF16)
    weighed = normed.astype(F32) * w_sgate[...][None, :].astype(F32)
    gate = sigmoid(jnp.sum(weighed, axis=-1, keepdims=True))
    for copy in copies[0]:
        copy.wait()
    gate_part = dot(normed, weights[0], ((1,), (1,)))
    for copy in copies[1]:
        copy.wait()
    up_part = dot(normed, weights[1], ((1,), (1,)))
    hidden = (silu(gate_part) * up_part).astype(BF16)
    for copy in copies[2]:
        copy.wait()
    layer[...] = (residual.astype(F32) + gate * dot(hidden, weights[2])).astype(BF16)


def expert_call(rows, more_up, free_up, free_down, more_down, tokens, gain, w_sgate, shared):
    vmem = pl.BlockSpec(memory_space=pltpu.VMEM)
    return pl.pallas_call(
        expert_kernel,
        out_shape=(jax.ShapeDtypeStruct(tokens.shape, BF16),) * 2,
        in_specs=[vmem] * 8 + [pl.BlockSpec(memory_space=pltpu.HBM)],
        out_specs=[vmem] * 2,
        scratch_shapes=[pltpu.VMEM(shared.shape, BF16), pltpu.SemaphoreType.DMA((12,))],
        compiler_params=pltpu.CompilerParams(vmem_limit_bytes=32 * MIB),
        cost_estimate=pl.CostEstimate(flops=800_000_000, bytes_accessed=9_000_000, transcendentals=0),
        name="expert",
    )(rows, more_up, free_up, free_down, more_down, tokens, gain, w_sgate, hold(shared))


def per_device(
    tokens,
    stretch_prompt,
    last_fill,
    ln1_gain,
    w_qk,
    w_vz,
    w_ba,
    conv_qk,
    conv_value,
    decay_log,
    dt_bias,
    norm_gain,
    w_out,
    ln2_gain,
    w_sgate,
    shared_weights,
):
    width = tokens.shape[1]
    place_y = lax.axis_index("y")
    place_core = lax.axis_index("core")
    device = lax.axis_index("z") * NX + lax.axis_index("x")
    normed = norm_call(tokens, ln1_gain)

    below = turn(normed, "y", 1, NY)
    above = turn(normed, "y", -1, NY)
    beside = turn(normed, "core", 1, NC)
    flat_vz = w_vz.reshape(width, -1)
    half_vz = flat_vz.shape[1] // 2
    weight = jnp.concatenate(
        [
            w_qk.reshape(width, -1),
            flat_vz[:, :half_vz],
            jnp.pad(w_ba.reshape(width, -1), ((0, 0), (0, 128 - 2 * HEADS))),
        ],
        axis=1,
    )
    weight_z = flat_vz[:, half_vz:]

    def project(weight, *parts):
        rows = jnp.concatenate(parts, axis=0)
        return jnp.dot(rows, weight, preferred_element_type=F32).astype(BF16)

    piece_a = project(weight, normed, beside)
    below, above, piece_a = lax.optimization_barrier((below, above, piece_a))
    across_up = turn(below[: ROWS // 2], "y", 1, NY)
    across_down = turn(above[ROWS // 2 :], "y", -1, NY)
    above_beside = turn(above, "core", 1, NC)
    below_beside = turn(below, "core", 1, NC)
    above, below, above_beside, below_beside = lax.optimization_barrier(
        (above, below, above_beside, below_beside)
    )
    piece_b = project(weight, above, below, above_beside, below_beside)
    across_up, across_down, piece_b = lax.optimization_barrier((across_up, across_down, piece_b))
    across = jnp.concatenate([across_up, across_down], axis=0)
    across_beside = turn(across, "core", 1, NC)
    piece_c = project(weight, across, across_beside)
    shared_weights, piece_c = lax.optimization_barrier((shared_weights, piece_c))
    pieces = (piece_a, piece_b, piece_c)
    gathered = lax.all_gather(shared_weights, ("y", "core"), axis=1, tiled=True)

    first_slot = device * 2
    before = jnp.concatenate([jnp.full((1,), -1, jnp.int32), stretch_prompt])
    later = jnp.concatenate([stretch_prompt, jnp.full((1,), -1, jnp.int32)])
    current = lax.dynamic_slice_in_dim(stretch_prompt, first_slot, 2)
    starts = current != lax.dynamic_slice_in_dim(before, first_slot, 2)
    finishes = current != lax.dynamic_slice_in_dim(later, first_slot + 1, 2)
    fill = jnp.where(finishes, lax.dynamic_slice_in_dim(last_fill, first_slot, 2), STRETCH)
    scal = jnp.concatenate(
        [jnp.stack([place_y, place_core]).astype(jnp.int32), starts.astype(jnp.int32), fill]
    )

    last_place = (NY - 1 - place_y) * NC + (NC - 1 - place_core)
    ends = piece_a[ROWS - LEAD : ROWS, :COL_BA]
    for (steps, other), (piece, block) in PLACES.items():
        rows = pieces[piece][(block + 1) * ROWS - LEAD : (block + 1) * ROWS, :COL_BA]
        ends = jnp.where(last_place == steps * NC + other, rows, ends)
    tail = push(ends, ("z", "x"), 1, NZ * NX)

    def gates(*parts):
        rows = jnp.concatenate(parts, axis=0)
        gate = jnp.dot(rows, weight_z, preferred_element_type=F32).astype(BF16)
        return gate.reshape(NY, ROWS, -1)

    gates_beside = gates(beside, above_beside, across_beside, below_beside)
    gates_own = gates(normed, above, across, below)
    tail, gates_own = lax.optimization_barrier((tail, gates_own))
    taps_qk = conv_qk.astype(F32)
    taps_kv = jnp.concatenate([taps_qk[:, 1, :], conv_value.astype(F32)], axis=1)
    pad = ((HEADS, 128 - 2 * HEADS),)
    decay = jnp.pad(decay_log, pad)[None, :]
    bias = jnp.pad(dt_bias, pad)[None, :]
    xend, xs, vs, khat, logs = state_call(scal, pieces, tail, taps_kv, decay, bias)

    parts = lax.all_to_all(xend, "x", 0, 0, tiled=True)
    given = (tail[:, :COL_K], taps_qk[:, 0, :], xs, vs, khat, logs)
    found = read_call(0, scal, pieces, *given)
    parts, gates_beside, found = lax.optimization_barrier((parts, gates_beside, found))
    leads, whole, sums = row_call(parts)
    earlier = [push(whole if steps < 4 else sums, "z", steps, NZ) for steps in (1, 2, 3, 4)]
    openings = open_call(earlier, leads)
    opening = lax.all_to_all(openings, "x", 0, 0, tiled=True)

    found = read_call(1, scal, pieces, *given, found)

    gain = norm_gain.astype(F32)[None, :]
    lent = out_call(1, scal, found, gates_beside, opening, gain, w_out)
    received = turn(lent, "core", 1, NC)
    own = out_call(0, scal, found, gates_own, opening, gain, w_out)

    own_rows, pass_up, pass_down, free_up, free_down, more_up, more_down = sum_call(own, received)
    pass_up = turn(pass_up, "y", 1, NY)
    pass_down = turn(pass_down, "y", -1, NY)
    free_up = turn(free_up, "y", 1, NY)
    free_down = turn(free_down, "y", -1, NY)
    more_up = turn((more_up.astype(F32) + pass_up.astype(F32)).astype(BF16), "y", 1, NY)
    more_down = turn((more_down.astype(F32) + pass_down.astype(F32)).astype(BF16), "y", -1, NY)
    return expert_call(
        own_rows, more_up, free_up, free_down, more_down, tokens, ln2_gain, w_sgate, gathered
    )


def solution(mesh):
    fine = Mesh(mesh.devices.reshape(NZ, NX, NY, NC), ("z", "x", "y", "core"))
    rows = P(("z", "x", "y", "core"), None)
    head = ("y", "core")
    return jax.shard_map(
        per_device,
        mesh=fine,
        in_specs=(
            rows,
            P(),
            P(),
            P(),
            P(None, None, head),
            P(None, None, head),
            P(None, None, head),
            P(None, None, head),
            P(None, head),
            P(head),
            P(head),
            P(),
            P(head, None),
            P(),
            P(),
            P(None, head, None),
        ),
        out_specs=(rows, rows),
        check_vma=False,
    )
```
